512 devices in a mesh: st: 64 (over z, x, core), tile: 8 (over y).
Axes of the slice: x: 4, y: 8, z: 8, core: 2. Of those that a mesh axis runs over, the one named last changes fastest.
Arguments:
- grid: bfloat16 [8, 2048, 128], P(None, 'tile'), may hold values from -6 to 6
- a_terms: float32 [512, 2, 4, 1024], P('st'), may hold values from -5 to 5
- stations: int32 [4096, 2], P(('st', 'tile')), may hold values from 0 to 511, as said below
- intervals: int32 [4096], P(('st', 'tile')), may hold values from 0 to 1
- offsets: int32 [4096, 2], P(('st', 'tile')), may hold values from 0 to 2016, as said below
- uv: float32 [4096, 2, 512], P(('st', 'tile')), may hold values from -12 to 12
- observed: float32 [4096, 8, 512], P(('st', 'tile')), may hold values from -6 to 6
- flags: int32 [4096, 512], P(('st', 'tile')), may hold values 0 or 1
Outputs:
- residual: float32 [4096, 8, 512], P(('st', 'tile'))
- a_grad: float32 [512, 2, 4, 1024], P('st')
The draws below stay inside these ranges and needn't reach their ends.
Inputs may be any that keep to these rules, and one draw needn't show every extreme that they name: Among the 8 subgrids of one device, at most 2 station ends (first and second stations together) lie in one block of 8 consecutive stations starting at a multiple of 8, and some such block gets exactly 2; the two stations of a subgrid differ. `offsets`: column 0 is the grid row, column 1 the grid column of the corner. A subgrid's 32 rows lie inside one block of 256 consecutive rows starting at a multiple of 256, and its columns inside the strip. Among the 8 subgrids of one device at most 2 lie in one such block, and some block gets exactly 2.
All inputs are finite; a program needn't handle non-finite values. No bound on the sum of `flags` on one device may be relied on, other than what follows from the above.
Results may differ from the reference program's by a relative error of at most 0.0003.
Values may be sent and summed in bfloat16 or wider, within the bound.
No kernel may reach another device: no remote copies, remote signals or barrier semaphores. Data moves between devices by JAX's collectives and lax.ppermute only.
A program may use at most 64 MiB of HBM per device.

```python
import jax
import jax.numpy as jnp
from jax import lax

SUBSIZE = 32
VIS = 512
INTERVALS = 2
STA_DEV = 8
STATIONS = 512
SUB_DEV = 8
SUBGRIDS = 4096
TILE_U = 256
GRID_U = 2048
GRID_V = 128
CAP = 2
CT = 2


def spread_owners(key, ends, owners, most):
    key_a, key_b, key_c = jax.random.split(key, 3)
    rest = jax.random.permutation(key_a, owners * most - most)[:ends - most] + most
    slots = jnp.concatenate([jnp.arange(most, dtype=jnp.int32), rest.astype(jnp.int32)])
    owner = slots // most
    relabel = jax.random.permutation(key_b, owners).astype(jnp.int32)
    owner = relabel[owner]
    order = jax.random.permutation(key_c, ends)
    return owner[order]


def draw_stations(key, part):
    key = jax.random.fold_in(key, 11)
    owners = STATIONS // STA_DEV
    blocks = SUBGRIDS // SUB_DEV

    def one_block(block_key):
        key_a, key_b = jax.random.split(block_key)
        owner = spread_owners(key_a, 2 * SUB_DEV, owners, CAP).reshape(2, SUB_DEV).T
        local = jax.random.randint(key_b, (SUB_DEV, 2), 0, STA_DEV).astype(jnp.int32)
        same = (owner[:, 0] == owner[:, 1]) & (local[:, 0] == local[:, 1])
        second = jnp.where(same, (local[:, 1] + 1) % STA_DEV, local[:, 1])
        local = jnp.stack([local[:, 0], second], axis=1)
        return owner * STA_DEV + local
    result = jax.vmap(one_block)(jax.random.split(key, blocks))
    return result.reshape(SUBGRIDS, 2).astype(jnp.int32)


def draw_offsets(key, part):
    key = jax.random.fold_in(key, 23)
    tiles = GRID_U // TILE_U
    blocks = SUBGRIDS // SUB_DEV

    def one_block(block_key):
        key_a, key_b, key_c = jax.random.split(block_key, 3)
        owner = spread_owners(key_a, SUB_DEV, tiles, CT)
        row = owner * TILE_U + jax.random.randint(key_b, (SUB_DEV,), 0, TILE_U - SUBSIZE + 1).astype(jnp.int32)
        column = jax.random.randint(key_c, (SUB_DEV,), 0, GRID_V - SUBSIZE + 1).astype(jnp.int32)
        return jnp.stack([row, column], axis=1)
    result = jax.vmap(one_block)(jax.random.split(key, blocks))
    return result.reshape(SUBGRIDS, 2).astype(jnp.int32)


def with_ends(drawn, stream_key, smallest, top_value):
    shape = drawn.shape
    place = [jax.random.randint(jax.random.fold_in(stream_key, axis), (), 0, shape[axis]) for axis in range(len(shape))]
    drawn = drawn.at[tuple(place)].set(smallest)
    longest = shape.index(max(shape))
    place[longest] = (place[longest] + 1) % shape[longest]
    return drawn.at[tuple(place)].set(top_value)


def shard_levels(own_key, shape, cuts, least, top_value):
    factor_of, own = 1.0, jax.random.fold_in(own_key, 6)
    for position, parts in cuts:
        steps = jnp.exp(jax.random.uniform(jax.random.fold_in(own, position), (parts,), jnp.float32, least / len(cuts), top_value / len(cuts)))
        factor_of = factor_of * jnp.repeat(steps, shape[position] // parts).reshape([-1 if axis == position else 1 for axis in range(len(shape))])
    return factor_of


def centred(rng, dims, width, reach, cuts=(), held_as=jnp.bfloat16):
    drawn = width * jax.random.normal(rng, dims, jnp.float32)
    if cuts:
        drawn = drawn * shard_levels(rng, dims, cuts, -0.22, 0.18)
    return jnp.clip(drawn, -reach, reach).astype(held_as)


def setup_inputs(seed: int = 0) -> dict:
    streams_of = jax.random.split(jax.random.key(seed), 9)
    return {
        "grid": centred(streams_of[0], (8, GRID_U, GRID_V), 1.0, 6.0, ((1, 8),)),
        "a_terms": centred(streams_of[1], (STATIONS, INTERVALS, 4, SUBSIZE * SUBSIZE), 1.0, 5.0, ((0, 64),), jnp.float32),
        "stations": draw_stations(jax.random.fold_in(streams_of[8], 71), 0),
        "intervals": with_ends(jax.random.randint(streams_of[3], (SUBGRIDS,), 0, INTERVALS), jax.random.fold_in(streams_of[3], 1), 0, INTERVALS - 1).astype(jnp.int32),
        "offsets": draw_offsets(jax.random.fold_in(streams_of[8], 71), 0),
        "uv": jnp.clip(jax.random.uniform(streams_of[5], (SUBGRIDS, 2, VIS), jnp.float32, -12.0, 12.0) * shard_levels(streams_of[5], (SUBGRIDS, 2, VIS), ((0, 512),), -0.4, 0.0), -12.0, 12.0),
        "observed": centred(streams_of[6], (SUBGRIDS, 8, VIS), 1.0, 6.0, ((0, 512),), jnp.float32),
        "flags": with_ends((jax.random.randint(streams_of[7], (SUBGRIDS, VIS), 0, 8) < 7).astype(jnp.int32), jax.random.fold_in(streams_of[7], 1), 0, 1),
    }


HIGH = lax.Precision.HIGHEST

def tables(side):
    index = jnp.arange(side, dtype=jnp.float32)
    angle = 2.0 * jnp.pi * index[:, None] * index[None, :] / side
    f_real = jnp.cos(angle) / side
    f_imag = jnp.sin(angle) / side
    edge = jnp.cos(jnp.pi * (index - (side - 1) / 2.0) / side)
    return (f_real, f_imag, edge[:, None] * edge[None, :])

def predict_residual(patches, a_p, a_q, coords, observed, flags):
    side = SUBSIZE
    count = patches.shape[0]
    f_real, f_imag, taper = tables(side)
    g_re = patches[:, :4].reshape(count, 4, side, side)
    g_im = patches[:, 4:].reshape(count, 4, side, side)
    x_re = jnp.einsum('la,bpam->bplm', f_real, g_re, precision=HIGH) - jnp.einsum('la,bpam->bplm', f_imag, g_im, precision=HIGH)
    x_im = jnp.einsum('la,bpam->bplm', f_real, g_im, precision=HIGH) + jnp.einsum('la,bpam->bplm', f_imag, g_re, precision=HIGH)
    i_re = jnp.einsum('bplk,mk->bplm', x_re, f_real, precision=HIGH) - jnp.einsum('bplk,mk->bplm', x_im, f_imag, precision=HIGH)
    i_im = jnp.einsum('bplk,mk->bplm', x_re, f_imag, precision=HIGH) + jnp.einsum('bplk,mk->bplm', x_im, f_real, precision=HIGH)
    i_re = i_re.reshape(count, 2, 2, side, side)
    i_im = i_im.reshape(count, 2, 2, side, side)
    p_re = a_p[:, 0:2].reshape(count, 2, 1, side, side)
    p_im = a_p[:, 2:4].reshape(count, 2, 1, side, side)
    q_re = a_q[:, 0:2].reshape(count, 1, 2, side, side)
    q_im = a_q[:, 2:4].reshape(count, 1, 2, side, side)
    y_re = i_re * q_re + i_im * q_im
    y_im = i_im * q_re - i_re * q_im
    z_re = ((p_re * y_re - p_im * y_im) * taper).reshape(count, 4, side, side)
    z_im = ((p_re * y_im + p_im * y_re) * taper).reshape(count, 4, side, side)
    zt_re = z_re.transpose(0, 3, 1, 2).reshape(count, side, 4 * side)
    zt_im = z_im.transpose(0, 3, 1, 2).reshape(count, side, 4 * side)
    centre = jnp.arange(side, dtype=jnp.float32) - side / 2.0
    phase_u = 2.0 * jnp.pi * coords[:, 0, :, None] * centre / side
    phase_v = 2.0 * jnp.pi * coords[:, 1, :, None] * centre / side
    eu_re, eu_im = (jnp.cos(phase_u), jnp.sin(phase_u))
    ev_re, ev_im = (jnp.cos(phase_v), jnp.sin(phase_v))
    w_re = jnp.einsum('bvm,bmq->bvq', ev_re, zt_re, precision=HIGH) - jnp.einsum('bvm,bmq->bvq', ev_im, zt_im, precision=HIGH)
    w_im = jnp.einsum('bvm,bmq->bvq', ev_re, zt_im, precision=HIGH) + jnp.einsum('bvm,bmq->bvq', ev_im, zt_re, precision=HIGH)
    vcount = coords.shape[2]
    w_re = w_re.reshape(count, vcount, 4, side)
    w_im = w_im.reshape(count, vcount, 4, side)
    eu_re = eu_re[:, :, None, :]
    eu_im = eu_im[:, :, None, :]
    v_re = lax.optimization_barrier(jnp.sum(eu_re * w_re - eu_im * w_im, axis=-1))
    v_im = lax.optimization_barrier(jnp.sum(eu_re * w_im + eu_im * w_re, axis=-1))
    model = jnp.concatenate([v_re, v_im], axis=-1).transpose(0, 2, 1)
    return flags[:, None, :].astype(jnp.float32) * (observed - model)

def cut_patch(source, row, column):
    start = jnp.zeros((), jnp.int32)
    piece = lax.dynamic_slice(source, (start, row.astype(jnp.int32), column.astype(jnp.int32)), (8, SUBSIZE, SUBSIZE))
    return piece.reshape(8, SUBSIZE * SUBSIZE)

def reference(grid, a_terms, stations, intervals, offsets, uv, observed, flags):
    pixels = SUBSIZE * SUBSIZE
    screens = STATIONS * INTERVALS
    flat = a_terms.reshape(screens, 4, pixels)
    block = min(SUBGRIDS, 64)
    blocks = SUBGRIDS // block
    id_p = (stations[:, 0] * INTERVALS + intervals).astype(jnp.int32)
    id_q = (stations[:, 1] * INTERVALS + intervals).astype(jnp.int32)
    items = tuple((a.reshape((blocks, block) + a.shape[1:]) for a in (id_p, id_q, offsets, uv, observed, flags)))

    def advance(total, item):
        ip, iq, corner, coords, seen, usable = item
        patches = jax.vmap(cut_patch, in_axes=(None, 0, 0))(grid, corner[:, 0], corner[:, 1]).astype(jnp.float32)

        def forward(first, second):
            return predict_residual(patches, first, second, coords, seen, usable)
        result, pullback = jax.vjp(forward, flat[ip], flat[iq])
        grad_p, grad_q = pullback(result)
        total = total.at[ip].add(grad_p).at[iq].add(grad_q)
        return (total, result)
    total, result = lax.scan(advance, jnp.zeros((screens, 4, pixels), jnp.float32), items)
    return (result.reshape(SUBGRIDS, 8, VIS), total.reshape(STATIONS, INTERVALS, 4, pixels))
```

```python
import math

import jax
import jax.numpy as jnp
import numpy as np
from jax import lax
from jax.experimental import pallas as pl
from jax.experimental.pallas import tpu as pltpu
from jax.sharding import Mesh
from jax.sharding import PartitionSpec as P

SIDE = 32
SUBS = 8
ENDS = 2 * SUBS
VIS = 512
PEERS = 32
BLOCKS = 16
ROWS = 64
SCREENS = BLOCKS * ROWS
LANES = 128
SLOTS = 16

F32 = jnp.float32
BF16 = jnp.bfloat16
S32 = jnp.int32


def bf16_parts(array, count):
    rest = np.asarray(array, np.float64)
    parts = []
    for _ in range(count):
        part = rest.astype(np.float32).astype(jnp.bfloat16)
        parts.append(part)
        rest = rest - part.astype(np.float64)
    return parts


def dft_tables():
    index = np.arange(SIDE)
    angle = 2.0 * np.pi * (index[:, None] * index[None, :] % SIDE) / SIDE
    f_real = np.cos(angle) / SIDE
    f_imag = np.sin(angle) / SIDE
    rows = np.concatenate([f_real, f_imag], axis=0)
    rows_parts = np.concatenate(bf16_parts(rows, 3), axis=1)
    eye = np.eye(4)
    cols = np.concatenate([np.kron(eye, f_real.T), np.kron(eye, f_imag.T)], axis=1)
    hi, lo = bf16_parts(cols, 2)
    cols_parts = np.concatenate([hi, hi, lo], axis=0)
    edge = np.cos(np.pi * (index - (SIDE - 1) / 2.0) / SIDE)
    taper = np.tile(edge[:, None] * edge[None, :], (1, 4)).astype(np.float32)
    return rows_parts, cols_parts, taper


def turn_polynomials():
    nodes = 0.25 * np.cos(np.pi * (np.arange(400) + 0.5) / 400) ** 2
    r = np.sqrt(nodes)
    scaled = nodes * 4.0
    sine = np.polynomial.polynomial.polyfit(scaled, np.sin(2 * np.pi * r) / r, 7)
    cosine = np.polynomial.polynomial.polyfit(scaled, np.cos(2 * np.pi * r), 8)
    power = 4.0 ** np.arange(9)
    return [float(a) for a in sine * power[:8]], [float(a) for a in cosine * power]


SINE, COSINE = turn_polynomials()


def unit_circle(turns):
    r = turns - jnp.floor(turns + 0.5)
    r2 = r * r
    s = jnp.full_like(r, SINE[-1])
    for a in SINE[-2::-1]:
        s = s * r2 + a
    c = jnp.full_like(r, COSINE[-1])
    for a in COSINE[-2::-1]:
        c = c * r2 + a
    return c, s * r


def split(x):
    hi = x.astype(BF16)
    return hi, (x - hi.astype(F32)).astype(BF16)


def dot(a, b, contract):
    return lax.dot_general(a, b, ((contract[:1], contract[1:]), ((), ())), preferred_element_type=F32)


def cut_kernel(place_ref, wanted_ref, strip_ref, out_ref, wide_ref):
    wide_ref[...] = strip_ref[...].astype(F32)
    tile = place_ref[0]
    lane = lax.broadcasted_iota(S32, (SIDE, LANES), 1) // SIDE

    def one(i, carry):
        total = jnp.zeros((SIDE, LANES), F32)
        for slot in range(2):
            code = wanted_ref[i, 2 * tile + slot]
            row = code // LANES
            column = code - row * LANES
            for part in range(2):
                piece = wide_ref[part, pl.ds(row, SIDE), :]
                spot = 2 * slot + part
                piece = pltpu.roll(piece, (spot * SIDE + LANES - column) % LANES, 1)
                total = jnp.where(lane == spot, piece, total)
        out_ref[i] = total.astype(BF16)
        return carry

    lax.fori_loop(0, PEERS, one, 0)


def gather_kernel(table_ref, row_ref, patch_ref, out_ref):
    hi, lo = split(table_ref[...])
    table = jnp.concatenate([hi, lo], axis=1)
    ids = lax.broadcasted_iota(S32, (PEERS * ENDS, SCREENS), 1)
    chosen = jnp.where(ids == row_ref[...], 1.0, 0.0).astype(BF16)
    found = dot(chosen, table, (1, 0))
    out_ref[:, 0:16, :] = found[:, :LANES].reshape(PEERS, ENDS, LANES).astype(BF16)
    out_ref[:, 16:32, :] = found[:, LANES:].reshape(PEERS, ENDS, LANES).astype(BF16)
    out_ref[:, 32:64, :] = patch_ref[...]


def scatter_kernel(grads_ref, row_ref, out_ref):
    hi, lo = split(grads_ref[...])
    grads = jnp.concatenate([hi, lo], axis=1)
    ids = lax.broadcasted_iota(S32, (SCREENS, PEERS * ENDS), 0)
    chosen = jnp.where(ids == row_ref[...], 1.0, 0.0).astype(BF16)
    total = dot(chosen, grads, (1, 0))
    out_ref[...] = total[:, :LANES] + total[:, LANES:]


def add_kernel(parts_ref, out_ref):
    total = parts_ref[0]
    for i in range(1, BLOCKS):
        total = total + parts_ref[i]
    for i in range(PEERS):
        part = i // 8
        out_ref[i] = total[part * ENDS : (part + 1) * ENDS, :]


def place_kernel(parts_ref, out_ref):
    lane = lax.broadcasted_iota(S32, (ENDS, LANES), 1) // SIDE
    for block in range(8):
        rows = [parts_ref[4 * block + i] for i in range(4)]
        turned = [[rows[i] if d == 0 else pltpu.roll(rows[i], d * SIDE, 1) for d in range(4)] for i in range(4)]
        for comp in range(4):
            total = turned[0][(0 - comp) % 4]
            for i in range(1, 4):
                total = jnp.where(lane == i, turned[i][(i - comp) % 4], total)
            out_ref[:, comp, block * LANES : (block + 1) * LANES] = total


def main_kernel(slot_ref, got_ref, uv_ref, seen_ref, flag_ref, rows_ref, cols_ref, taper_ref, res_ref, grad_ref, beam_ref):
    got = got_ref[:, 0:16, :].astype(F32) + got_ref[:, 16:32, :].astype(F32)
    beam_ref[...] = got.reshape(PEERS * ENDS, LANES)
    lane = lax.broadcasted_iota(S32, (SIDE, LANES), 1) // SIDE
    centre = (lax.broadcasted_iota(S32, (SIDE, VIS), 0).astype(F32) - SIDE / 2.0) * (1.0 / SIDE)
    taper = taper_ref[...]

    def turn(x, blocks):
        return pltpu.roll(x, blocks * SIDE, 1)

    def one(k, carry):
        slot = slot_ref[k]
        tile = slot // 2
        second = (slot - 2 * tile) > 0
        pieces = [got_ref[8 * i + tile, 32:64, :].astype(F32) for i in range(4)]
        spun = [turn(p, 2) for p in pieces]
        halves = []
        for a, b in ((0, 1), (2, 3)):
            left = jnp.where(second, spun[a], pieces[a])
            right = jnp.where(second, pieces[b], spun[b])
            halves.append(jnp.where(lane < 2, left, right))
        patch = jnp.concatenate(halves, axis=1).astype(BF16)
        patch3 = jnp.concatenate([patch, patch, patch], axis=0)
        a = dot(rows_ref[...], patch3, (1, 0))
        x_re = a[:SIDE, :LANES] - a[SIDE:, LANES:]
        x_im = a[:SIDE, LANES:] + a[SIDE:, :LANES]
        hi, lo = split(jnp.concatenate([x_re, x_im], axis=0))
        b = dot(jnp.concatenate([hi, lo, hi], axis=1), cols_ref[...], (1, 0))
        i_re = b[:SIDE, :LANES] - b[SIDE:, LANES:]
        i_im = b[:SIDE, LANES:] + b[SIDE:, :LANES]

        g = beam_ref[pl.ds(k, SIDE, stride=ENDS), :]
        g1, g2, g3 = turn(g, 1), turn(g, 2), turn(g, 3)
        p_re = jnp.where(lane == 0, g, jnp.where(lane == 3, g2, g1))
        p_im = jnp.where(lane == 0, g2, jnp.where(lane == 3, g, g3))
        g = beam_ref[pl.ds(k + SUBS, SIDE, stride=ENDS), :]
        g2 = turn(g, 2)
        q_re = jnp.where(lane < 2, g, g2)
        q_im = jnp.where(lane < 2, g2, g)

        y_re = i_re * q_re + i_im * q_im
        y_im = i_im * q_re - i_re * q_im
        z_re = (p_re * y_re - p_im * y_im) * taper
        z_im = (p_re * y_im + p_im * y_re) * taper

        eu_re, eu_im = unit_circle(uv_ref[k, 0:1, :] * centre)
        ev_re, ev_im = unit_circle(uv_ref[k, 1:2, :] * centre)
        eu_hi, eu_lo = split(jnp.concatenate([eu_re, eu_im], axis=0))

        z = jnp.concatenate(
            [jnp.concatenate([z_re, z_im], axis=1), jnp.concatenate([-z_im, z_re], axis=1)], axis=0
        )
        z_hi, z_lo = split(z)
        w = dot(
            jnp.concatenate([z_hi, z_lo, z_hi], axis=0),
            jnp.concatenate([eu_hi, eu_hi, eu_lo], axis=0),
            (0, 0),
        )
        reals, imags = [], []
        for pol in range(4):
            w_re = w[pol * SIDE : (pol + 1) * SIDE]
            w_im = w[LANES + pol * SIDE : LANES + (pol + 1) * SIDE]
            reals.append(jnp.sum(w_re * ev_re - w_im * ev_im, axis=0, keepdims=True))
            imags.append(jnp.sum(w_re * ev_im + w_im * ev_re, axis=0, keepdims=True))
        model = jnp.concatenate(reals + imags, axis=0)
        used = flag_ref[pl.ds(k, 1), :].astype(F32)
        res = used * (seen_ref[k] - model)
        res_ref[k] = res
        back = -used * res

        t_re, t_im = [], []
        for pol in range(4):
            d_re = back[pol : pol + 1]
            d_im = back[4 + pol : 5 + pol]
            t_re.append(ev_re * d_re + ev_im * d_im)
            t_im.append(ev_re * d_im - ev_im * d_re)
        t_hi, t_lo = split(jnp.concatenate(t_re + t_im, axis=0))
        both = dot(jnp.concatenate([eu_hi, eu_lo], axis=0), t_hi, (1, 1))
        d = both[: 2 * SIDE] + both[2 * SIDE :] + dot(eu_hi, t_lo, (1, 1))
        dz_re = (d[:SIDE, :LANES] + d[SIDE:, LANES:]) * taper
        dz_im = (d[:SIDE, LANES:] - d[SIDE:, :LANES]) * taper

        dp_re = dz_re * y_re + dz_im * y_im
        dp_im = dz_im * y_re - dz_re * y_im
        dp_re = dp_re + turn(dp_re, 3)
        dp_im = dp_im + turn(dp_im, 3)
        grad_p = jnp.where(
            lane == 0, dp_re, jnp.where(lane == 1, turn(dp_re, 3), jnp.where(lane == 2, turn(dp_im, 2), turn(dp_im, 1)))
        )
        dy_re = dz_re * p_re + dz_im * p_im
        dy_im = dz_im * p_re - dz_re * p_im
        dq_re = dy_re * i_re + dy_im * i_im
        dq_im = dy_re * i_im - dy_im * i_re
        dq_re = dq_re + turn(dq_re, 2)
        dq_im = dq_im + turn(dq_im, 2)
        grad_q = jnp.where(lane < 2, dq_re, dq_im)
        grad_ref[pl.ds(k, SIDE, stride=ENDS), :] = grad_p
        grad_ref[pl.ds(k + SUBS, SIDE, stride=ENDS), :] = grad_q
        return carry

    lax.fori_loop(0, SUBS, one, 0)


SMEM = pl.BlockSpec(memory_space=pltpu.SMEM)
VMEM = pl.BlockSpec(memory_space=pltpu.VMEM)
PARAMS = pltpu.CompilerParams(vmem_limit_bytes=40 * 1024 * 1024)


def call(kernel, shapes, specs, out_specs, scratch=()):
    return pl.pallas_call(
        kernel,
        out_shape=shapes,
        in_specs=specs,
        out_specs=out_specs,
        scratch_shapes=list(scratch),
        compiler_params=PARAMS,
    )


def shape(dims, dtype=F32):
    return jax.ShapeDtypeStruct(dims, dtype)


def cut(place, wanted, grid):
    return pl.pallas_call(
        cut_kernel,
        out_shape=shape((PEERS, SIDE, LANES), BF16),
        grid_spec=pltpu.PrefetchScalarGridSpec(
            num_scalar_prefetch=2,
            grid=(1,),
            in_specs=[pl.BlockSpec((2, grid.shape[1], LANES), lambda i, place, wanted: (place[1], 0, 0))],
            out_specs=pl.BlockSpec((PEERS, SIDE, LANES), lambda i, place, wanted: (0, 0, 0)),
            scratch_shapes=[pltpu.VMEM((2, grid.shape[1], LANES), F32)],
        ),
        compiler_params=PARAMS,
    )(place, wanted, grid)


def exchange(x, axes):
    return lax.all_to_all(x, axes, split_axis=0, concat_axis=0, tiled=True)


ACROSS = ("x", "tile")
DEPTH = ("z", "core")


def body(grid, a_terms, stations, intervals, offsets, uv, observed, flags):
    tile = lax.axis_index("tile").astype(S32)
    mine = lax.dynamic_index_in_dim(a_terms, tile, 0, keepdims=False)
    mine = mine.reshape(2, 4, SIDE, SIDE).transpose(2, 0, 1, 3).reshape(SIDE, 2, LANES)

    ends = jnp.concatenate([stations[:, 0], stations[:, 1]])
    depth = (ends >> 6) * 2 + ((ends >> 3) & 1)
    row = (depth * PEERS + ((ends >> 4) & 3) * 8 + (ends & 7)) * 2 + jnp.concatenate([intervals, intervals])
    owner = offsets[:, 0] >> 8
    same = owner[:, None] == owner[None, :]
    earlier = jnp.arange(SUBS)[:, None] > jnp.arange(SUBS)[None, :]
    slot = owner * 2 + jnp.sum((same & earlier).astype(S32), axis=1)
    code = (offsets[:, 0] & 255) * LANES + offsets[:, 1]
    placed = slot[:, None] == jnp.arange(SLOTS, dtype=S32)[None, :]
    codes = jnp.sum(jnp.where(placed, code[:, None], 0), axis=0)
    asked = jnp.concatenate([row, codes, jnp.zeros((LANES - ENDS - SLOTS,), S32)]).astype(F32)
    asked = jnp.broadcast_to(asked[None, None, :], (PEERS, 1, LANES))

    got_a = exchange(jnp.concatenate([mine, asked, jnp.zeros_like(asked)], axis=1), ACROSS)
    part = got_a[:, :2, :].reshape(1, ROWS, LANES)
    table = exchange(jnp.broadcast_to(part, (BLOCKS, ROWS, LANES)), DEPTH)

    wanted = got_a[:, 2, :].astype(S32)
    rows = wanted[:, :ENDS].reshape(PEERS * ENDS)
    place = jnp.stack([tile, lax.axis_index("x").astype(S32)])
    patches = cut(place, wanted[:, ENDS : ENDS + SLOTS], grid)

    found = call(
        gather_kernel, shape((PEERS, 64, LANES), BF16), [VMEM] * 3, VMEM
    )(table.reshape(SCREENS, LANES), rows[:, None], patches)
    got_c = exchange(found, ACROSS)

    tables = [jnp.asarray(t) for t in dft_tables()]
    result, grads = call(
        main_kernel,
        (shape((SUBS, 8, VIS)), shape((PEERS * ENDS, LANES))),
        [SMEM] + [VMEM] * 7,
        (VMEM, VMEM),
        [pltpu.VMEM((PEERS * ENDS, LANES), F32)],
    )(slot, got_c, uv, observed, flags, *tables)

    back_c = exchange(grads.reshape(PEERS, ENDS, LANES), ACROSS)
    dense = call(
        scatter_kernel, shape((SCREENS, LANES)), [VMEM] * 2, VMEM
    )(back_c.reshape(PEERS * ENDS, LANES), rows[None, :])
    back_b = exchange(dense.reshape(BLOCKS, ROWS, LANES), DEPTH)
    summed = call(add_kernel, shape((PEERS, ENDS, LANES)), [VMEM], VMEM)(back_b)
    back_a = exchange(summed, ACROSS)
    total = call(place_kernel, shape((ENDS, 4, SIDE * SIDE)), [VMEM], VMEM)(back_a)
    return (result, total.reshape(8, 2, 4, SIDE * SIDE))


def solution(mesh):
    fine = Mesh(mesh.devices.reshape(8, 4, 2, 8), ("z", "x", "core", "tile"))
    st = ("z", "x", "core")
    every = ("z", "x", "core", "tile")
    placed = (
        P(None, "tile", None),
        P(st, None, None, None),
        P(every, None),
        P(every),
        P(every, None),
        P(every, None, None),
        P(every, None, None),
        P(every, None),
    )
    return jax.shard_map(
        body,
        mesh=fine,
        in_specs=placed,
        out_specs=(P(every, None, None), P(st, None, None, None)),
        check_vma=False,
    )
```

```python
import jax
import jax.numpy as jnp
import numpy as np
from jax import lax
from jax.experimental import pallas as pl
from jax.experimental.pallas import tpu as pltpu
from jax.sharding import Mesh
from jax.sharding import PartitionSpec as P

SIDE = 32
SUBS = 8
ENDS = 2 * SUBS
VIS = 512
PEERS = 32
LAYERS = 8
ROWS = 64
HALF = LAYERS * ROWS
UNROLL = 8
LANES = 128
SLOTS = 16

F32 = jnp.float32
BF16 = jnp.bfloat16
S32 = jnp.int32


def bf16_parts(array, count):
    rest = np.asarray(array, np.float64)
    parts = []
    for _ in range(count):
        part = rest.astype(np.float32).astype(jnp.bfloat16)
        parts.append(part)
        rest = rest - part.astype(np.float64)
    return parts


def dft_tables():
    index = np.arange(SIDE)
    angle = 2.0 * np.pi * (index[:, None] * index[None, :] % SIDE) / SIDE
    f_real = np.cos(angle) / SIDE
    f_imag = np.sin(angle) / SIDE
    rows = np.concatenate([f_real, f_imag], axis=0)
    rows_parts = np.concatenate(bf16_parts(rows, 3), axis=1)
    eye = np.eye(4)
    cols = np.concatenate([np.kron(eye, f_real.T), np.kron(eye, f_imag.T)], axis=1)
    hi, lo = bf16_parts(cols, 2)
    cols_parts = np.concatenate([hi, hi, lo], axis=0)
    edge = np.cos(np.pi * (index - (SIDE - 1) / 2.0) / SIDE)
    taper = np.tile(edge[:, None] * edge[None, :], (1, 4)).astype(np.float32)
    return rows_parts, cols_parts, taper


def turn_polynomials():
    nodes = 0.25 * np.cos(np.pi * (np.arange(400) + 0.5) / 400) ** 2
    r = np.sqrt(nodes)
    scaled = nodes * 4.0
    sine = np.polynomial.polynomial.polyfit(scaled, np.sin(2 * np.pi * r) / r, 7)
    cosine = np.polynomial.polynomial.polyfit(scaled, np.cos(2 * np.pi * r), 8)
    power = 4.0 ** np.arange(9)
    return [float(a) for a in sine * power[:8]], [float(a) for a in cosine * power]


SINE, COSINE = turn_polynomials()


def unit_circle(turns):
    r = turns - jnp.floor(turns + 0.5)
    r2 = r * r
    s = jnp.full_like(r, SINE[-1])
    for a in SINE[-2::-1]:
        s = s * r2 + a
    c = jnp.full_like(r, COSINE[-1])
    for a in COSINE[-2::-1]:
        c = c * r2 + a
    return c, s * r


def split(x):
    hi = x.astype(BF16)
    return hi, (x - hi.astype(F32)).astype(BF16)


def dot(a, b, contract):
    return lax.dot_general(a, b, ((contract[:1], contract[1:]), ((), ())), preferred_element_type=F32)


def slots(offsets_ref):
    tiles = [offsets_ref[0, k] >> 8 for k in range(SUBS)]
    seconds = []
    for k in range(SUBS):
        second = jnp.zeros((), S32)
        for j in range(k):
            second = jnp.where(tiles[j] == tiles[k], 1, second)
        seconds.append(second)
    return tiles, seconds


def prep_kernel(
    stations_in, intervals_in, offsets_in, terms_in, out_ref, stations_ref, intervals_ref, offsets_ref, terms_ref, sems
):
    own = lax.axis_index("tile")
    copies = [
        pltpu.make_async_copy(stations_in, stations_ref, sems.at[0]),
        pltpu.make_async_copy(intervals_in, intervals_ref, sems.at[1]),
        pltpu.make_async_copy(offsets_in, offsets_ref, sems.at[2]),
        pltpu.make_async_copy(terms_in.at[own], terms_ref, sems.at[3]),
    ]
    for copy in copies:
        copy.start()
    for copy in copies[:3]:
        copy.wait()
    spot = lax.broadcasted_iota(S32, (1, LANES), 1)
    asked = jnp.zeros((1, LANES), S32)
    tiles, seconds = slots(offsets_ref)
    for k in range(SUBS):
        for end in range(2):
            station = stations_ref[end, k]
            depth = ((station >> 3) & 1) * LAYERS + (station >> 6)
            row = depth * ROWS + (((station >> 4) & 3) * 8 + (station & 7)) * 2 + intervals_ref[k]
            asked = jnp.where(spot == end * SUBS + k, row, asked)
        code = (offsets_ref[0, k] & 255) * LANES + offsets_ref[1, k]
        asked = jnp.where(spot == ENDS + 2 * tiles[k] + seconds[k], code, asked)
    out_ref[:, 2:4, :] = jnp.broadcast_to(asked.astype(F32).reshape(1, 1, LANES), (PEERS, 2, LANES))
    copies[3].wait()
    lane = lax.broadcasted_iota(S32, (2, LANES), 1) // SIDE
    for block in range(8):
        comps = [terms_ref[:, comp, block * LANES : (block + 1) * LANES] for comp in range(4)]
        for i in range(4):
            total = comps[i]
            for comp in range(4):
                if comp != i:
                    total = jnp.where(lane == comp, pltpu.roll(comps[comp], (comp - i) % 4 * SIDE, 1), total)
            out_ref[4 * block + i, 0:2, :] = total


def wave_kernel(uv_ref, row_wave_ref, column_wave_ref):
    centre = (lax.broadcasted_iota(S32, (SIDE, VIS), 0).astype(F32) - SIDE / 2.0) * (1.0 / SIDE)

    def one(k, carry):
        real, imag = unit_circle(uv_ref[k, 0:1, :] * centre)
        hi, lo = split(jnp.concatenate([real, imag], axis=0))
        row_wave_ref[k] = jnp.concatenate([hi, hi, lo], axis=0)
        real, imag = unit_circle(uv_ref[k, 1:2, :] * centre)
        column_wave_ref[k] = jnp.concatenate([real, imag], axis=0)
        return carry

    lax.fori_loop(0, SUBS, one, 0)


def cut_kernel(place_ref, wanted_ref, strip_ref, out_ref, wide_ref):
    wide_ref[...] = strip_ref[...].astype(F32)
    tile = place_ref[0]
    lane = lax.broadcasted_iota(S32, (SIDE, LANES), 1) // SIDE

    def one(i, carry):
        total = jnp.zeros((SIDE, LANES), F32)
        for slot in range(2):
            code = wanted_ref[i, 2 * tile + slot]
            row = code >> 7
            column = code & (LANES - 1)
            for part in range(2):
                spot = 2 * slot + part
                piece = wide_ref[part, pl.ds(row, SIDE), :]
                piece = pltpu.roll(piece, (spot * SIDE + LANES - column) & (LANES - 1), 1)
                total = jnp.where(lane == spot, piece, total)
        out_ref[i] = total.astype(BF16)
        return carry

    lax.fori_loop(0, PEERS, one, 0, unroll=4)


def spread_kernel(got_ref, out_ref):
    part = got_ref[:, 0:2, :].reshape(ROWS, LANES)
    for i in range(LAYERS):
        out_ref[i] = part


def pick(table, rows, first):
    hi, lo = split(table)
    ids = lax.broadcasted_iota(S32, (PEERS * ENDS, HALF), 1) + first
    chosen = jnp.where(ids == rows, 1.0, 0.0).astype(BF16)
    return dot(chosen, jnp.concatenate([hi, lo], axis=1), (1, 0))


def near_kernel(place_ref, table_ref, row_ref, out_ref):
    out_ref[...] = pick(table_ref[...], row_ref[...], HALF * place_ref[2]).astype(BF16)


def gather_kernel(place_ref, table_ref, row_ref, near_ref, patch_ref, out_ref):
    found = pick(table_ref[...], row_ref[...], HALF * (1 - place_ref[2])) + near_ref[...].astype(F32)
    out_ref[:, 0:16, :] = found[:, :LANES].reshape(PEERS, ENDS, LANES).astype(BF16)
    out_ref[:, 16:32, :] = found[:, LANES:].reshape(PEERS, ENDS, LANES).astype(BF16)
    out_ref[:, 32:64, :] = patch_ref[...]


def scatter_kernel(first_ref, grads_ref, row_ref, out_ref):
    hi, lo = split(grads_ref[...])
    grads = jnp.concatenate([hi, lo], axis=1)
    ids = lax.broadcasted_iota(S32, (HALF, PEERS * ENDS), 0) + first_ref[0]
    chosen = jnp.where(ids == row_ref[...], 1.0, 0.0).astype(BF16)
    total = dot(chosen, grads, (1, 0))
    out_ref[...] = total[:, :LANES] + total[:, LANES:]


def pair_kernel(keep_ref, other_ref, out_ref):
    out_ref[...] = keep_ref[...] + other_ref[...]


def add_kernel(parts_ref, out_ref):
    total = parts_ref[0]
    for i in range(1, LAYERS):
        total = total + parts_ref[i]
    for i in range(PEERS):
        part = i // 8
        out_ref[i] = total[part * ENDS : (part + 1) * ENDS, :]


def place_kernel(parts_ref, out_ref):
    lane = lax.broadcasted_iota(S32, (ENDS, LANES), 1) // SIDE
    for block in range(8):
        rows = [parts_ref[4 * block + i] for i in range(4)]
        turned = [[rows[i] if d == 0 else pltpu.roll(rows[i], d * SIDE, 1) for d in range(4)] for i in range(4)]
        for comp in range(4):
            total = turned[0][(0 - comp) % 4]
            for i in range(1, 4):
                total = jnp.where(lane == i, turned[i][(i - comp) % 4], total)
            out_ref[:, comp, block * LANES : (block + 1) * LANES] = total


def main_kernel(
    slot_ref, got_ref, row_wave_in, column_wave_in, seen_in, flag_in, rows_ref, cols_ref, taper_ref,
    res_ref, grad_ref, beam_ref, row_wave_ref, column_wave_ref, seen_ref, flag_ref, side_ref, z_ref, dz_ref, sems,
):
    copies = [
        pltpu.make_async_copy(a, b, sems.at[i])
        for i, (a, b) in enumerate(
            ((row_wave_in, row_wave_ref), (column_wave_in, column_wave_ref), (seen_in, seen_ref), (flag_in, flag_ref))
        )
    ]
    for copy in copies:
        copy.start()
    got = got_ref[:, 0:16, :].astype(F32) + got_ref[:, 16:32, :].astype(F32)
    beam_ref[...] = got.reshape(PEERS * ENDS, LANES)
    lane = lax.broadcasted_iota(S32, (SIDE, LANES), 1) // SIDE
    taper = taper_ref[...]

    def turn(x, blocks):
        return pltpu.roll(x, blocks * SIDE, 1)

    patches = []
    for k in range(SUBS):
        slot = slot_ref[k]
        tile = slot >> 1
        second = (slot & 1) > 0
        pieces = [got_ref[8 * i + tile, 32:64, :].astype(F32) for i in range(4)]
        for a, b in ((0, 1), (2, 3)):
            left = jnp.where(second, turn(pieces[a], 2), pieces[a])
            right = jnp.where(second, pieces[b], turn(pieces[b], 2))
            patches.append(jnp.where(lane < 2, left, right).astype(BF16))
    patch = jnp.concatenate(patches, axis=1)
    a = dot(rows_ref[...], jnp.concatenate([patch, patch, patch], axis=0), (1, 0))
    mixed = []
    for k in range(SUBS):
        re = a[:, 2 * k * LANES : (2 * k + 1) * LANES]
        im = a[:, (2 * k + 1) * LANES : (2 * k + 2) * LANES]
        mixed += [re[:SIDE] - im[SIDE:], im[:SIDE] + re[SIDE:]]
    hi, lo = split(jnp.concatenate(mixed, axis=0))
    images = dot(jnp.concatenate([hi, lo, hi], axis=1), cols_ref[...], (1, 0))

    for k in range(SUBS):
        b = images[2 * k * SIDE : 2 * (k + 1) * SIDE]
        i_re = b[:SIDE, :LANES] - b[SIDE:, LANES:]
        i_im = b[:SIDE, LANES:] + b[SIDE:, :LANES]

        g = beam_ref[pl.ds(k, SIDE, stride=ENDS), :]
        g1, g2, g3 = turn(g, 1), turn(g, 2), turn(g, 3)
        p_re = jnp.where(lane == 0, g, jnp.where(lane == 3, g2, g1))
        p_im = jnp.where(lane == 0, g2, jnp.where(lane == 3, g, g3))
        g = beam_ref[pl.ds(k + SUBS, SIDE, stride=ENDS), :]
        g2 = turn(g, 2)
        q_re = jnp.where(lane < 2, g, g2)
        q_im = jnp.where(lane < 2, g2, g)

        y_re = i_re * q_re + i_im * q_im
        y_im = i_im * q_re - i_re * q_im
        z_re = (p_re * y_re - p_im * y_im) * taper
        z_im = (p_re * y_im + p_im * y_re) * taper
        for i, part in enumerate((i_re, i_im, p_re, p_im, y_re, y_im)):
            side_ref[k, i] = part * taper if i > 3 else part
        z = jnp.concatenate(
            [jnp.concatenate([z_re, z_im], axis=1), jnp.concatenate([-z_im, z_re], axis=1)], axis=0
        )
        z_hi, z_lo = split(z)
        z_ref[k] = jnp.concatenate([z_hi, z_lo, z_hi], axis=0)

    for copy in copies:
        copy.wait()

    def one(k, carry):
        row_wave = row_wave_ref[k]
        ev_re = column_wave_ref[k, :SIDE, :]
        ev_im = column_wave_ref[k, SIDE:, :]
        w = dot(z_ref[k], row_wave, (0, 0))
        reals, imags = [], []
        for pol in range(4):
            w_re = w[pol * SIDE : (pol + 1) * SIDE]
            w_im = w[LANES + pol * SIDE : LANES + (pol + 1) * SIDE]
            reals.append(jnp.sum(w_re * ev_re - w_im * ev_im, axis=0, keepdims=True))
            imags.append(jnp.sum(w_re * ev_im + w_im * ev_re, axis=0, keepdims=True))
        model = jnp.concatenate(reals + imags, axis=0)
        used = flag_ref[pl.ds(k, 1), :].astype(F32)
        res = used * (seen_ref[k] - model)
        res_ref[k] = res
        back = -used * res

        t_re, t_im = [], []
        for pol in range(4):
            d_re = back[pol : pol + 1]
            d_im = back[4 + pol : 5 + pol]
            t_re.append(ev_re * d_re + ev_im * d_im)
            t_im.append(ev_re * d_im - ev_im * d_re)
        t_hi, t_lo = split(jnp.concatenate(t_re + t_im, axis=0))
        both = dot(row_wave[2 * SIDE :], t_hi, (1, 1))
        dz_ref[k] = both[: 2 * SIDE] + both[2 * SIDE :] + dot(row_wave[: 2 * SIDE], t_lo, (1, 1))
        return carry

    lax.fori_loop(0, SUBS, one, 0, unroll=UNROLL)

    for k in range(SUBS):
        d = dz_ref[k]
        i_re, i_im, p_re, p_im, y_re, y_im = (side_ref[k, i] for i in range(6))
        dz_re = d[:SIDE, :LANES] + d[SIDE:, LANES:]
        dz_im = d[:SIDE, LANES:] - d[SIDE:, :LANES]

        dp_re = dz_re * y_re + dz_im * y_im
        dp_im = dz_im * y_re - dz_re * y_im
        dp_re = dp_re + turn(dp_re, 3)
        dp_im = dp_im + turn(dp_im, 3)
        grad_p = jnp.where(
            lane == 0, dp_re, jnp.where(lane == 1, turn(dp_re, 3), jnp.where(lane == 2, turn(dp_im, 2), turn(dp_im, 1)))
        )
        i_re = i_re * taper
        i_im = i_im * taper
        dy_re = dz_re * p_re + dz_im * p_im
        dy_im = dz_im * p_re - dz_re * p_im
        dq_re = dy_re * i_re + dy_im * i_im
        dq_im = dy_re * i_im - dy_im * i_re
        dq_re = dq_re + turn(dq_re, 2)
        dq_im = dq_im + turn(dq_im, 2)
        grad_ref[pl.ds(k, SIDE, stride=ENDS), :] = grad_p
        grad_ref[pl.ds(k + SUBS, SIDE, stride=ENDS), :] = jnp.where(lane < 2, dq_re, dq_im)


SMEM = pl.BlockSpec(memory_space=pltpu.SMEM)
VMEM = pl.BlockSpec(memory_space=pltpu.VMEM)
HBM = pl.BlockSpec(memory_space=pltpu.HBM)
WAVES = pl.BlockSpec(memory_space=pl.ANY)
PARAMS = pltpu.CompilerParams(vmem_limit_bytes=40 * 1024 * 1024)


def call(kernel, shapes, specs, out_specs, scratch=()):
    return pl.pallas_call(
        kernel,
        out_shape=shapes,
        in_specs=specs,
        out_specs=out_specs,
        scratch_shapes=list(scratch),
        compiler_params=PARAMS,
    )


def shape(dims, dtype=F32):
    return jax.ShapeDtypeStruct(dims, dtype)


def cut(place, wanted, grid):
    return pl.pallas_call(
        cut_kernel,
        out_shape=shape((PEERS, SIDE, LANES), BF16),
        grid_spec=pltpu.PrefetchScalarGridSpec(
            num_scalar_prefetch=2,
            grid=(1,),
            in_specs=[pl.BlockSpec((2, grid.shape[1], LANES), lambda i, place, wanted: (place[1], 0, 0))],
            out_specs=pl.BlockSpec((PEERS, SIDE, LANES), lambda i, place, wanted: (0, 0, 0)),
            scratch_shapes=[pltpu.VMEM((2, grid.shape[1], LANES), F32)],
        ),
        compiler_params=PARAMS,
    )(place, wanted, grid)


def in_hbm(x):
    return pltpu.with_memory_space_constraint(x, pltpu.HBM)


def exchange(x, axes):
    return lax.all_to_all(x, axes, split_axis=0, concat_axis=0, tiled=True)


def main(*args):
    tables = [jnp.asarray(t) for t in dft_tables()]
    return call(
        main_kernel,
        (shape((SUBS, 8, VIS)), shape((PEERS * ENDS, LANES))),
        [SMEM, VMEM] + [WAVES] * 2 + [HBM] * 2 + [VMEM] * 3,
        (VMEM, VMEM),
        [
            pltpu.VMEM((PEERS * ENDS, LANES), F32),
            pltpu.VMEM((SUBS, 6 * SIDE, VIS), BF16),
            pltpu.VMEM((SUBS, 2 * SIDE, VIS), F32),
            pltpu.VMEM((SUBS, 8, VIS), F32),
            pltpu.VMEM((SUBS, VIS), S32),
            pltpu.VMEM((SUBS, 6, SIDE, LANES), F32),
            pltpu.VMEM((SUBS, 6 * SIDE, 2 * LANES), BF16),
            pltpu.VMEM((SUBS, 2 * SIDE, 2 * LANES), F32),
            pltpu.SemaphoreType.DMA((4,)),
        ],
    )(*args, *tables)


ACROSS = ("x", "tile")
SWAP = ((0, 1), (1, 0))


def body(grid, a_terms, stations, intervals, offsets, uv, observed, flags):
    place = jnp.stack([lax.axis_index(name).astype(S32) for name in ("tile", "x", "core")])
    offsets = offsets.T
    sent = call(
        prep_kernel,
        shape((PEERS, 4, LANES)),
        [HBM] * 4,
        VMEM,
        [
            pltpu.SMEM((2, SUBS), S32),
            pltpu.SMEM((SUBS,), S32),
            pltpu.SMEM((2, SUBS), S32),
            pltpu.VMEM((2, 4, SIDE * SIDE), F32),
            pltpu.SemaphoreType.DMA((4,)),
        ],
    )(*(in_hbm(x) for x in (stations.T, intervals, offsets, a_terms)))
    got_a = exchange(sent, ACROSS)
    spread = call(spread_kernel, shape((LAYERS, ROWS, LANES)), [VMEM], VMEM)(got_a)
    own = exchange(spread, "z").reshape(HALF, LANES)

    wanted = got_a[:, 2, :].astype(S32)
    rows = wanted[:, :ENDS].reshape(PEERS * ENDS)
    patches = cut(place, wanted[:, ENDS : ENDS + SLOTS], grid)
    own, patches = lax.optimization_barrier((own, patches))
    other = lax.ppermute(own, "core", SWAP)
    waves = call(
        wave_kernel, (shape((SUBS, 6 * SIDE, VIS), BF16), shape((SUBS, 2 * SIDE, VIS))), [VMEM], (VMEM, VMEM)
    )(uv)

    column = rows[:, None]
    near = call(near_kernel, shape((PEERS * ENDS, 2 * LANES), BF16), [SMEM] + [VMEM] * 2, VMEM)(place, own, column)
    found = call(
        gather_kernel, shape((PEERS, 64, LANES), BF16), [SMEM] + [VMEM] * 4, VMEM
    )(place, other, column, near, patches)
    got_c = exchange(found, ACROSS)

    owner = offsets[0] >> 8
    same = owner[:, None] == owner[None, :]
    earlier = jnp.arange(SUBS)[:, None] > jnp.arange(SUBS)[None, :]
    slot = owner * 2 + jnp.sum((same & earlier).astype(S32), axis=1)
    result, grads = main(slot, got_c, *waves, observed, flags)

    back_c = exchange(grads.reshape(PEERS, ENDS, LANES), ACROSS)
    half = shape((HALF, LANES))
    back_c = back_c.reshape(PEERS * ENDS, LANES)
    first = HALF * place[2:3]
    scatter = call(scatter_kernel, half, [SMEM, VMEM, VMEM], VMEM)
    lend = scatter(HALF - first, back_c, rows[None, :])
    other = lax.ppermute(lend, "core", SWAP)
    keep = scatter(first, back_c, rows[None, :])
    dense = call(pair_kernel, half, [VMEM] * 2, VMEM)(keep, other)
    back_b = exchange(dense.reshape(LAYERS, ROWS, LANES), "z")
    summed = call(add_kernel, shape((PEERS, ENDS, LANES)), [VMEM], VMEM)(back_b)
    back_a = exchange(summed, ACROSS)
    total = call(place_kernel, shape((ENDS, 4, SIDE * SIDE)), [VMEM], VMEM)(back_a)
    return (result, total.reshape(8, 2, 4, SIDE * SIDE))


def solution(mesh):
    fine = Mesh(mesh.devices.reshape(8, 4, 2, 8), ("z", "x", "core", "tile"))
    st = ("z", "x", "core")
    every = ("z", "x", "core", "tile")
    placed = (
        P(None, "tile", None),
        P(st, None, None, None),
        P(every, None),
        P(every),
        P(every, None),
        P(every, None, None),
        P(every, None, None),
        P(every, None),
    )
    return jax.shard_map(
        body,
        mesh=fine,
        in_specs=placed,
        out_specs=(P(every, None, None), P(st, None, None, None)),
        check_vma=False,
    )
```

```python
import jax
import jax.numpy as jnp
import numpy as np
from jax import lax
from jax.experimental import pallas as pl
from jax.experimental.pallas import tpu as pltpu
from jax.sharding import Mesh
from jax.sharding import PartitionSpec as P

SIDE = 32
SUBS = 8
ENDS = 2 * SUBS
VIS = 512
PEERS = 64
GROUPS = 8
ROWS = 64
TABLE = GROUPS * ROWS
LANES = 128
SLOTS = 16

F32 = jnp.float32
BF16 = jnp.bfloat16
S32 = jnp.int32


def bf16_parts(array, count):
    rest = np.asarray(array, np.float64)
    parts = []
    for _ in range(count):
        part = rest.astype(np.float32).astype(jnp.bfloat16)
        parts.append(part)
        rest = rest - part.astype(np.float64)
    return parts


def dft_tables():
    index = np.arange(SIDE)
    angle = 2.0 * np.pi * (index[:, None] * index[None, :] % SIDE) / SIDE
    f_real = np.cos(angle) / SIDE
    f_imag = np.sin(angle) / SIDE
    rows = np.concatenate([f_real, f_imag], axis=0)
    rows_parts = np.concatenate(bf16_parts(rows, 3), axis=1)
    eye = np.eye(4)
    cols = np.concatenate([np.kron(eye, f_real.T), np.kron(eye, f_imag.T)], axis=1)
    hi, lo = bf16_parts(cols, 2)
    cols_parts = np.concatenate([hi, hi, lo], axis=0)
    edge = np.cos(np.pi * (index - (SIDE - 1) / 2.0) / SIDE)
    taper = np.tile(edge[:, None] * edge[None, :], (1, 4)).astype(np.float32)
    return rows_parts, cols_parts, taper


def turn_polynomials():
    nodes = 0.25 * np.cos(np.pi * (np.arange(400) + 0.5) / 400) ** 2
    r = np.sqrt(nodes)
    scaled = nodes * 4.0
    sine = np.polynomial.polynomial.polyfit(scaled, np.sin(2 * np.pi * r) / r, 7)
    cosine = np.polynomial.polynomial.polyfit(scaled, np.cos(2 * np.pi * r), 8)
    power = 4.0 ** np.arange(9)
    return [float(a) for a in sine * power[:8]], [float(a) for a in cosine * power]


SINE, COSINE = turn_polynomials()


def unit_circle(turns):
    r = turns - jnp.floor(turns + 0.5)
    r2 = r * r
    s = jnp.full_like(r, SINE[-1])
    for a in SINE[-2::-1]:
        s = s * r2 + a
    c = jnp.full_like(r, COSINE[-1])
    for a in COSINE[-2::-1]:
        c = c * r2 + a
    return c, s * r


def split(x):
    hi = x.astype(BF16)
    return hi, (x - hi.astype(F32)).astype(BF16)


def dot(a, b, contract):
    return lax.dot_general(a, b, ((contract[:1], contract[1:]), ((), ())), preferred_element_type=F32)


def slots(offsets_ref):
    tiles = [offsets_ref[0, k] >> 8 for k in range(SUBS)]
    seconds = []
    for k in range(SUBS):
        second = jnp.zeros((), S32)
        for j in range(k):
            second = jnp.where(tiles[j] == tiles[k], 1, second)
        seconds.append(second)
    return tiles, seconds


def prep_kernel(
    stations_in, intervals_in, offsets_in, terms_in, out_ref, stations_ref, intervals_ref, offsets_ref, terms_ref, sems
):
    own = lax.axis_index("tile")
    copies = [
        pltpu.make_async_copy(stations_in, stations_ref, sems.at[0]),
        pltpu.make_async_copy(intervals_in, intervals_ref, sems.at[1]),
        pltpu.make_async_copy(offsets_in, offsets_ref, sems.at[2]),
        pltpu.make_async_copy(terms_in.at[own], terms_ref, sems.at[3]),
    ]
    for copy in copies:
        copy.start()
    for copy in copies[:3]:
        copy.wait()
    spot = lax.broadcasted_iota(S32, (1, LANES), 1)
    asked = jnp.zeros((1, LANES), S32)
    tiles, seconds = slots(offsets_ref)
    for k in range(SUBS):
        for end in range(2):
            station = stations_ref[end, k]
            row = ((station >> 3) & 7) * ROWS + (station >> 6) * 8 + (station & 7)
            asked = jnp.where(spot == end * SUBS + k, row + TABLE * intervals_ref[k], asked)
        code = (offsets_ref[0, k] & 255) * LANES + offsets_ref[1, k]
        asked = jnp.where(spot == ENDS + 2 * tiles[k] + seconds[k], code, asked)
    out_ref[:, 1:2, :] = jnp.broadcast_to(asked.astype(F32).reshape(1, 1, LANES), (PEERS, 1, LANES))
    copies[3].wait()
    lane = spot // SIDE
    for block in range(8):
        turned = []
        for interval in range(2):
            comps = terms_ref[interval, :, block * LANES : (block + 1) * LANES]
            turned.append([comps if d == 0 else pltpu.roll(comps, d * SIDE, 1) for d in range(4)])
        for i in range(4):
            for half in range(2):
                total = jnp.zeros((1, LANES), F32)
                for place in range(4):
                    comp = 2 * half + (place & 1)
                    piece = turned[place >> 1][(place - i) % 4][comp : comp + 1, :]
                    total = piece if place == 0 else jnp.where(lane == place, piece, total)
                out_ref[(4 * block + i) * 2 + half, 0:1, :] = total


def wave_kernel(uv_ref, row_wave_ref, column_wave_ref):
    centre = (lax.broadcasted_iota(S32, (SIDE, VIS), 0).astype(F32) - SIDE / 2.0) * (1.0 / SIDE)

    def one(k, carry):
        real, imag = unit_circle(uv_ref[k, 0:1, :] * centre)
        hi, lo = split(jnp.concatenate([real, imag], axis=0))
        row_wave_ref[k] = jnp.concatenate([hi, lo], axis=0)
        real, imag = unit_circle(uv_ref[k, 1:2, :] * centre)
        column_wave_ref[k] = jnp.concatenate([real, imag], axis=0)
        return carry

    lax.fori_loop(0, SUBS, one, 0)


def cut_kernel(place_ref, wanted_ref, strip_ref, out_ref, wide_ref):
    wide_ref[...] = strip_ref[0].astype(F32)
    tile = place_ref[0]
    part_of = place_ref[1]
    half = SIDE // 2
    lane = lax.broadcasted_iota(S32, (half, LANES), 1) // SIDE

    def one(i, carry):
        total = jnp.zeros((half, LANES), F32)
        for slot in range(2):
            code = wanted_ref[i, 2 * tile + slot]
            row = code >> 7
            column = code & (LANES - 1)
            for part in range(2):
                spot = (part_of + 2 * slot + part) & 3
                piece = wide_ref[pl.ds(row + half * part, half), :]
                piece = pltpu.roll(piece, (spot * SIDE + LANES - column) & (LANES - 1), 1)
                total = jnp.where(lane == spot, piece, total)
        out_ref[i] = total.astype(BF16)
        return carry

    lax.fori_loop(0, PEERS, one, 0, unroll=8)


def spread_kernel(got_ref, out_ref):
    part = got_ref[:, 0:1, :].reshape(ROWS, LANES)
    for i in range(GROUPS):
        out_ref[i] = part


def gather_kernel(table_ref, first_ref, second_ref, patch_ref, out_ref):
    hi, lo = split(table_ref[...])
    table = jnp.concatenate([hi, lo], axis=1)
    ids = lax.broadcasted_iota(S32, (TABLE, TABLE), 1)
    left = lax.broadcasted_iota(S32, (TABLE, LANES), 1) < LANES // 2
    sides = []
    for code_ref in (first_ref, second_ref):
        code = code_ref[...]
        chosen = jnp.where(ids == (code & (TABLE - 1)), 1.0, 0.0).astype(BF16)
        found = dot(chosen, table, (1, 0))
        found = found[:, :LANES] + found[:, LANES:]
        sides.append((found, pltpu.roll(found, LANES // 2, 1), code >= TABLE))
    first = jnp.where(sides[0][2], sides[0][1], sides[0][0])
    second = jnp.where(sides[1][2], sides[1][0], sides[1][1])
    beams = jnp.where(left, first, second)
    hi = beams.astype(BF16).astype(F32)
    both = jnp.concatenate([hi.reshape(PEERS, SUBS, LANES), (beams - hi).reshape(PEERS, SUBS, LANES)], axis=1)
    out_ref[:, 0:ENDS, :] = both.astype(BF16)
    out_ref[:, ENDS : 2 * ENDS, :] = patch_ref[...]


def scatter_kernel(got_ref, first_ref, second_ref, first_row_ref, second_row_ref, out_ref):
    got = got_ref[...]
    turned = pltpu.roll(got, LANES // 2, 1)
    left = lax.broadcasted_iota(S32, (TABLE, LANES), 1) < LANES // 2
    ids = lax.broadcasted_iota(S32, (TABLE, TABLE), 0)
    values, chosen = [], []
    for spread, code_ref, row_ref in (
        (jnp.where(left, got, turned), first_ref, first_row_ref),
        (jnp.where(left, turned, got), second_ref, second_row_ref),
    ):
        late = code_ref[...] >= TABLE
        values.append(jnp.where(late != left, spread, 0.0))
        chosen.append(jnp.where(ids == (row_ref[...] & (TABLE - 1)), 1.0, 0.0).astype(BF16))
    hi, lo = split(jnp.concatenate(values, axis=0))
    total = dot(jnp.concatenate(chosen, axis=1), jnp.concatenate([hi, lo], axis=1), (1, 0))
    out_ref[...] = total[:, :LANES] + total[:, LANES:]


def add_kernel(parts_ref, out_ref):
    total = parts_ref[0]
    for i in range(1, GROUPS):
        total = total + parts_ref[i]
    for i in range(PEERS):
        part = i // 8
        out_ref[i] = total[part * SUBS : (part + 1) * SUBS, :]


def place_kernel(parts_ref, out_ref):
    lane = lax.broadcasted_iota(S32, (SUBS, LANES), 1) // SIDE
    for block in range(8):
        for half in range(2):
            rows = [parts_ref[2 * (4 * block + i) + half] for i in range(4)]
            turned = [[rows[i] if d == 0 else pltpu.roll(rows[i], d * SIDE, 1) for d in range(4)] for i in range(4)]
            for interval in range(2):
                for part in range(2):
                    at = 2 * interval + part
                    total = turned[0][(0 - at) % 4]
                    for i in range(1, 4):
                        total = jnp.where(lane == i, turned[i][(i - at) % 4], total)
                    out_ref[:, interval, 2 * half + part, block * LANES : (block + 1) * LANES] = total


def main_kernel(
    slot_ref, got_ref, row_wave_in, column_wave_in, seen_in, flag_in, rows_ref, cols_ref, taper_ref,
    res_ref, grad_ref, beam_ref, row_wave_ref, column_wave_ref, seen_ref, flag_ref, side_ref, z_ref, dz_ref, held_ref, sems,
):
    copies = [
        pltpu.make_async_copy(a, b, sems.at[i])
        for i, (a, b) in enumerate(
            ((row_wave_in, row_wave_ref), (column_wave_in, column_wave_ref), (seen_in, seen_ref), (flag_in, flag_ref))
        )
    ]
    for copy in copies:
        copy.start()
    got = got_ref[:, 0:ENDS, :].astype(F32)
    beam_ref[...] = (got[:, :SUBS] + got[:, SUBS:]).reshape(TABLE, LANES)
    narrow = lax.broadcasted_iota(S32, (SIDE // 2, LANES), 1) // SIDE
    lane = lax.broadcasted_iota(S32, (SIDE, LANES), 1) // SIDE
    taper = taper_ref[...]

    def turn(x, blocks):
        return pltpu.roll(x, blocks * SIDE, 1)

    patches = []
    for k in range(SUBS):
        slot = slot_ref[k]
        tile = slot >> 1
        second = (slot & 1) > 0
        shift = 2 * (slot & 1)
        upper = (narrow - shift) & 3
        lower = (narrow - shift - 1) & 3
        for part in range(2):
            top = jnp.zeros((SIDE // 2, LANES), F32)
            low = top
            for i in range(4):
                piece = got_ref[8 * (4 * part + i) + tile, ENDS : 2 * ENDS, :].astype(F32)
                top = jnp.where(upper == i, piece, top)
                low = jnp.where(lower == i, piece, low)
            top = jnp.where(second, turn(top, 2), top)
            low = jnp.where(second, turn(low, 1), turn(low, 3))
            patches.append(jnp.concatenate([top, low], axis=0).astype(BF16))
    patch = jnp.concatenate(patches, axis=1)
    a = dot(rows_ref[...], jnp.concatenate([patch, patch, patch], axis=0), (1, 0))
    mixed = []
    for k in range(SUBS):
        re = a[:, 2 * k * LANES : (2 * k + 1) * LANES]
        im = a[:, (2 * k + 1) * LANES : (2 * k + 2) * LANES]
        mixed += [re[:SIDE] - im[SIDE:], im[:SIDE] + re[SIDE:]]
    hi, lo = split(jnp.concatenate(mixed, axis=0))
    images = dot(jnp.concatenate([hi, lo, hi], axis=1), cols_ref[...], (1, 0))

    for k in range(SUBS):
        b = images[2 * k * SIDE : 2 * (k + 1) * SIDE]
        i_re = b[:SIDE, :LANES] - b[SIDE:, LANES:]
        i_im = b[:SIDE, LANES:] + b[SIDE:, :LANES]

        sides = []
        for half in range(2):
            g = beam_ref[pl.ds(k + SUBS * half, SIDE, stride=2 * SUBS), :]
            g1, g2 = turn(g, 1), turn(g, 2)
            sides.append((jnp.where(lane == 0, g, jnp.where(lane == 3, g2, g1)), jnp.where(lane < 2, g2, g)))
        (p_re, q_re), (p_im, q_im) = sides

        y_re = i_re * q_re + i_im * q_im
        y_im = i_im * q_re - i_re * q_im
        z_re = (p_re * y_re - p_im * y_im) * taper
        z_im = (p_re * y_im + p_im * y_re) * taper
        for i, part in enumerate((i_re, i_im, p_re, p_im, y_re, y_im)):
            side_ref[k, i] = part * taper if i > 3 else part
        z = jnp.concatenate(
            [jnp.concatenate([z_re, z_im], axis=1), jnp.concatenate([-z_im, z_re], axis=1)], axis=0
        )
        z_hi, z_lo = split(z)
        z_ref[k] = jnp.concatenate([z_hi, z_lo, z_hi], axis=0)

    for copy in copies:
        copy.wait()

    def one(k, carry):
        row_wave = row_wave_ref[k]
        ev_re = column_wave_ref[k, :SIDE, :]
        ev_im = column_wave_ref[k, SIDE:, :]
        w = dot(z_ref[k], jnp.concatenate([row_wave[: 2 * SIDE], row_wave], axis=0), (0, 0))
        reals, imags = [], []
        for pol in range(4):
            w_re = w[pol * SIDE : (pol + 1) * SIDE]
            w_im = w[LANES + pol * SIDE : LANES + (pol + 1) * SIDE]
            reals.append(jnp.sum(w_re * ev_re - w_im * ev_im, axis=0, keepdims=True))
            imags.append(jnp.sum(w_re * ev_im + w_im * ev_re, axis=0, keepdims=True))
        model = jnp.concatenate(reals + imags, axis=0)
        used = flag_ref[pl.ds(k, 1), :].astype(F32)
        res = used * (seen_ref[k] - model)
        res_ref[k] = res
        back = -used * res

        t_re, t_im = [], []
        for pol in range(4):
            d_re = back[pol : pol + 1]
            d_im = back[4 + pol : 5 + pol]
            t_re.append(ev_re * d_re + ev_im * d_im)
            t_im.append(ev_re * d_im - ev_im * d_re)
        t_hi, t_lo = split(jnp.concatenate(t_re + t_im, axis=0))
        held_ref[k, 0] = t_hi
        held_ref[k, 1] = t_lo
        return carry

    def two(k, carry):
        row_wave = row_wave_ref[k]
        t_hi = held_ref[k, 0]
        t_lo = held_ref[k, 1]
        both = dot(row_wave, t_hi, (1, 1))
        dz_ref[k] = both[: 2 * SIDE] + both[2 * SIDE :] + dot(row_wave[: 2 * SIDE], t_lo, (1, 1))
        return carry

    for k in range(SUBS):
        one(k, 0)
    for k in range(SUBS):
        two(k, 0)

    for k in range(SUBS):
        d = dz_ref[k]
        i_re, i_im, p_re, p_im, y_re, y_im = (side_ref[k, i] for i in range(6))
        dz_re = d[:SIDE, :LANES] + d[SIDE:, LANES:]
        dz_im = d[:SIDE, LANES:] - d[SIDE:, :LANES]

        dp_re = dz_re * y_re + dz_im * y_im
        dp_im = dz_im * y_re - dz_re * y_im
        dp_re = dp_re + turn(dp_re, 3)
        dp_im = dp_im + turn(dp_im, 3)
        i_re = i_re * taper
        i_im = i_im * taper
        dy_re = dz_re * p_re + dz_im * p_im
        dy_im = dz_im * p_re - dz_re * p_im
        dq_re = dy_re * i_re + dy_im * i_im
        dq_im = dy_re * i_im - dy_im * i_re
        dq_re = dq_re + turn(dq_re, 2)
        dq_im = dq_im + turn(dq_im, 2)
        for half, (dp, dq) in enumerate(((dp_re, dq_re), (dp_im, dq_im))):
            grad = jnp.where(lane == 0, dp, jnp.where(lane == 1, turn(dp, 3), dq))
            grad_ref[pl.ds(k + SUBS * half, SIDE, stride=2 * SUBS), :] = grad


SMEM = pl.BlockSpec(memory_space=pltpu.SMEM)
VMEM = pl.BlockSpec(memory_space=pltpu.VMEM)
HBM = pl.BlockSpec(memory_space=pltpu.HBM)
PARAMS = pltpu.CompilerParams(vmem_limit_bytes=40 * 1024 * 1024)


def call(kernel, shapes, specs, out_specs, scratch=()):
    return pl.pallas_call(
        kernel,
        out_shape=shapes,
        in_specs=specs,
        out_specs=out_specs,
        scratch_shapes=list(scratch),
        compiler_params=PARAMS,
    )


def shape(dims, dtype=F32):
    return jax.ShapeDtypeStruct(dims, dtype)


def cut(place, wanted, grid):
    return pl.pallas_call(
        cut_kernel,
        out_shape=shape((PEERS, ENDS, LANES), BF16),
        grid_spec=pltpu.PrefetchScalarGridSpec(
            num_scalar_prefetch=2,
            grid=(1,),
            in_specs=[pl.BlockSpec((1, grid.shape[1], LANES), lambda i, place, wanted: (place[1], 0, 0))],
            out_specs=pl.BlockSpec((PEERS, ENDS, LANES), lambda i, place, wanted: (0, 0, 0)),
            scratch_shapes=[pltpu.VMEM((grid.shape[1], LANES), F32)],
        ),
        compiler_params=PARAMS,
    )(place, wanted, grid)


def in_hbm(x):
    return pltpu.with_memory_space_constraint(x, pltpu.HBM)


def exchange(x, axes):
    return lax.all_to_all(x, axes, split_axis=0, concat_axis=0, tiled=True)


def main(slot, got, *rest):
    tables = [jnp.asarray(t) for t in dft_tables()]
    return call(
        main_kernel,
        (shape((SUBS, 8, VIS)), shape((TABLE, LANES))),
        [SMEM, VMEM] + [HBM] * 4 + [VMEM] * 3,
        (VMEM, VMEM),
        [
            pltpu.VMEM((TABLE, LANES), F32),
            pltpu.VMEM((SUBS, 4 * SIDE, VIS), BF16),
            pltpu.VMEM((SUBS, 2 * SIDE, VIS), F32),
            pltpu.VMEM((SUBS, 8, VIS), F32),
            pltpu.VMEM((SUBS, VIS), S32),
            pltpu.VMEM((SUBS, 6, SIDE, LANES), F32),
            pltpu.VMEM((SUBS, 6 * SIDE, 2 * LANES), BF16),
            pltpu.VMEM((SUBS, 2 * SIDE, 2 * LANES), F32),
            pltpu.VMEM((SUBS, 2, 2 * LANES, VIS), BF16),
            pltpu.SemaphoreType.DMA((4,)),
        ],
    )(slot, got, *(in_hbm(x) for x in rest), *tables)


ACROSS = ("z", "tile")
NEAR = ("x", "core")


def body(grid, a_terms, stations, intervals, offsets, uv, observed, flags):
    place = jnp.stack([lax.axis_index(name).astype(S32) for name in ("tile", "z")])
    offsets = offsets.T
    sent = call(
        prep_kernel,
        shape((PEERS, 2, LANES)),
        [HBM] * 4,
        VMEM,
        [
            pltpu.SMEM((2, SUBS), S32),
            pltpu.SMEM((SUBS,), S32),
            pltpu.SMEM((2, SUBS), S32),
            pltpu.VMEM((2, 4, SIDE * SIDE), F32),
            pltpu.SemaphoreType.DMA((4,)),
        ],
    )(*(in_hbm(x) for x in (stations.T, intervals, offsets, a_terms)))
    got_a = exchange(sent, ACROSS)
    spread = call(spread_kernel, shape((GROUPS, ROWS, LANES)), [VMEM], VMEM)(got_a)
    table = exchange(spread, NEAR).reshape(TABLE, LANES)

    wanted = got_a[:, 1, :].astype(S32)
    first = wanted[:, :SUBS].reshape(TABLE)
    second = wanted[:, SUBS:ENDS].reshape(TABLE)
    columns = (first[:, None], second[:, None])
    patches = cut(place, wanted[:, ENDS : ENDS + SLOTS], grid)
    waves = call(
        wave_kernel, (shape((SUBS, 4 * SIDE, VIS), BF16), shape((SUBS, 2 * SIDE, VIS))), [VMEM], (VMEM, VMEM)
    )(uv)

    found = call(gather_kernel, shape((PEERS, 2 * ENDS, LANES), BF16), [VMEM] * 4, VMEM)(table, *columns, patches)
    got_c = exchange(found, ACROSS)

    owner = offsets[0] >> 8
    same = owner[:, None] == owner[None, :]
    earlier = jnp.arange(SUBS)[:, None] > jnp.arange(SUBS)[None, :]
    slot = owner * 2 + jnp.sum((same & earlier).astype(S32), axis=1)
    result, grads = main(slot, got_c, *waves, observed, flags)

    back_c = exchange(grads.reshape(PEERS, SUBS, LANES), ACROSS).reshape(TABLE, LANES)
    dense = call(scatter_kernel, shape((TABLE, LANES)), [VMEM] * 5, VMEM)(
        back_c, *columns, first[None, :], second[None, :]
    )
    back_b = exchange(dense.reshape(GROUPS, ROWS, LANES), NEAR)
    summed = call(add_kernel, shape((PEERS, SUBS, LANES)), [VMEM], VMEM)(back_b)
    back_a = exchange(summed, ACROSS)
    total = call(place_kernel, shape((SUBS, 2, 4, SIDE * SIDE)), [VMEM], VMEM)(back_a)
    return (result, total)


def solution(mesh):
    fine = Mesh(mesh.devices.reshape(8, 4, 2, 8), ("z", "x", "core", "tile"))
    st = ("z", "x", "core")
    every = ("z", "x", "core", "tile")
    placed = (
        P(None, "tile", None),
        P(st, None, None, None),
        P(every, None),
        P(every),
        P(every, None),
        P(every, None, None),
        P(every, None, None),
        P(every, None),
    )
    return jax.shard_map(
        body,
        mesh=fine,
        in_specs=placed,
        out_specs=(P(every, None, None), P(st, None, None, None)),
        check_vma=False,
    )
```

```python
import jax
import jax.numpy as jnp
import numpy as np
from jax import lax
from jax.experimental import pallas as pl
from jax.experimental.pallas import tpu as pltpu
from jax.sharding import Mesh
from jax.sharding import PartitionSpec as P

SIDE = 32
SUBS = 8
ENDS = 2 * SUBS
VIS = 512
PEERS = 64
GROUPS = 8
ROWS = 64
TABLE = GROUPS * ROWS
LANES = 128
SLOTS = 16

F32 = jnp.float32
BF16 = jnp.bfloat16
S32 = jnp.int32


def bf16_parts(array, count):
    rest = np.asarray(array, np.float64)
    parts = []
    for _ in range(count):
        part = rest.astype(np.float32).astype(jnp.bfloat16)
        parts.append(part)
        rest = rest - part.astype(np.float64)
    return parts


def dft_tables():
    index = np.arange(SIDE)
    angle = 2.0 * np.pi * (index[:, None] * index[None, :] % SIDE) / SIDE
    f_real = np.cos(angle) / SIDE
    f_imag = np.sin(angle) / SIDE
    rows = np.concatenate([f_real, f_imag], axis=0)
    rows_parts = np.concatenate(bf16_parts(rows, 3), axis=1)
    eye = np.eye(4)
    cols = np.concatenate([np.kron(eye, f_real.T), np.kron(eye, f_imag.T)], axis=1)
    hi, lo = bf16_parts(cols, 2)
    cols_parts = np.concatenate([hi, hi, lo], axis=0)
    edge = np.cos(np.pi * (index - (SIDE - 1) / 2.0) / SIDE)
    taper = np.tile(edge[:, None] * edge[None, :], (1, 4)).astype(np.float32)
    return rows_parts, cols_parts, taper


def turn_polynomials():
    nodes = 0.25 * np.cos(np.pi * (np.arange(400) + 0.5) / 400) ** 2
    r = np.sqrt(nodes)
    scaled = nodes * 4.0
    sine = np.polynomial.polynomial.polyfit(scaled, np.sin(2 * np.pi * r) / r, 7)
    cosine = np.polynomial.polynomial.polyfit(scaled, np.cos(2 * np.pi * r), 8)
    power = 4.0 ** np.arange(9)
    return [float(a) for a in sine * power[:8]], [float(a) for a in cosine * power]


SINE, COSINE = turn_polynomials()


def unit_circle(turns):
    r = turns - jnp.floor(turns + 0.5)
    r2 = r * r
    s = jnp.full_like(r, SINE[-1])
    for a in SINE[-2::-1]:
        s = s * r2 + a
    c = jnp.full_like(r, COSINE[-1])
    for a in COSINE[-2::-1]:
        c = c * r2 + a
    return c, s * r


def split(x):
    hi = x.astype(BF16)
    return hi, (x - hi.astype(F32)).astype(BF16)


def dot(a, b, contract):
    return lax.dot_general(a, b, ((contract[:1], contract[1:]), ((), ())), preferred_element_type=F32)


def slots(offsets_ref):
    tiles = [offsets_ref[0, k] >> 8 for k in range(SUBS)]
    seconds = []
    for k in range(SUBS):
        second = jnp.zeros((), S32)
        for j in range(k):
            second = jnp.where(tiles[j] == tiles[k], 1, second)
        seconds.append(second)
    return tiles, seconds


def prep_kernel(
    stations_in, intervals_in, offsets_in, terms_in, out_ref, stations_ref, intervals_ref, offsets_ref, terms_ref, sems
):
    own = lax.axis_index("tile")
    copies = [
        pltpu.make_async_copy(stations_in, stations_ref, sems.at[0]),
        pltpu.make_async_copy(intervals_in, intervals_ref, sems.at[1]),
        pltpu.make_async_copy(offsets_in, offsets_ref, sems.at[2]),
        pltpu.make_async_copy(terms_in.at[own], terms_ref, sems.at[3]),
    ]
    for copy in copies:
        copy.start()
    for copy in copies[:3]:
        copy.wait()
    spot = lax.broadcasted_iota(S32, (1, LANES), 1)
    asked = jnp.zeros((1, LANES), S32)
    tiles, seconds = slots(offsets_ref)
    for k in range(SUBS):
        for end in range(2):
            station = stations_ref[end, k]
            row = ((station >> 3) & 7) * ROWS + (station >> 6) * 8 + (station & 7)
            asked = jnp.where(spot == end * SUBS + k, row + TABLE * intervals_ref[k], asked)
        code = (offsets_ref[0, k] & 255) * LANES + offsets_ref[1, k]
        asked = jnp.where(spot == ENDS + 2 * tiles[k] + seconds[k], code, asked)
    out_ref[:, 1:2, :] = jnp.broadcast_to(asked.astype(F32).reshape(1, 1, LANES), (PEERS, 1, LANES))
    copies[3].wait()
    lane = spot // SIDE
    for block in range(8):
        turned = []
        for interval in range(2):
            comps = terms_ref[interval, :, block * LANES : (block + 1) * LANES]
            turned.append([comps if d == 0 else pltpu.roll(comps, d * SIDE, 1) for d in range(4)])
        for i in range(4):
            for half in range(2):
                total = jnp.zeros((1, LANES), F32)
                for place in range(4):
                    comp = 2 * half + (place & 1)
                    piece = turned[place >> 1][(place - i) % 4][comp : comp + 1, :]
                    total = piece if place == 0 else jnp.where(lane == place, piece, total)
                out_ref[(4 * block + i) * 2 + half, 0:1, :] = total


def wave_kernel(uv_ref, row_wave_ref, column_wave_ref):
    centre = (lax.broadcasted_iota(S32, (SIDE, VIS), 0).astype(F32) - SIDE / 2.0) * (1.0 / SIDE)

    def one(k, carry):
        real, imag = unit_circle(uv_ref[k, 0:1, :] * centre)
        hi, lo = split(jnp.concatenate([real, imag], axis=0))
        row_wave_ref[k] = jnp.concatenate([hi, lo], axis=0)
        real, imag = unit_circle(uv_ref[k, 1:2, :] * centre)
        column_wave_ref[k] = jnp.concatenate([real, imag], axis=0)
        return carry

    lax.fori_loop(0, SUBS, one, 0)


def cut_kernel(place_ref, wanted_ref, strip_ref, out_ref, wide_ref):
    wide_ref[...] = strip_ref[0].astype(F32)
    tile = place_ref[0]
    part_of = place_ref[1]
    half = SIDE // 2
    lane = lax.broadcasted_iota(S32, (half, LANES), 1) // SIDE

    def one(i, carry):
        total = jnp.zeros((half, LANES), F32)
        for slot in range(2):
            code = wanted_ref[i, 2 * tile + slot]
            row = code >> 7
            column = code & (LANES - 1)
            for part in range(2):
                spot = (part_of + 2 * slot + part) & 3
                piece = wide_ref[pl.ds(row + half * part, half), :]
                piece = pltpu.roll(piece, (spot * SIDE + LANES - column) & (LANES - 1), 1)
                total = jnp.where(lane == spot, piece, total)
        out_ref[i] = total.astype(BF16)
        return carry

    lax.fori_loop(0, PEERS, one, 0, unroll=8)


def spread_kernel(got_ref, out_ref):
    part = got_ref[:, 0:1, :].reshape(ROWS, LANES)
    for i in range(GROUPS):
        out_ref[i] = part


def gather_kernel(table_ref, first_ref, second_ref, patch_ref, out_ref):
    hi, lo = split(table_ref[...])
    table = jnp.concatenate([hi, lo], axis=1)
    ids = lax.broadcasted_iota(S32, (TABLE, TABLE), 1)
    left = lax.broadcasted_iota(S32, (TABLE, LANES), 1) < LANES // 2
    sides = []
    for code_ref in (first_ref, second_ref):
        code = code_ref[...]
        chosen = jnp.where(ids == (code & (TABLE - 1)), 1.0, 0.0).astype(BF16)
        found = dot(chosen, table, (1, 0))
        found = found[:, :LANES] + found[:, LANES:]
        sides.append((found, pltpu.roll(found, LANES // 2, 1), code >= TABLE))
    first = jnp.where(sides[0][2], sides[0][1], sides[0][0])
    second = jnp.where(sides[1][2], sides[1][0], sides[1][1])
    beams = jnp.where(left, first, second)
    hi = beams.astype(BF16).astype(F32)
    both = jnp.concatenate([hi.reshape(PEERS, SUBS, LANES), (beams - hi).reshape(PEERS, SUBS, LANES)], axis=1)
    out_ref[:, 0:ENDS, :] = both.astype(BF16)
    out_ref[:, ENDS : 2 * ENDS, :] = patch_ref[...]


def scatter_kernel(got_ref, first_ref, second_ref, first_row_ref, second_row_ref, out_ref):
    got = got_ref[...]
    turned = pltpu.roll(got, LANES // 2, 1)
    left = lax.broadcasted_iota(S32, (TABLE, LANES), 1) < LANES // 2
    ids = lax.broadcasted_iota(S32, (TABLE, TABLE), 0)
    values, chosen = [], []
    for spread, code_ref, row_ref in (
        (jnp.where(left, got, turned), first_ref, first_row_ref),
        (jnp.where(left, turned, got), second_ref, second_row_ref),
    ):
        late = code_ref[...] >= TABLE
        values.append(jnp.where(late != left, spread, 0.0))
        chosen.append(jnp.where(ids == (row_ref[...] & (TABLE - 1)), 1.0, 0.0).astype(BF16))
    hi, lo = split(jnp.concatenate(values, axis=0))
    total = dot(jnp.concatenate(chosen, axis=1), jnp.concatenate([hi, lo], axis=1), (1, 0))
    out_ref[...] = total[:, :LANES] + total[:, LANES:]


def add_kernel(parts_ref, out_ref):
    total = parts_ref[0]
    for i in range(1, GROUPS):
        total = total + parts_ref[i]
    for i in range(PEERS):
        part = i // 8
        out_ref[i] = total[part * SUBS : (part + 1) * SUBS, :]


def place_kernel(parts_ref, out_hbm, out_ref, sems):
    copies = []
    lane = lax.broadcasted_iota(S32, (SUBS, LANES), 1) // SIDE
    for block in range(8):
        for half in range(2):
            rows = [parts_ref[2 * (4 * block + i) + half] for i in range(4)]
            turned = [[rows[i] if d == 0 else pltpu.roll(rows[i], d * SIDE, 1) for d in range(4)] for i in range(4)]
            for interval in range(2):
                for part in range(2):
                    at = 2 * interval + part
                    total = turned[0][(0 - at) % 4]
                    for i in range(1, 4):
                        total = jnp.where(lane == i, turned[i][(i - at) % 4], total)
                    out_ref[:, interval, 2 * half + part, block * LANES : (block + 1) * LANES] = total
        lanes = pl.ds(block * LANES, LANES)
        copies.append(
            pltpu.make_async_copy(out_ref.at[:, :, :, lanes], out_hbm.at[:, :, :, lanes], sems.at[block])
        )
        copies[-1].start()
    for copy in copies:
        copy.wait()


def main_kernel(
    slot_ref, got_ref, row_wave_ref, column_wave_ref, seen_in, flag_in, rows_ref, cols_ref, taper_ref,
    res_ref, grad_ref, beam_ref, seen_ref, flag_ref, side_ref, z_ref, dz_ref, held_ref, sems,
):
    copies = [
        pltpu.make_async_copy(a, b, sems.at[i])
        for i, (a, b) in enumerate(
            ((seen_in, seen_ref), (flag_in, flag_ref))
        )
    ]
    for copy in copies:
        copy.start()
    got = got_ref[:, 0:ENDS, :].astype(F32)
    beam_ref[...] = (got[:, :SUBS] + got[:, SUBS:]).reshape(TABLE, LANES)
    narrow = lax.broadcasted_iota(S32, (SIDE // 2, LANES), 1) // SIDE
    lane = lax.broadcasted_iota(S32, (SIDE, LANES), 1) // SIDE
    taper = taper_ref[...]

    def turn(x, blocks):
        return pltpu.roll(x, blocks * SIDE, 1)

    patches = []
    for k in range(SUBS):
        slot = slot_ref[k]
        tile = slot >> 1
        second = (slot & 1) > 0
        shift = 2 * (slot & 1)
        upper = (narrow - shift) & 3
        lower = (narrow - shift - 1) & 3
        for part in range(2):
            top = jnp.zeros((SIDE // 2, LANES), F32)
            low = top
            for i in range(4):
                piece = got_ref[8 * (4 * part + i) + tile, ENDS : 2 * ENDS, :].astype(F32)
                top = jnp.where(upper == i, piece, top)
                low = jnp.where(lower == i, piece, low)
            top = jnp.where(second, turn(top, 2), top)
            low = jnp.where(second, turn(low, 1), turn(low, 3))
            patches.append(jnp.concatenate([top, low], axis=0).astype(BF16))
    patch = jnp.concatenate(patches, axis=1)
    a = dot(rows_ref[...], jnp.concatenate([patch, patch, patch], axis=0), (1, 0))
    mixed = []
    for k in range(SUBS):
        re = a[:, 2 * k * LANES : (2 * k + 1) * LANES]
        im = a[:, (2 * k + 1) * LANES : (2 * k + 2) * LANES]
        mixed += [re[:SIDE] - im[SIDE:], im[:SIDE] + re[SIDE:]]
    hi, lo = split(jnp.concatenate(mixed, axis=0))
    images = dot(jnp.concatenate([hi, lo, hi], axis=1), cols_ref[...], (1, 0))

    for k in range(SUBS):
        b = images[2 * k * SIDE : 2 * (k + 1) * SIDE]
        i_re = b[:SIDE, :LANES] - b[SIDE:, LANES:]
        i_im = b[:SIDE, LANES:] + b[SIDE:, :LANES]

        sides = []
        for half in range(2):
            g = beam_ref[pl.ds(k + SUBS * half, SIDE, stride=2 * SUBS), :]
            g1, g2 = turn(g, 1), turn(g, 2)
            sides.append((jnp.where(lane == 0, g, jnp.where(lane == 3, g2, g1)), jnp.where(lane < 2, g2, g)))
        (p_re, q_re), (p_im, q_im) = sides

        y_re = i_re * q_re + i_im * q_im
        y_im = i_im * q_re - i_re * q_im
        z_re = (p_re * y_re - p_im * y_im) * taper
        z_im = (p_re * y_im + p_im * y_re) * taper
        for i, part in enumerate((i_re, i_im, p_re, p_im, y_re, y_im)):
            side_ref[k, i] = part * taper if i > 3 else part
        z = jnp.concatenate(
            [jnp.concatenate([z_re, z_im], axis=1), jnp.concatenate([-z_im, z_re], axis=1)], axis=0
        )
        z_hi, z_lo = split(z)
        z_ref[k] = jnp.concatenate([z_hi, z_lo, z_hi], axis=0)

    for copy in copies:
        copy.wait()

    def one(k, carry):
        row_wave = row_wave_ref[k]
        ev_re = column_wave_ref[k, :SIDE, :]
        ev_im = column_wave_ref[k, SIDE:, :]
        w = dot(z_ref[k], jnp.concatenate([row_wave[: 2 * SIDE], row_wave], axis=0), (0, 0))
        reals, imags = [], []
        for pol in range(4):
            w_re = w[pol * SIDE : (pol + 1) * SIDE]
            w_im = w[LANES + pol * SIDE : LANES + (pol + 1) * SIDE]
            reals.append(jnp.sum(w_re * ev_re - w_im * ev_im, axis=0, keepdims=True))
            imags.append(jnp.sum(w_re * ev_im + w_im * ev_re, axis=0, keepdims=True))
        model = jnp.concatenate(reals + imags, axis=0)
        used = flag_ref[pl.ds(k, 1), :].astype(F32)
        res = used * (seen_ref[k] - model)
        res_ref[k] = res
        back = -used * res

        t_re, t_im = [], []
        for pol in range(4):
            d_re = back[pol : pol + 1]
            d_im = back[4 + pol : 5 + pol]
            t_re.append(ev_re * d_re + ev_im * d_im)
            t_im.append(ev_re * d_im - ev_im * d_re)
        t_hi, t_lo = split(jnp.concatenate(t_re + t_im, axis=0))
        held_ref[k, 0] = t_hi
        held_ref[k, 1] = t_lo
        return carry

    def two(k, carry):
        row_wave = row_wave_ref[k]
        t_hi = held_ref[k, 0]
        t_lo = held_ref[k, 1]
        both = dot(row_wave, t_hi, (1, 1))
        dz_ref[k] = both[: 2 * SIDE] + both[2 * SIDE :] + dot(row_wave[: 2 * SIDE], t_lo, (1, 1))
        return carry

    for k in range(SUBS):
        one(k, 0)
    for k in range(SUBS):
        two(k, 0)

    for k in range(SUBS):
        d = dz_ref[k]
        i_re, i_im, p_re, p_im, y_re, y_im = (side_ref[k, i] for i in range(6))
        dz_re = d[:SIDE, :LANES] + d[SIDE:, LANES:]
        dz_im = d[:SIDE, LANES:] - d[SIDE:, :LANES]

        dp_re = dz_re * y_re + dz_im * y_im
        dp_im = dz_im * y_re - dz_re * y_im
        dp_re = dp_re + turn(dp_re, 3)
        dp_im = dp_im + turn(dp_im, 3)
        i_re = i_re * taper
        i_im = i_im * taper
        dy_re = dz_re * p_re + dz_im * p_im
        dy_im = dz_im * p_re - dz_re * p_im
        dq_re = dy_re * i_re + dy_im * i_im
        dq_im = dy_re * i_im - dy_im * i_re
        dq_re = dq_re + turn(dq_re, 2)
        dq_im = dq_im + turn(dq_im, 2)
        for half, (dp, dq) in enumerate(((dp_re, dq_re), (dp_im, dq_im))):
            grad = jnp.where(lane == 0, dp, jnp.where(lane == 1, turn(dp, 3), dq))
            grad_ref[pl.ds(k + SUBS * half, SIDE, stride=2 * SUBS), :] = grad


SMEM = pl.BlockSpec(memory_space=pltpu.SMEM)
VMEM = pl.BlockSpec(memory_space=pltpu.VMEM)
HBM = pl.BlockSpec(memory_space=pltpu.HBM)
PARAMS = pltpu.CompilerParams(vmem_limit_bytes=40 * 1024 * 1024)


def call(kernel, shapes, specs, out_specs, scratch=()):
    return pl.pallas_call(
        kernel,
        out_shape=shapes,
        in_specs=specs,
        out_specs=out_specs,
        scratch_shapes=list(scratch),
        compiler_params=PARAMS,
    )


def shape(dims, dtype=F32):
    return jax.ShapeDtypeStruct(dims, dtype)


def cut(place, wanted, grid):
    return pl.pallas_call(
        cut_kernel,
        out_shape=shape((PEERS, ENDS, LANES), BF16),
        grid_spec=pltpu.PrefetchScalarGridSpec(
            num_scalar_prefetch=2,
            grid=(1,),
            in_specs=[pl.BlockSpec((1, grid.shape[1], LANES), lambda i, place, wanted: (place[1], 0, 0))],
            out_specs=pl.BlockSpec((PEERS, ENDS, LANES), lambda i, place, wanted: (0, 0, 0)),
            scratch_shapes=[pltpu.VMEM((grid.shape[1], LANES), F32)],
        ),
        compiler_params=PARAMS,
    )(place, wanted, grid)


def in_hbm(x):
    return pltpu.with_memory_space_constraint(x, pltpu.HBM)


def exchange(x, axes):
    return lax.all_to_all(x, axes, split_axis=0, concat_axis=0, tiled=True)


def main(slot, got, row_waves, column_waves, *rest):
    waves = [pltpu.with_memory_space_constraint(x, pltpu.VMEM) for x in (row_waves, column_waves)]
    tables = [jnp.asarray(t) for t in dft_tables()]
    return call(
        main_kernel,
        (shape((SUBS, 8, VIS)), shape((TABLE, LANES))),
        [SMEM] + [VMEM] * 3 + [HBM] * 2 + [VMEM] * 3,
        (VMEM, VMEM),
        [
            pltpu.VMEM((TABLE, LANES), F32),
            pltpu.VMEM((SUBS, 8, VIS), F32),
            pltpu.VMEM((SUBS, VIS), S32),
            pltpu.VMEM((SUBS, 6, SIDE, LANES), F32),
            pltpu.VMEM((SUBS, 6 * SIDE, 2 * LANES), BF16),
            pltpu.VMEM((SUBS, 2 * SIDE, 2 * LANES), F32),
            pltpu.VMEM((SUBS, 2, 2 * LANES, VIS), BF16),
            pltpu.SemaphoreType.DMA((4,)),
        ],
    )(slot, got, *waves, *(in_hbm(x) for x in rest), *tables)


ACROSS = ("z", "tile")
NEAR = ("x", "core")


def body(grid, a_terms, stations, intervals, offsets, uv, observed, flags):
    place = jnp.stack([lax.axis_index(name).astype(S32) for name in ("tile", "z")])
    offsets = offsets.T
    sent = call(
        prep_kernel,
        shape((PEERS, 2, LANES)),
        [HBM] * 4,
        VMEM,
        [
            pltpu.SMEM((2, SUBS), S32),
            pltpu.SMEM((SUBS,), S32),
            pltpu.SMEM((2, SUBS), S32),
            pltpu.VMEM((2, 4, SIDE * SIDE), F32),
            pltpu.SemaphoreType.DMA((4,)),
        ],
    )(*(in_hbm(x) for x in (stations.T, intervals, offsets, a_terms)))
    got_a = exchange(sent, ACROSS)
    spread = call(spread_kernel, shape((GROUPS, ROWS, LANES)), [VMEM], VMEM)(got_a)
    table = exchange(spread, NEAR).reshape(TABLE, LANES)

    wanted = got_a[:, 1, :].astype(S32)
    first = wanted[:, :SUBS].reshape(TABLE)
    second = wanted[:, SUBS:ENDS].reshape(TABLE)
    columns = (first[:, None], second[:, None])
    patches = cut(place, wanted[:, ENDS : ENDS + SLOTS], grid)
    waves = call(
        wave_kernel, (shape((SUBS, 4 * SIDE, VIS), BF16), shape((SUBS, 2 * SIDE, VIS))), [VMEM], (VMEM, VMEM)
    )(uv)

    found = call(gather_kernel, shape((PEERS, 2 * ENDS, LANES), BF16), [VMEM] * 4, VMEM)(table, *columns, patches)
    got_c = exchange(found, ACROSS)

    owner = offsets[0] >> 8
    same = owner[:, None] == owner[None, :]
    earlier = jnp.arange(SUBS)[:, None] > jnp.arange(SUBS)[None, :]
    slot = owner * 2 + jnp.sum((same & earlier).astype(S32), axis=1)
    result, grads = main(slot, got_c, *waves, observed, flags)

    back_c = exchange(grads.reshape(PEERS, SUBS, LANES), ACROSS).reshape(TABLE, LANES)
    dense = call(scatter_kernel, shape((TABLE, LANES)), [VMEM] * 5, VMEM)(
        back_c, *columns, first[None, :], second[None, :]
    )
    back_b = exchange(dense.reshape(GROUPS, ROWS, LANES), NEAR)
    summed = call(add_kernel, shape((PEERS, SUBS, LANES)), [VMEM], VMEM)(back_b)
    back_a = exchange(summed, ACROSS)
    total = call(
        place_kernel,
        shape((SUBS, 2, 4, SIDE * SIDE)),
        [VMEM],
        HBM,
        [pltpu.VMEM((SUBS, 2, 4, SIDE * SIDE), F32), pltpu.SemaphoreType.DMA((8,))],
    )(back_a)
    return (result, total)


def solution(mesh):
    fine = Mesh(mesh.devices.reshape(8, 4, 2, 8), ("z", "x", "core", "tile"))
    st = ("z", "x", "core")
    every = ("z", "x", "core", "tile")
    placed = (
        P(None, "tile", None),
        P(st, None, None, None),
        P(every, None),
        P(every),
        P(every, None),
        P(every, None, None),
        P(every, None, None),
        P(every, None),
    )
    return jax.shard_map(
        body,
        mesh=fine,
        in_specs=placed,
        out_specs=(P(every, None, None), P(st, None, None, None)),
        check_vma=False,
    )
```

```python
import jax
import jax.numpy as jnp
import numpy as np
from jax import lax
from jax.experimental import pallas as pl
from jax.experimental.pallas import tpu as pltpu
from jax.sharding import Mesh
from jax.sharding import PartitionSpec as P

SIDE = 32
SUBS = 8
ENDS = 2 * SUBS
VIS = 512
PEERS = 64
GROUPS = 8
ROWS = 64
TABLE = GROUPS * ROWS
LANES = 128
SLOTS = 16

F32 = jnp.float32
BF16 = jnp.bfloat16
S32 = jnp.int32


def bf16_parts(array, count):
    rest = np.asarray(array, np.float64)
    parts = []
    for _ in range(count):
        part = rest.astype(np.float32).astype(jnp.bfloat16)
        parts.append(part)
        rest = rest - part.astype(np.float64)
    return parts


def dft_tables():
    index = np.arange(SIDE)
    angle = 2.0 * np.pi * (index[:, None] * index[None, :] % SIDE) / SIDE
    f_real = np.cos(angle) / SIDE
    f_imag = np.sin(angle) / SIDE
    rows = np.concatenate([f_real, f_imag], axis=0)
    rows_parts = np.concatenate(bf16_parts(rows, 3), axis=1)
    eye = np.eye(4)
    cols = np.concatenate([np.kron(eye, f_real.T), np.kron(eye, f_imag.T)], axis=1)
    hi, lo = bf16_parts(cols, 2)
    cols_parts = np.concatenate([hi, hi, lo], axis=0)
    edge = np.cos(np.pi * (index - (SIDE - 1) / 2.0) / SIDE)
    taper = np.tile(edge[:, None] * edge[None, :], (1, 4)).astype(np.float32)
    return rows_parts, cols_parts, taper


def turn_polynomials():
    nodes = 0.25 * np.cos(np.pi * (np.arange(400) + 0.5) / 400) ** 2
    r = np.sqrt(nodes)
    scaled = nodes * 4.0
    sine = np.polynomial.polynomial.polyfit(scaled, np.sin(2 * np.pi * r) / r, 7)
    cosine = np.polynomial.polynomial.polyfit(scaled, np.cos(2 * np.pi * r), 8)
    power = 4.0 ** np.arange(9)
    return [float(a) for a in sine * power[:8]], [float(a) for a in cosine * power]


SINE, COSINE = turn_polynomials()


def unit_circle(turns):
    r = turns - jnp.floor(turns + 0.5)
    r2 = r * r
    s = jnp.full_like(r, SINE[-1])
    for a in SINE[-2::-1]:
        s = s * r2 + a
    c = jnp.full_like(r, COSINE[-1])
    for a in COSINE[-2::-1]:
        c = c * r2 + a
    return c, s * r


def split(x):
    hi = x.astype(BF16)
    return hi, (x - hi.astype(F32)).astype(BF16)


def dot(a, b, contract):
    return lax.dot_general(a, b, ((contract[:1], contract[1:]), ((), ())), preferred_element_type=F32)


def slots(offsets_ref):
    tiles = [offsets_ref[0, k] >> 8 for k in range(SUBS)]
    seconds = []
    for k in range(SUBS):
        second = jnp.zeros((), S32)
        for j in range(k):
            second = jnp.where(tiles[j] == tiles[k], 1, second)
        seconds.append(second)
    return tiles, seconds


def prep_kernel(
    stations_in, intervals_in, offsets_in, terms_in, out_ref, stations_ref, intervals_ref, offsets_ref, terms_ref, sems
):
    own = lax.axis_index("tile")
    copies = [
        pltpu.make_async_copy(stations_in, stations_ref, sems.at[0]),
        pltpu.make_async_copy(intervals_in, intervals_ref, sems.at[1]),
        pltpu.make_async_copy(offsets_in, offsets_ref, sems.at[2]),
        pltpu.make_async_copy(terms_in.at[own], terms_ref, sems.at[3]),
    ]
    for copy in copies:
        copy.start()
    for copy in copies:
        copy.wait()
    spot = lax.broadcasted_iota(S32, (1, LANES), 1)
    asked = jnp.zeros((1, LANES), S32)
    tiles, seconds = slots(offsets_ref)
    for k in range(SUBS):
        for end in range(2):
            station = stations_ref[end, k]
            row = ((station >> 3) & 7) * ROWS + (station >> 6) * 8 + (station & 7)
            asked = jnp.where(spot == end * SUBS + k, row + TABLE * intervals_ref[k], asked)
        code = (offsets_ref[0, k] & 255) * LANES + offsets_ref[1, k]
        asked = jnp.where(spot == ENDS + 2 * tiles[k] + seconds[k], code, asked)
    out_ref[:, 1:2, :] = jnp.broadcast_to(asked.astype(F32).reshape(1, 1, LANES), (PEERS, 1, LANES))
    lane = spot // SIDE
    for block in range(8):
        turned = []
        for interval in range(2):
            comps = terms_ref[interval, :, block * LANES : (block + 1) * LANES]
            turned.append([comps if d == 0 else pltpu.roll(comps, d * SIDE, 1) for d in range(4)])
        for i in range(4):
            for half in range(2):
                total = jnp.zeros((1, LANES), F32)
                for place in range(4):
                    comp = 2 * half + (place & 1)
                    piece = turned[place >> 1][(place - i) % 4][comp : comp + 1, :]
                    total = piece if place == 0 else jnp.where(lane == place, piece, total)
                out_ref[(4 * block + i) * 2 + half, 0:1, :] = total


def wave_kernel(uv_ref, row_wave_ref, column_wave_ref):
    centre = (lax.broadcasted_iota(S32, (SIDE, VIS), 0).astype(F32) - SIDE / 2.0) * (1.0 / SIDE)

    def one(k, carry):
        real, imag = unit_circle(uv_ref[k, 0:1, :] * centre)
        hi, lo = split(jnp.concatenate([real, imag], axis=0))
        row_wave_ref[k] = jnp.concatenate([hi, lo], axis=0)
        real, imag = unit_circle(uv_ref[k, 1:2, :] * centre)
        column_wave_ref[k] = jnp.concatenate([real, imag], axis=0)
        return carry

    lax.fori_loop(0, SUBS, one, 0)


def cut_kernel(place_ref, wanted_ref, strip_ref, out_hbm, wide_ref, out_ref, sem):
    wide_ref[...] = strip_ref[0].astype(F32)
    tile = place_ref[0]
    part_of = place_ref[1]
    half = SIDE // 2
    lane = lax.broadcasted_iota(S32, (half, LANES), 1) // SIDE

    def one(i, carry):
        total = jnp.zeros((half, LANES), F32)
        for slot in range(2):
            code = wanted_ref[i, 2 * tile + slot]
            row = code >> 7
            column = code & (LANES - 1)
            for part in range(2):
                spot = (part_of + 2 * slot + part) & 3
                piece = wide_ref[pl.ds(row + half * part, half), :]
                piece = pltpu.roll(piece, (spot * SIDE + LANES - column) & (LANES - 1), 1)
                total = jnp.where(lane == spot, piece, total)
        out_ref[i] = total.astype(BF16)
        return carry

    lax.fori_loop(0, PEERS, one, 0, unroll=8)
    copy = pltpu.make_async_copy(out_ref, out_hbm.at[:, pl.ds(ENDS, ENDS), :], sem)
    copy.start()
    copy.wait()


def spread_kernel(got_ref, out_hbm, part_ref, sems):
    part_ref[...] = got_ref[:, 0:1, :].reshape(ROWS, LANES)
    copies = [pltpu.make_async_copy(part_ref, out_hbm.at[i], sems.at[i]) for i in range(GROUPS)]
    for copy in copies:
        copy.start()
    for copy in copies:
        copy.wait()


def gather_kernel(table_ref, first_ref, second_ref, patched_hbm, out_hbm, out_ref, sem):
    hi, lo = split(table_ref[...])
    table = jnp.concatenate([hi, lo], axis=1)
    ids = lax.broadcasted_iota(S32, (TABLE, TABLE), 1)
    left = lax.broadcasted_iota(S32, (TABLE, LANES), 1) < LANES // 2
    sides = []
    for code_ref in (first_ref, second_ref):
        code = code_ref[...]
        chosen = jnp.where(ids == (code & (TABLE - 1)), 1.0, 0.0).astype(BF16)
        found = dot(chosen, table, (1, 0))
        found = found[:, :LANES] + found[:, LANES:]
        sides.append((found, pltpu.roll(found, LANES // 2, 1), code >= TABLE))
    first = jnp.where(sides[0][2], sides[0][1], sides[0][0])
    second = jnp.where(sides[1][2], sides[1][0], sides[1][1])
    beams = jnp.where(left, first, second)
    hi = beams.astype(BF16).astype(F32)
    both = jnp.concatenate([hi.reshape(PEERS, SUBS, LANES), (beams - hi).reshape(PEERS, SUBS, LANES)], axis=1)
    out_ref[...] = both.astype(BF16)
    copy = pltpu.make_async_copy(out_ref, out_hbm.at[:, pl.ds(0, ENDS), :], sem)
    copy.start()
    copy.wait()


def scatter_kernel(got_ref, first_ref, second_ref, first_row_ref, second_row_ref, out_ref):
    got = got_ref[...]
    turned = pltpu.roll(got, LANES // 2, 1)
    left = lax.broadcasted_iota(S32, (TABLE, LANES), 1) < LANES // 2
    ids = lax.broadcasted_iota(S32, (TABLE, TABLE), 0)
    values, chosen = [], []
    for spread, code_ref, row_ref in (
        (jnp.where(left, got, turned), first_ref, first_row_ref),
        (jnp.where(left, turned, got), second_ref, second_row_ref),
    ):
        late = code_ref[...] >= TABLE
        values.append(jnp.where(late != left, spread, 0.0))
        chosen.append(jnp.where(ids == (row_ref[...] & (TABLE - 1)), 1.0, 0.0).astype(BF16))
    hi, lo = split(jnp.concatenate(values, axis=0))
    total = dot(jnp.concatenate(chosen, axis=1), jnp.concatenate([hi, lo], axis=1), (1, 0))
    out_ref[...] = total[:, :LANES] + total[:, LANES:]


def add_kernel(parts_ref, out_ref):
    total = parts_ref[0]
    for i in range(1, GROUPS):
        total = total + parts_ref[i]
    for i in range(PEERS):
        part = i // 8
        out_ref[i] = total[part * SUBS : (part + 1) * SUBS, :]


def place_kernel(parts_ref, out_hbm, out_ref, sems):
    copies = []
    lane = lax.broadcasted_iota(S32, (SUBS, LANES), 1) // SIDE
    for block in range(8):
        for half in range(2):
            rows = [parts_ref[2 * (4 * block + i) + half] for i in range(4)]
            turned = [[rows[i] if d == 0 else pltpu.roll(rows[i], d * SIDE, 1) for d in range(4)] for i in range(4)]
            for interval in range(2):
                for part in range(2):
                    at = 2 * interval + part
                    total = turned[0][(0 - at) % 4]
                    for i in range(1, 4):
                        total = jnp.where(lane == i, turned[i][(i - at) % 4], total)
                    out_ref[:, interval, 2 * half + part, block * LANES : (block + 1) * LANES] = total
        lanes = pl.ds(block * LANES, LANES)
        copies.append(
            pltpu.make_async_copy(out_ref.at[:, :, :, lanes], out_hbm.at[:, :, :, lanes], sems.at[block])
        )
        copies[-1].start()
    for copy in copies:
        copy.wait()


def main_kernel(
    slot_ref, got_ref, row_wave_ref, column_wave_ref, seen_in, flag_in, rows_ref, cols_ref, taper_ref,
    res_ref, grad_ref, beam_ref, seen_ref, flag_ref, side_ref, z_ref, dz_ref, held_ref, sems,
):
    copies = [
        pltpu.make_async_copy(a, b, sems.at[i])
        for i, (a, b) in enumerate(
            ((seen_in, seen_ref), (flag_in, flag_ref))
        )
    ]
    for copy in copies:
        copy.start()
    got = got_ref[:, 0:ENDS, :].astype(F32)
    beam_ref[...] = (got[:, :SUBS] + got[:, SUBS:]).reshape(TABLE, LANES)
    narrow = lax.broadcasted_iota(S32, (SIDE // 2, LANES), 1) // SIDE
    lane = lax.broadcasted_iota(S32, (SIDE, LANES), 1) // SIDE
    taper = taper_ref[...]

    def turn(x, blocks):
        return pltpu.roll(x, blocks * SIDE, 1)

    patches = []
    for k in range(SUBS):
        slot = slot_ref[k]
        tile = slot >> 1
        second = (slot & 1) > 0
        shift = 2 * (slot & 1)
        upper = (narrow - shift) & 3
        lower = (narrow - shift - 1) & 3
        for part in range(2):
            top = jnp.zeros((SIDE // 2, LANES), F32)
            low = top
            for i in range(4):
                piece = got_ref[8 * (4 * part + i) + tile, ENDS : 2 * ENDS, :].astype(F32)
                top = jnp.where(upper == i, piece, top)
                low = jnp.where(lower == i, piece, low)
            top = jnp.where(second, turn(top, 2), top)
            low = jnp.where(second, turn(low, 1), turn(low, 3))
            patches.append(jnp.concatenate([top, low], axis=0).astype(BF16))
    patch = jnp.concatenate(patches, axis=1)
    a = dot(rows_ref[...], jnp.concatenate([patch, patch, patch], axis=0), (1, 0))
    mixed = []
    for k in range(SUBS):
        re = a[:, 2 * k * LANES : (2 * k + 1) * LANES]
        im = a[:, (2 * k + 1) * LANES : (2 * k + 2) * LANES]
        mixed += [re[:SIDE] - im[SIDE:], im[:SIDE] + re[SIDE:]]
    hi, lo = split(jnp.concatenate(mixed, axis=0))
    images = dot(jnp.concatenate([hi, lo, hi], axis=1), cols_ref[...], (1, 0))

    for k in range(SUBS):
        b = images[2 * k * SIDE : 2 * (k + 1) * SIDE]
        i_re = b[:SIDE, :LANES] - b[SIDE:, LANES:]
        i_im = b[:SIDE, LANES:] + b[SIDE:, :LANES]

        sides = []
        for half in range(2):
            g = beam_ref[pl.ds(k + SUBS * half, SIDE, stride=2 * SUBS), :]
            g1, g2 = turn(g, 1), turn(g, 2)
            sides.append((jnp.where(lane == 0, g, jnp.where(lane == 3, g2, g1)), jnp.where(lane < 2, g2, g)))
        (p_re, q_re), (p_im, q_im) = sides

        y_re = i_re * q_re + i_im * q_im
        y_im = i_im * q_re - i_re * q_im
        z_re = (p_re * y_re - p_im * y_im) * taper
        z_im = (p_re * y_im + p_im * y_re) * taper
        for i, part in enumerate((i_re, i_im, p_re, p_im, y_re, y_im)):
            side_ref[k, i] = part * taper if i > 3 else part
        z = jnp.concatenate(
            [jnp.concatenate([z_re, z_im], axis=1), jnp.concatenate([-z_im, z_re], axis=1)], axis=0
        )
        z_hi, z_lo = split(z)
        z_ref[k] = jnp.concatenate([z_hi, z_lo, z_hi], axis=0)

    for copy in copies:
        copy.wait()

    def one(k, carry):
        row_wave = row_wave_ref[k]
        ev_re = column_wave_ref[k, :SIDE, :]
        ev_im = column_wave_ref[k, SIDE:, :]
        w = dot(z_ref[k], jnp.concatenate([row_wave[: 2 * SIDE], row_wave], axis=0), (0, 0))
        reals, imags = [], []
        for pol in range(4):
            w_re = w[pol * SIDE : (pol + 1) * SIDE]
            w_im = w[LANES + pol * SIDE : LANES + (pol + 1) * SIDE]
            reals.append(jnp.sum(w_re * ev_re - w_im * ev_im, axis=0, keepdims=True))
            imags.append(jnp.sum(w_re * ev_im + w_im * ev_re, axis=0, keepdims=True))
        model = jnp.concatenate(reals + imags, axis=0)
        used = flag_ref[pl.ds(k, 1), :].astype(F32)
        res = used * (seen_ref[k] - model)
        res_ref[k] = res
        back = -used * res

        t_re, t_im = [], []
        for pol in range(4):
            d_re = back[pol : pol + 1]
            d_im = back[4 + pol : 5 + pol]
            t_re.append(ev_re * d_re + ev_im * d_im)
            t_im.append(ev_re * d_im - ev_im * d_re)
        t_hi, t_lo = split(jnp.concatenate(t_re + t_im, axis=0))
        held_ref[k, 0] = t_hi
        held_ref[k, 1] = t_lo
        return carry

    def two(k, carry):
        row_wave = row_wave_ref[k]
        t_hi = held_ref[k, 0]
        t_lo = held_ref[k, 1]
        both = dot(row_wave, t_hi, (1, 1))
        dz_ref[k] = both[: 2 * SIDE] + both[2 * SIDE :] + dot(row_wave[: 2 * SIDE], t_lo, (1, 1))
        return carry

    for k in range(SUBS + 1):
        if k < SUBS:
            one(k, 0)
        if k > 0:
            two(k - 1, 0)

    for k in range(SUBS):
        d = dz_ref[k]
        i_re, i_im, p_re, p_im, y_re, y_im = (side_ref[k, i] for i in range(6))
        dz_re = d[:SIDE, :LANES] + d[SIDE:, LANES:]
        dz_im = d[:SIDE, LANES:] - d[SIDE:, :LANES]

        dp_re = dz_re * y_re + dz_im * y_im
        dp_im = dz_im * y_re - dz_re * y_im
        dp_re = dp_re + turn(dp_re, 3)
        dp_im = dp_im + turn(dp_im, 3)
        i_re = i_re * taper
        i_im = i_im * taper
        dy_re = dz_re * p_re + dz_im * p_im
        dy_im = dz_im * p_re - dz_re * p_im
        dq_re = dy_re * i_re + dy_im * i_im
        dq_im = dy_re * i_im - dy_im * i_re
        dq_re = dq_re + turn(dq_re, 2)
        dq_im = dq_im + turn(dq_im, 2)
        for half, (dp, dq) in enumerate(((dp_re, dq_re), (dp_im, dq_im))):
            grad = jnp.where(lane == 0, dp, jnp.where(lane == 1, turn(dp, 3), dq))
            grad_ref[pl.ds(k + SUBS * half, SIDE, stride=2 * SUBS), :] = grad


SMEM = pl.BlockSpec(memory_space=pltpu.SMEM)
VMEM = pl.BlockSpec(memory_space=pltpu.VMEM)
HBM = pl.BlockSpec(memory_space=pltpu.HBM)
PARAMS = pltpu.CompilerParams(vmem_limit_bytes=40 * 1024 * 1024)


def call(kernel, shapes, specs, out_specs, scratch=(), aliases=None):
    return pl.pallas_call(
        kernel,
        out_shape=shapes,
        in_specs=specs,
        out_specs=out_specs,
        scratch_shapes=list(scratch),
        input_output_aliases=aliases or {},
        compiler_params=PARAMS,
    )


def shape(dims, dtype=F32):
    return jax.ShapeDtypeStruct(dims, dtype)


def cut(place, wanted, grid):
    return pl.pallas_call(
        cut_kernel,
        out_shape=shape((PEERS, 2 * ENDS, LANES), BF16),
        grid_spec=pltpu.PrefetchScalarGridSpec(
            num_scalar_prefetch=2,
            grid=(1,),
            in_specs=[pl.BlockSpec((1, grid.shape[1], LANES), lambda i, place, wanted: (place[1], 0, 0))],
            out_specs=HBM,
            scratch_shapes=[
                pltpu.VMEM((grid.shape[1], LANES), F32),
                pltpu.VMEM((PEERS, ENDS, LANES), BF16),
                pltpu.SemaphoreType.DMA,
            ],
        ),
        compiler_params=PARAMS,
    )(place, wanted, grid)


def in_hbm(x):
    return pltpu.with_memory_space_constraint(x, pltpu.HBM)


def exchange(x, axes):
    return lax.all_to_all(x, axes, split_axis=0, concat_axis=0, tiled=True)


def main(slot, got, row_waves, column_waves, *rest):
    waves = [pltpu.with_memory_space_constraint(x, pltpu.VMEM) for x in (row_waves, column_waves)]
    tables = [jnp.asarray(t) for t in dft_tables()]
    return call(
        main_kernel,
        (shape((SUBS, 8, VIS)), shape((TABLE, LANES))),
        [SMEM] + [VMEM] * 3 + [HBM] * 2 + [VMEM] * 3,
        (VMEM, VMEM),
        [
            pltpu.VMEM((TABLE, LANES), F32),
            pltpu.VMEM((SUBS, 8, VIS), F32),
            pltpu.VMEM((SUBS, VIS), S32),
            pltpu.VMEM((SUBS, 6, SIDE, LANES), F32),
            pltpu.VMEM((SUBS, 6 * SIDE, 2 * LANES), BF16),
            pltpu.VMEM((SUBS, 2 * SIDE, 2 * LANES), F32),
            pltpu.VMEM((SUBS, 2, 2 * LANES, VIS), BF16),
            pltpu.SemaphoreType.DMA((4,)),
        ],
    )(slot, got, *waves, *(in_hbm(x) for x in rest), *tables)


ACROSS = ("z", "tile")
NEAR = ("x", "core")


def body(grid, a_terms, stations, intervals, offsets, uv, observed, flags):
    place = jnp.stack([lax.axis_index(name).astype(S32) for name in ("tile", "z")])
    offsets = offsets.T
    sent = call(
        prep_kernel,
        shape((PEERS, 2, LANES)),
        [HBM] * 4,
        VMEM,
        [
            pltpu.SMEM((2, SUBS), S32),
            pltpu.SMEM((SUBS,), S32),
            pltpu.SMEM((2, SUBS), S32),
            pltpu.VMEM((2, 4, SIDE * SIDE), F32),
            pltpu.SemaphoreType.DMA((4,)),
        ],
    )(*(in_hbm(x) for x in (stations.T, intervals, offsets, a_terms)))
    got_a = exchange(sent, ACROSS)
    spread = call(
        spread_kernel,
        shape((GROUPS, ROWS, LANES)),
        [VMEM],
        HBM,
        [pltpu.VMEM((ROWS, LANES), F32), pltpu.SemaphoreType.DMA((GROUPS,))],
    )(got_a)
    table = exchange(spread, NEAR).reshape(TABLE, LANES)

    wanted = got_a[:, 1, :].astype(S32)
    first = wanted[:, :SUBS].reshape(TABLE)
    second = wanted[:, SUBS:ENDS].reshape(TABLE)
    columns = (first[:, None], second[:, None])
    patches = cut(place, wanted[:, ENDS : ENDS + SLOTS], grid)
    waves = call(
        wave_kernel, (shape((SUBS, 4 * SIDE, VIS), BF16), shape((SUBS, 2 * SIDE, VIS))), [VMEM], (VMEM, VMEM)
    )(uv)

    found = call(
        gather_kernel,
        shape((PEERS, 2 * ENDS, LANES), BF16),
        [VMEM] * 3 + [HBM],
        HBM,
        [pltpu.VMEM((PEERS, ENDS, LANES), BF16), pltpu.SemaphoreType.DMA],
        {3: 0},
    )(table, *columns, patches)
    got_c = exchange(found, ACROSS)

    owner = offsets[0] >> 8
    same = owner[:, None] == owner[None, :]
    earlier = jnp.arange(SUBS)[:, None] > jnp.arange(SUBS)[None, :]
    slot = owner * 2 + jnp.sum((same & earlier).astype(S32), axis=1)
    result, grads = main(slot, got_c, *waves, observed, flags)

    back_c = exchange(grads.reshape(PEERS, SUBS, LANES), ACROSS).reshape(TABLE, LANES)
    dense = call(scatter_kernel, shape((TABLE, LANES)), [VMEM] * 5, VMEM)(
        back_c, *columns, first[None, :], second[None, :]
    )
    back_b = exchange(dense.reshape(GROUPS, ROWS, LANES), NEAR)
    summed = call(add_kernel, shape((PEERS, SUBS, LANES)), [VMEM], VMEM)(back_b)
    back_a = exchange(summed, ACROSS)
    total = call(
        place_kernel,
        shape((SUBS, 2, 4, SIDE * SIDE)),
        [VMEM],
        HBM,
        [pltpu.VMEM((SUBS, 2, 4, SIDE * SIDE), F32), pltpu.SemaphoreType.DMA((8,))],
    )(back_a)
    return (result, total)


def solution(mesh):
    fine = Mesh(mesh.devices.reshape(8, 4, 2, 8), ("z", "x", "core", "tile"))
    st = ("z", "x", "core")
    every = ("z", "x", "core", "tile")
    placed = (
        P(None, "tile", None),
        P(st, None, None, None),
        P(every, None),
        P(every),
        P(every, None),
        P(every, None, None),
        P(every, None, None),
        P(every, None),
    )
    return jax.shard_map(
        body,
        mesh=fine,
        in_specs=placed,
        out_specs=(P(every, None, None), P(st, None, None, None)),
        check_vma=False,
    )
```

```python
import jax
import jax.numpy as jnp
import numpy as np
from jax import lax
from jax.experimental import pallas as pl
from jax.experimental.pallas import tpu as pltpu
from jax.sharding import Mesh
from jax.sharding import PartitionSpec as P

SIDE = 32
SUBS = 8
ENDS = 2 * SUBS
VIS = 512
PEERS = 64
GROUPS = 8
ROWS = 64
TABLE = GROUPS * ROWS
LANES = 128
SLOTS = 16

F32 = jnp.float32
BF16 = jnp.bfloat16
S32 = jnp.int32


def bf16_parts(array, count):
    rest = np.asarray(array, np.float64)
    parts = []
    for _ in range(count):
        part = rest.astype(np.float32).astype(jnp.bfloat16)
        parts.append(part)
        rest = rest - part.astype(np.float64)
    return parts


def dft_tables():
    index = np.arange(SIDE)
    angle = 2.0 * np.pi * (index[:, None] * index[None, :] % SIDE) / SIDE
    f_real = np.cos(angle) / SIDE
    f_imag = np.sin(angle) / SIDE
    rows = np.concatenate([f_real, f_imag], axis=0)
    rows_parts = np.concatenate(bf16_parts(rows, 3), axis=1)
    eye = np.eye(4)
    cols = np.concatenate([np.kron(eye, f_real.T), np.kron(eye, f_imag.T)], axis=1)
    hi, lo = bf16_parts(cols, 2)
    cols_parts = np.concatenate([hi, hi, lo], axis=0)
    edge = np.cos(np.pi * (index - (SIDE - 1) / 2.0) / SIDE)
    taper = np.tile(edge[:, None] * edge[None, :], (1, 4)).astype(np.float32)
    return rows_parts, cols_parts, taper


def turn_polynomials():
    nodes = 0.25 * np.cos(np.pi * (np.arange(400) + 0.5) / 400) ** 2
    r = np.sqrt(nodes)
    scaled = nodes * 4.0
    sine = np.polynomial.polynomial.polyfit(scaled, np.sin(2 * np.pi * r) / r, 7)
    cosine = np.polynomial.polynomial.polyfit(scaled, np.cos(2 * np.pi * r), 8)
    power = 4.0 ** np.arange(9)
    return [float(a) for a in sine * power[:8]], [float(a) for a in cosine * power]


SINE, COSINE = turn_polynomials()


def unit_circle(turns):
    r = turns - jnp.floor(turns + 0.5)
    r2 = r * r
    s = jnp.full_like(r, SINE[-1])
    for a in SINE[-2::-1]:
        s = s * r2 + a
    c = jnp.full_like(r, COSINE[-1])
    for a in COSINE[-2::-1]:
        c = c * r2 + a
    return c, s * r


def split(x):
    hi = x.astype(BF16)
    return hi, (x - hi.astype(F32)).astype(BF16)


def dot(a, b, contract):
    return lax.dot_general(a, b, ((contract[:1], contract[1:]), ((), ())), preferred_element_type=F32)


def slots(offsets_ref):
    tiles = [offsets_ref[0, k] >> 8 for k in range(SUBS)]
    seconds = []
    for k in range(SUBS):
        second = jnp.zeros((), S32)
        for j in range(k):
            second = jnp.where(tiles[j] == tiles[k], 1, second)
        seconds.append(second)
    return tiles, seconds


def prep_kernel(
    stations_in, intervals_in, offsets_in, terms_in, out_ref, stations_ref, intervals_ref, offsets_ref, terms_ref, sems
):
    own = lax.axis_index("tile")
    copies = [
        pltpu.make_async_copy(stations_in, stations_ref, sems.at[0]),
        pltpu.make_async_copy(intervals_in, intervals_ref, sems.at[1]),
        pltpu.make_async_copy(offsets_in, offsets_ref, sems.at[2]),
        pltpu.make_async_copy(terms_in.at[own], terms_ref, sems.at[3]),
    ]
    for copy in copies:
        copy.start()
    for copy in copies:
        copy.wait()
    spot = lax.broadcasted_iota(S32, (1, LANES), 1)
    asked = jnp.zeros((1, LANES), S32)
    tiles, seconds = slots(offsets_ref)
    for k in range(SUBS):
        for end in range(2):
            station = stations_ref[end, k]
            row = ((station >> 3) & 7) * ROWS + (station >> 6) * 8 + (station & 7)
            asked = jnp.where(spot == end * SUBS + k, row + TABLE * intervals_ref[k], asked)
        code = (offsets_ref[0, k] & 255) * LANES + offsets_ref[1, k]
        asked = jnp.where(spot == ENDS + 2 * tiles[k] + seconds[k], code, asked)
    out_ref[:, 1:2, :] = jnp.broadcast_to(asked.astype(F32).reshape(1, 1, LANES), (PEERS, 1, LANES))
    lane = spot // SIDE
    for block in range(8):
        turned = []
        for interval in range(2):
            comps = terms_ref[interval, :, block * LANES : (block + 1) * LANES]
            turned.append([comps if d == 0 else pltpu.roll(comps, d * SIDE, 1) for d in range(4)])
        for i in range(4):
            for half in range(2):
                total = jnp.zeros((1, LANES), F32)
                for place in range(4):
                    comp = 2 * half + (place & 1)
                    piece = turned[place >> 1][(place - i) % 4][comp : comp + 1, :]
                    total = piece if place == 0 else jnp.where(lane == place, piece, total)
                out_ref[(4 * block + i) * 2 + half, 0:1, :] = total


def wave_kernel(uv_ref, row_wave_ref, column_wave_ref):
    centre = (lax.broadcasted_iota(S32, (SIDE, VIS), 0).astype(F32) - SIDE / 2.0) * (1.0 / SIDE)

    def one(k, carry):
        real, imag = unit_circle(uv_ref[k, 0:1, :] * centre)
        hi, lo = split(jnp.concatenate([real, imag], axis=0))
        row_wave_ref[k] = jnp.concatenate([hi, lo], axis=0)
        real, imag = unit_circle(uv_ref[k, 1:2, :] * centre)
        column_wave_ref[k] = jnp.concatenate([real, imag], axis=0)
        return carry

    lax.fori_loop(0, SUBS, one, 0)


def cut_kernel(place_ref, wanted_ref, strip_ref, out_hbm, wide_ref, out_ref, sem):
    wide_ref[...] = strip_ref[0].astype(F32)
    tile = place_ref[0]
    part_of = place_ref[1]
    half = SIDE // 2
    lane = lax.broadcasted_iota(S32, (half, LANES), 1) // SIDE

    def one(i, carry):
        total = jnp.zeros((half, LANES), F32)
        for slot in range(2):
            code = wanted_ref[i, 2 * tile + slot]
            row = code >> 7
            column = code & (LANES - 1)
            for part in range(2):
                spot = (part_of + 2 * slot + part) & 3
                piece = wide_ref[pl.ds(row + half * part, half), :]
                piece = pltpu.roll(piece, (spot * SIDE + LANES - column) & (LANES - 1), 1)
                total = jnp.where(lane == spot, piece, total)
        out_ref[i] = total.astype(BF16)
        return carry

    lax.fori_loop(0, PEERS, one, 0, unroll=8)
    copy = pltpu.make_async_copy(out_ref, out_hbm.at[:, pl.ds(ENDS, ENDS), :], sem)
    copy.start()
    copy.wait()


def spread_kernel(got_ref, out_ref):
    part = got_ref[:, 0:1, :].reshape(ROWS, LANES)
    for i in range(GROUPS):
        out_ref[i] = part


def gather_kernel(table_ref, first_ref, second_ref, patched_hbm, out_hbm, out_ref, sem):
    hi, lo = split(table_ref[...])
    table = jnp.concatenate([hi, lo], axis=1)
    ids = lax.broadcasted_iota(S32, (TABLE, TABLE), 1)
    left = lax.broadcasted_iota(S32, (TABLE, LANES), 1) < LANES // 2
    sides = []
    for code_ref in (first_ref, second_ref):
        code = code_ref[...]
        chosen = jnp.where(ids == (code & (TABLE - 1)), 1.0, 0.0).astype(BF16)
        found = dot(chosen, table, (1, 0))
        found = found[:, :LANES] + found[:, LANES:]
        sides.append((found, pltpu.roll(found, LANES // 2, 1), code >= TABLE))
    first = jnp.where(sides[0][2], sides[0][1], sides[0][0])
    second = jnp.where(sides[1][2], sides[1][0], sides[1][1])
    beams = jnp.where(left, first, second)
    hi = beams.astype(BF16).astype(F32)
    both = jnp.concatenate([hi.reshape(PEERS, SUBS, LANES), (beams - hi).reshape(PEERS, SUBS, LANES)], axis=1)
    out_ref[...] = both.astype(BF16)
    copy = pltpu.make_async_copy(out_ref, out_hbm.at[:, pl.ds(0, ENDS), :], sem)
    copy.start()
    copy.wait()


def scatter_kernel(got_ref, first_ref, second_ref, first_row_ref, second_row_ref, out_ref):
    got = got_ref[...]
    turned = pltpu.roll(got, LANES // 2, 1)
    left = lax.broadcasted_iota(S32, (TABLE, LANES), 1) < LANES // 2
    ids = lax.broadcasted_iota(S32, (TABLE, TABLE), 0)
    values, chosen = [], []
    for spread, code_ref, row_ref in (
        (jnp.where(left, got, turned), first_ref, first_row_ref),
        (jnp.where(left, turned, got), second_ref, second_row_ref),
    ):
        late = code_ref[...] >= TABLE
        values.append(jnp.where(late != left, spread, 0.0))
        chosen.append(jnp.where(ids == (row_ref[...] & (TABLE - 1)), 1.0, 0.0).astype(BF16))
    hi, lo = split(jnp.concatenate(values, axis=0))
    total = dot(jnp.concatenate(chosen, axis=1), jnp.concatenate([hi, lo], axis=1), (1, 0))
    out_ref[...] = total[:, :LANES] + total[:, LANES:]


def add_kernel(parts_ref, out_ref):
    total = parts_ref[0]
    for i in range(1, GROUPS):
        total = total + parts_ref[i]
    for i in range(PEERS):
        part = i // 8
        out_ref[i] = total[part * SUBS : (part + 1) * SUBS, :]


def place_kernel(parts_ref, out_hbm, out_ref, sems):
    copies = []
    lane = lax.broadcasted_iota(S32, (SUBS, LANES), 1) // SIDE
    for block in range(8):
        for half in range(2):
            rows = [parts_ref[2 * (4 * block + i) + half] for i in range(4)]
            turned = [[rows[i] if d == 0 else pltpu.roll(rows[i], d * SIDE, 1) for d in range(4)] for i in range(4)]
            for interval in range(2):
                for part in range(2):
                    at = 2 * interval + part
                    total = turned[0][(0 - at) % 4]
                    for i in range(1, 4):
                        total = jnp.where(lane == i, turned[i][(i - at) % 4], total)
                    out_ref[:, interval, 2 * half + part, block * LANES : (block + 1) * LANES] = total
        lanes = pl.ds(block * LANES, LANES)
        copies.append(
            pltpu.make_async_copy(out_ref.at[:, :, :, lanes], out_hbm.at[:, :, :, lanes], sems.at[block])
        )
        copies[-1].start()
    for copy in copies:
        copy.wait()


def main_kernel(
    slot_ref, got_ref, row_wave_ref, column_wave_ref, seen_in, flag_in, rows_ref, cols_ref, taper_ref,
    res_ref, out_ref, grad_ref, beam_ref, seen_ref, flag_ref, side_ref, z_ref, dz_ref, held_ref, sems,
):
    copies = [
        pltpu.make_async_copy(a, b, sems.at[i])
        for i, (a, b) in enumerate(
            ((seen_in, seen_ref), (flag_in, flag_ref))
        )
    ]
    for copy in copies:
        copy.start()
    got = got_ref[:, 0:ENDS, :].astype(F32)
    beam_ref[0:TABLE, :] = (got[:, :SUBS] + got[:, SUBS:]).reshape(TABLE, LANES)
    narrow = lax.broadcasted_iota(S32, (SIDE // 2, LANES), 1) // SIDE
    lane = lax.broadcasted_iota(S32, (SIDE, LANES), 1) // SIDE
    taper = taper_ref[...]

    def turn(x, blocks):
        return pltpu.roll(x, blocks * SIDE, 1)

    patches = []
    for k in range(SUBS):
        slot = slot_ref[k]
        tile = slot >> 1
        second = (slot & 1) > 0
        shift = 2 * (slot & 1)
        upper = (narrow - shift) & 3
        lower = (narrow - shift - 1) & 3
        for part in range(2):
            top = jnp.zeros((SIDE // 2, LANES), F32)
            low = top
            for i in range(4):
                piece = got_ref[8 * (4 * part + i) + tile, ENDS : 2 * ENDS, :].astype(F32)
                top = jnp.where(upper == i, piece, top)
                low = jnp.where(lower == i, piece, low)
            top = jnp.where(second, turn(top, 2), top)
            low = jnp.where(second, turn(low, 1), turn(low, 3))
            patches.append(jnp.concatenate([top, low], axis=0).astype(BF16))
    patch = jnp.concatenate(patches, axis=1)
    a = dot(rows_ref[...], jnp.concatenate([patch, patch, patch], axis=0), (1, 0))
    mixed = []
    for k in range(SUBS):
        re = a[:, 2 * k * LANES : (2 * k + 1) * LANES]
        im = a[:, (2 * k + 1) * LANES : (2 * k + 2) * LANES]
        mixed += [re[:SIDE] - im[SIDE:], im[:SIDE] + re[SIDE:]]
    hi, lo = split(jnp.concatenate(mixed, axis=0))
    images = dot(jnp.concatenate([hi, lo, hi], axis=1), cols_ref[...], (1, 0))

    for k in range(SUBS):
        b = images[2 * k * SIDE : 2 * (k + 1) * SIDE]
        i_re = b[:SIDE, :LANES] - b[SIDE:, LANES:]
        i_im = b[:SIDE, LANES:] + b[SIDE:, :LANES]

        sides = []
        for half in range(2):
            g = beam_ref[pl.ds(k + SUBS * half, SIDE, stride=2 * SUBS), :]
            g1, g2 = turn(g, 1), turn(g, 2)
            sides.append((jnp.where(lane == 0, g, jnp.where(lane == 3, g2, g1)), jnp.where(lane < 2, g2, g)))
        (p_re, q_re), (p_im, q_im) = sides

        y_re = i_re * q_re + i_im * q_im
        y_im = i_im * q_re - i_re * q_im
        z_re = (p_re * y_re - p_im * y_im) * taper
        z_im = (p_re * y_im + p_im * y_re) * taper
        for i, part in enumerate((i_re, i_im, p_re, p_im, y_re, y_im)):
            side_ref[k, i] = part * taper if i > 3 else part
        z = jnp.concatenate(
            [jnp.concatenate([z_re, z_im], axis=1), jnp.concatenate([-z_im, z_re], axis=1)], axis=0
        )
        z_hi, z_lo = split(z)
        z_ref[k] = jnp.concatenate([z_hi, z_lo, z_hi], axis=0)

    for copy in copies:
        copy.wait()

    def one(k, carry):
        row_wave = row_wave_ref[k]
        ev_re = column_wave_ref[k, :SIDE, :]
        ev_im = column_wave_ref[k, SIDE:, :]
        w = dot(z_ref[k], jnp.concatenate([row_wave[: 2 * SIDE], row_wave], axis=0), (0, 0))
        reals, imags = [], []
        for pol in range(4):
            w_re = w[pol * SIDE : (pol + 1) * SIDE]
            w_im = w[LANES + pol * SIDE : LANES + (pol + 1) * SIDE]
            reals.append(jnp.sum(w_re * ev_re - w_im * ev_im, axis=0, keepdims=True))
            imags.append(jnp.sum(w_re * ev_im + w_im * ev_re, axis=0, keepdims=True))
        model = jnp.concatenate(reals + imags, axis=0)
        used = flag_ref[pl.ds(k, 1), :].astype(F32)
        res = used * (seen_ref[k] - model)
        res_ref[k] = res
        back = -used * res

        t_re, t_im = [], []
        for pol in range(4):
            d_re = back[pol : pol + 1]
            d_im = back[4 + pol : 5 + pol]
            t_re.append(ev_re * d_re + ev_im * d_im)
            t_im.append(ev_re * d_im - ev_im * d_re)
        t_hi, t_lo = split(jnp.concatenate(t_re + t_im, axis=0))
        held_ref[k, 0] = t_hi
        held_ref[k, 1] = t_lo
        return carry

    def two(k, carry):
        row_wave = row_wave_ref[k]
        t_hi = held_ref[k, 0]
        t_lo = held_ref[k, 1]
        both = dot(row_wave, t_hi, (1, 1))
        dz_ref[k] = both[: 2 * SIDE] + both[2 * SIDE :] + dot(row_wave[: 2 * SIDE], t_lo, (1, 1))
        return carry

    for k in range(SUBS + 1):
        if k < SUBS:
            one(k, 0)
        if k > 0:
            two(k - 1, 0)

    for k in range(SUBS):
        d = dz_ref[k]
        i_re, i_im, p_re, p_im, y_re, y_im = (side_ref[k, i] for i in range(6))
        dz_re = d[:SIDE, :LANES] + d[SIDE:, LANES:]
        dz_im = d[:SIDE, LANES:] - d[SIDE:, :LANES]

        dp_re = dz_re * y_re + dz_im * y_im
        dp_im = dz_im * y_re - dz_re * y_im
        dp_re = dp_re + turn(dp_re, 3)
        dp_im = dp_im + turn(dp_im, 3)
        i_re = i_re * taper
        i_im = i_im * taper
        dy_re = dz_re * p_re + dz_im * p_im
        dy_im = dz_im * p_re - dz_re * p_im
        dq_re = dy_re * i_re + dy_im * i_im
        dq_im = dy_re * i_im - dy_im * i_re
        dq_re = dq_re + turn(dq_re, 2)
        dq_im = dq_im + turn(dq_im, 2)
        for half, (dp, dq) in enumerate(((dp_re, dq_re), (dp_im, dq_im))):
            grad = jnp.where(lane == 0, dp, jnp.where(lane == 1, turn(dp, 3), dq))
            grad_ref[pl.ds(k + SUBS * half, SIDE, stride=2 * SUBS), :] = grad
    out_ref[...] = grad_ref[0:TABLE, :]


SMEM = pl.BlockSpec(memory_space=pltpu.SMEM)
VMEM = pl.BlockSpec(memory_space=pltpu.VMEM)
HBM = pl.BlockSpec(memory_space=pltpu.HBM)
PARAMS = pltpu.CompilerParams(vmem_limit_bytes=40 * 1024 * 1024)


def call(kernel, shapes, specs, out_specs, scratch=(), aliases=None):
    return pl.pallas_call(
        kernel,
        out_shape=shapes,
        in_specs=specs,
        out_specs=out_specs,
        scratch_shapes=list(scratch),
        input_output_aliases=aliases or {},
        compiler_params=PARAMS,
    )


def shape(dims, dtype=F32):
    return jax.ShapeDtypeStruct(dims, dtype)


def cut(place, wanted, grid):
    return pl.pallas_call(
        cut_kernel,
        out_shape=shape((PEERS, 2 * ENDS, LANES), BF16),
        grid_spec=pltpu.PrefetchScalarGridSpec(
            num_scalar_prefetch=2,
            grid=(1,),
            in_specs=[pl.BlockSpec((1, grid.shape[1], LANES), lambda i, place, wanted: (place[1], 0, 0))],
            out_specs=HBM,
            scratch_shapes=[
                pltpu.VMEM((grid.shape[1], LANES), F32),
                pltpu.VMEM((PEERS, ENDS, LANES), BF16),
                pltpu.SemaphoreType.DMA,
            ],
        ),
        compiler_params=PARAMS,
    )(place, wanted, grid)


def in_hbm(x):
    return pltpu.with_memory_space_constraint(x, pltpu.HBM)


def exchange(x, axes):
    return lax.all_to_all(x, axes, split_axis=0, concat_axis=0, tiled=True)


def main(slot, got, row_waves, column_waves, *rest):
    waves = [pltpu.with_memory_space_constraint(x, pltpu.VMEM) for x in (row_waves, column_waves)]
    tables = [jnp.asarray(t) for t in dft_tables()]
    return call(
        main_kernel,
        (shape((SUBS, 8, VIS)), shape((TABLE, LANES))),
        [SMEM] + [VMEM] * 3 + [HBM] * 2 + [VMEM] * 3,
        (VMEM, VMEM),
        [
            pltpu.VMEM((TABLE + 2 * SUBS, LANES), F32),
            pltpu.VMEM((TABLE + 2 * SUBS, LANES), F32),
            pltpu.VMEM((SUBS, 8, VIS), F32),
            pltpu.VMEM((SUBS, VIS), S32),
            pltpu.VMEM((SUBS, 6, SIDE, LANES), F32),
            pltpu.VMEM((SUBS, 6 * SIDE, 2 * LANES), BF16),
            pltpu.VMEM((SUBS, 2 * SIDE, 2 * LANES), F32),
            pltpu.VMEM((SUBS, 2, 2 * LANES, VIS), BF16),
            pltpu.SemaphoreType.DMA((4,)),
        ],
    )(slot, got, *waves, *(in_hbm(x) for x in rest), *tables)


ACROSS = ("z", "tile")
NEAR = ("x", "core")


def body(grid, a_terms, stations, intervals, offsets, uv, observed, flags):
    place = jnp.stack([lax.axis_index(name).astype(S32) for name in ("tile", "z")])
    offsets = offsets.T
    sent = call(
        prep_kernel,
        shape((PEERS, 2, LANES)),
        [HBM] * 4,
        VMEM,
        [
            pltpu.SMEM((2, SUBS), S32),
            pltpu.SMEM((SUBS,), S32),
            pltpu.SMEM((2, SUBS), S32),
            pltpu.VMEM((2, 4, SIDE * SIDE), F32),
            pltpu.SemaphoreType.DMA((4,)),
        ],
    )(*(in_hbm(x) for x in (stations.T, intervals, offsets, a_terms)))
    got_a = exchange(sent, ACROSS)
    spread = call(spread_kernel, shape((GROUPS, ROWS, LANES)), [VMEM], VMEM)(got_a)
    table = exchange(spread, NEAR).reshape(TABLE, LANES)

    wanted = got_a[:, 1, :].astype(S32)
    first = wanted[:, :SUBS].reshape(TABLE)
    second = wanted[:, SUBS:ENDS].reshape(TABLE)
    columns = (first[:, None], second[:, None])
    patches = cut(place, wanted[:, ENDS : ENDS + SLOTS], grid)
    waves = call(
        wave_kernel, (shape((SUBS, 4 * SIDE, VIS), BF16), shape((SUBS, 2 * SIDE, VIS))), [VMEM], (VMEM, VMEM)
    )(uv)

    found = call(
        gather_kernel,
        shape((PEERS, 2 * ENDS, LANES), BF16),
        [VMEM] * 3 + [HBM],
        HBM,
        [pltpu.VMEM((PEERS, ENDS, LANES), BF16), pltpu.SemaphoreType.DMA],
        {3: 0},
    )(table, *columns, patches)
    got_c = exchange(found, ACROSS)

    owner = offsets[0] >> 8
    same = owner[:, None] == owner[None, :]
    earlier = jnp.arange(SUBS)[:, None] > jnp.arange(SUBS)[None, :]
    slot = owner * 2 + jnp.sum((same & earlier).astype(S32), axis=1)
    result, grads = main(slot, got_c, *waves, observed, flags)

    back_c = exchange(grads.reshape(PEERS, SUBS, LANES), ACROSS).reshape(TABLE, LANES)
    dense = call(scatter_kernel, shape((TABLE, LANES)), [VMEM] * 5, VMEM)(
        back_c, *columns, first[None, :], second[None, :]
    )
    back_b = exchange(dense.reshape(GROUPS, ROWS, LANES), NEAR)
    summed = call(add_kernel, shape((PEERS, SUBS, LANES)), [VMEM], VMEM)(back_b)
    back_a = exchange(summed, ACROSS)
    total = call(
        place_kernel,
        shape((SUBS, 2, 4, SIDE * SIDE)),
        [VMEM],
        HBM,
        [pltpu.VMEM((SUBS, 2, 4, SIDE * SIDE), F32), pltpu.SemaphoreType.DMA((8,))],
    )(back_a)
    return (result, total)


def solution(mesh):
    fine = Mesh(mesh.devices.reshape(8, 4, 2, 8), ("z", "x", "core", "tile"))
    st = ("z", "x", "core")
    every = ("z", "x", "core", "tile")
    placed = (
        P(None, "tile", None),
        P(st, None, None, None),
        P(every, None),
        P(every),
        P(every, None),
        P(every, None, None),
        P(every, None, None),
        P(every, None),
    )
    return jax.shard_map(
        body,
        mesh=fine,
        in_specs=placed,
        out_specs=(P(every, None, None), P(st, None, None, None)),
        check_vma=False,
    )
```

```python
import jax
import jax.numpy as jnp
import numpy as np
from jax import lax
from jax.experimental import pallas as pl
from jax.experimental.pallas import tpu as pltpu
from jax.sharding import Mesh
from jax.sharding import PartitionSpec as P

SIDE = 32
SUBS = 8
ENDS = 2 * SUBS
VIS = 512
PEERS = 64
GROUPS = 8
ROWS = 64
TABLE = GROUPS * ROWS
LANES = 128
SLOTS = 16

F32 = jnp.float32
BF16 = jnp.bfloat16
S32 = jnp.int32


def bf16_parts(array, count):
    rest = np.asarray(array, np.float64)
    parts = []
    for _ in range(count):
        part = rest.astype(np.float32).astype(jnp.bfloat16)
        parts.append(part)
        rest = rest - part.astype(np.float64)
    return parts


def dft_tables():
    index = np.arange(SIDE)
    angle = 2.0 * np.pi * (index[:, None] * index[None, :] % SIDE) / SIDE
    f_real = np.cos(angle) / SIDE
    f_imag = np.sin(angle) / SIDE
    rows = np.concatenate([f_real, f_imag], axis=0)
    rows_parts = np.concatenate(bf16_parts(rows, 3), axis=1)
    eye = np.eye(4)
    cols = np.concatenate([np.kron(eye, f_real.T), np.kron(eye, f_imag.T)], axis=1)
    hi, lo = bf16_parts(cols, 2)
    cols_parts = np.concatenate([hi, hi, lo], axis=0)
    edge = np.cos(np.pi * (index - (SIDE - 1) / 2.0) / SIDE)
    taper = np.tile(edge[:, None] * edge[None, :], (1, 4)).astype(np.float32)
    return rows_parts, cols_parts, taper


def turn_polynomials():
    nodes = 0.25 * np.cos(np.pi * (np.arange(400) + 0.5) / 400) ** 2
    r = np.sqrt(nodes)
    scaled = nodes * 4.0
    sine = np.polynomial.polynomial.polyfit(scaled, np.sin(2 * np.pi * r) / r, 7)
    cosine = np.polynomial.polynomial.polyfit(scaled, np.cos(2 * np.pi * r), 8)
    power = 4.0 ** np.arange(9)
    return [float(a) for a in sine * power[:8]], [float(a) for a in cosine * power]


SINE, COSINE = turn_polynomials()


def unit_circle(turns):
    r = turns - jnp.floor(turns + 0.5)
    r2 = r * r
    s = jnp.full_like(r, SINE[-1])
    for a in SINE[-2::-1]:
        s = s * r2 + a
    c = jnp.full_like(r, COSINE[-1])
    for a in COSINE[-2::-1]:
        c = c * r2 + a
    return c, s * r


def split(x):
    hi = x.astype(BF16)
    return hi, (x - hi.astype(F32)).astype(BF16)


def dot(a, b, contract):
    return lax.dot_general(a, b, ((contract[:1], contract[1:]), ((), ())), preferred_element_type=F32)


def slots(offsets_ref):
    tiles = [offsets_ref[0, k] >> 8 for k in range(SUBS)]
    seconds = []
    for k in range(SUBS):
        second = jnp.zeros((), S32)
        for j in range(k):
            second = jnp.where(tiles[j] == tiles[k], 1, second)
        seconds.append(second)
    return tiles, seconds


def prep_kernel(
    stations_in, intervals_in, offsets_in, terms_in, out_ref, stations_ref, intervals_ref, offsets_ref, terms_ref, sems
):
    own = lax.axis_index("tile")
    copies = [
        pltpu.make_async_copy(stations_in, stations_ref, sems.at[0]),
        pltpu.make_async_copy(intervals_in, intervals_ref, sems.at[1]),
        pltpu.make_async_copy(offsets_in, offsets_ref, sems.at[2]),
        pltpu.make_async_copy(terms_in.at[own], terms_ref, sems.at[3]),
    ]
    for copy in copies:
        copy.start()
    for copy in copies:
        copy.wait()
    spot = lax.broadcasted_iota(S32, (1, LANES), 1)
    asked = jnp.zeros((1, LANES), S32)
    tiles, seconds = slots(offsets_ref)
    for k in range(SUBS):
        for end in range(2):
            station = stations_ref[end, k]
            row = ((station >> 3) & 7) * ROWS + (station >> 6) * 8 + (station & 7)
            asked = jnp.where(spot == end * SUBS + k, row + TABLE * intervals_ref[k], asked)
        code = (offsets_ref[0, k] & 255) * LANES + offsets_ref[1, k]
        asked = jnp.where(spot == ENDS + 2 * tiles[k] + seconds[k], code, asked)
    out_ref[:, 1:2, :] = jnp.broadcast_to(asked.astype(F32).reshape(1, 1, LANES), (PEERS, 1, LANES))
    lane = spot // SIDE
    for block in range(8):
        turned = []
        for interval in range(2):
            comps = terms_ref[interval, :, block * LANES : (block + 1) * LANES]
            turned.append([comps if d == 0 else pltpu.roll(comps, d * SIDE, 1) for d in range(4)])
        for i in range(4):
            for half in range(2):
                total = jnp.zeros((1, LANES), F32)
                for place in range(4):
                    comp = 2 * half + (place & 1)
                    piece = turned[place >> 1][(place - i) % 4][comp : comp + 1, :]
                    total = piece if place == 0 else jnp.where(lane == place, piece, total)
                out_ref[(4 * block + i) * 2 + half, 0:1, :] = total


def wave_kernel(uv_ref, row_wave_ref, column_wave_ref):
    centre = (lax.broadcasted_iota(S32, (SIDE, VIS), 0).astype(F32) - SIDE / 2.0) * (1.0 / SIDE)

    def one(k, carry):
        real, imag = unit_circle(uv_ref[k, 0:1, :] * centre)
        hi, lo = split(jnp.concatenate([real, imag], axis=0))
        row_wave_ref[k] = jnp.concatenate([hi, lo], axis=0)
        real, imag = unit_circle(uv_ref[k, 1:2, :] * centre)
        column_wave_ref[k] = jnp.concatenate([real, imag], axis=0)
        return carry

    lax.fori_loop(0, SUBS, one, 0)


def cut_kernel(place_ref, wanted_ref, strip_ref, out_hbm, wide_ref, out_ref, sem):
    wide_ref[...] = strip_ref[0].astype(F32)
    tile = place_ref[0]
    part_of = place_ref[1]
    half = SIDE // 2
    lane = lax.broadcasted_iota(S32, (half, LANES), 1) // SIDE

    def one(i, carry):
        total = jnp.zeros((half, LANES), F32)
        for slot in range(2):
            code = wanted_ref[i, 2 * tile + slot]
            row = code >> 7
            column = code & (LANES - 1)
            for part in range(2):
                spot = (part_of + 2 * slot + part) & 3
                piece = wide_ref[pl.ds(row + half * part, half), :]
                piece = pltpu.roll(piece, (spot * SIDE + LANES - column) & (LANES - 1), 1)
                total = jnp.where(lane == spot, piece, total)
        out_ref[i] = total.astype(BF16)
        return carry

    lax.fori_loop(0, PEERS, one, 0, unroll=8)
    copy = pltpu.make_async_copy(out_ref, out_hbm.at[:, pl.ds(ENDS, ENDS), :], sem)
    copy.start()
    copy.wait()


def spread_kernel(got_ref, out_hbm, part_ref, sems):
    part_ref[...] = got_ref[:, 0:1, :].reshape(ROWS, LANES)
    copies = [pltpu.make_async_copy(part_ref, out_hbm.at[i], sems.at[i]) for i in range(GROUPS)]
    for copy in copies:
        copy.start()
    for copy in copies:
        copy.wait()


def gather_kernel(table_ref, first_ref, second_ref, patched_hbm, out_hbm, out_ref, sem):
    hi, lo = split(table_ref[...])
    table = jnp.concatenate([hi, lo], axis=1)
    ids = lax.broadcasted_iota(S32, (TABLE, TABLE), 1)
    left = lax.broadcasted_iota(S32, (TABLE, LANES), 1) < LANES // 2
    sides = []
    for code_ref in (first_ref, second_ref):
        code = code_ref[...]
        chosen = jnp.where(ids == (code & (TABLE - 1)), 1.0, 0.0).astype(BF16)
        found = dot(chosen, table, (1, 0))
        found = found[:, :LANES] + found[:, LANES:]
        sides.append((found, pltpu.roll(found, LANES // 2, 1), code >= TABLE))
    first = jnp.where(sides[0][2], sides[0][1], sides[0][0])
    second = jnp.where(sides[1][2], sides[1][0], sides[1][1])
    beams = jnp.where(left, first, second)
    hi = beams.astype(BF16).astype(F32)
    both = jnp.concatenate([hi.reshape(PEERS, SUBS, LANES), (beams - hi).reshape(PEERS, SUBS, LANES)], axis=1)
    out_ref[...] = both.astype(BF16)
    copy = pltpu.make_async_copy(out_ref, out_hbm.at[:, pl.ds(0, ENDS), :], sem)
    copy.start()
    copy.wait()


def scatter_kernel(got_ref, first_ref, second_ref, first_row_ref, second_row_ref, out_ref):
    got = got_ref[...]
    turned = pltpu.roll(got, LANES // 2, 1)
    left = lax.broadcasted_iota(S32, (TABLE, LANES), 1) < LANES // 2
    ids = lax.broadcasted_iota(S32, (TABLE, TABLE), 0)
    values, chosen = [], []
    for spread, code_ref, row_ref in (
        (jnp.where(left, got, turned), first_ref, first_row_ref),
        (jnp.where(left, turned, got), second_ref, second_row_ref),
    ):
        late = code_ref[...] >= TABLE
        values.append(jnp.where(late != left, spread, 0.0))
        chosen.append(jnp.where(ids == (row_ref[...] & (TABLE - 1)), 1.0, 0.0).astype(BF16))
    hi, lo = split(jnp.concatenate(values, axis=0))
    total = dot(jnp.concatenate(chosen, axis=1), jnp.concatenate([hi, lo], axis=1), (1, 0))
    out_ref[...] = total[:, :LANES] + total[:, LANES:]


def add_kernel(parts_ref, out_ref):
    total = parts_ref[0]
    for i in range(1, GROUPS):
        total = total + parts_ref[i]
    for i in range(PEERS):
        part = i // 8
        out_ref[i] = total[part * SUBS : (part + 1) * SUBS, :]


def place_kernel(parts_ref, out_hbm, out_ref, sems):
    copies = []
    lane = lax.broadcasted_iota(S32, (SUBS, LANES), 1) // SIDE
    for block in range(8):
        for half in range(2):
            rows = [parts_ref[2 * (4 * block + i) + half] for i in range(4)]
            turned = [[rows[i] if d == 0 else pltpu.roll(rows[i], d * SIDE, 1) for d in range(4)] for i in range(4)]
            for interval in range(2):
                for part in range(2):
                    at = 2 * interval + part
                    total = turned[0][(0 - at) % 4]
                    for i in range(1, 4):
                        total = jnp.where(lane == i, turned[i][(i - at) % 4], total)
                    out_ref[:, interval, 2 * half + part, block * LANES : (block + 1) * LANES] = total
        lanes = pl.ds(block * LANES, LANES)
        copies.append(
            pltpu.make_async_copy(out_ref.at[:, :, :, lanes], out_hbm.at[:, :, :, lanes], sems.at[block])
        )
        copies[-1].start()
    for copy in copies:
        copy.wait()


def main_kernel(
    slot_ref, got_ref, row_wave_ref, column_wave_ref, seen_in, flag_in, rows_ref, cols_ref, taper_ref,
    res_ref, out_ref, grad_ref, beam_ref, seen_ref, flag_ref, side_ref, z_ref, dz_ref, held_ref, sems,
):
    copies = [
        pltpu.make_async_copy(a, b, sems.at[i])
        for i, (a, b) in enumerate(
            ((seen_in, seen_ref), (flag_in, flag_ref))
        )
    ]
    for copy in copies:
        copy.start()
    got = got_ref[:, 0:ENDS, :].astype(F32)
    beam_ref[0:TABLE, :] = (got[:, :SUBS] + got[:, SUBS:]).reshape(TABLE, LANES)
    narrow = lax.broadcasted_iota(S32, (SIDE // 2, LANES), 1) // SIDE
    lane = lax.broadcasted_iota(S32, (SIDE, LANES), 1) // SIDE
    taper = taper_ref[...]

    def turn(x, blocks):
        return pltpu.roll(x, blocks * SIDE, 1)

    patches = []
    for k in range(SUBS):
        slot = slot_ref[k]
        tile = slot >> 1
        second = (slot & 1) > 0
        shift = 2 * (slot & 1)
        upper = (narrow - shift) & 3
        lower = (narrow - shift - 1) & 3
        for part in range(2):
            top = jnp.zeros((SIDE // 2, LANES), F32)
            low = top
            for i in range(4):
                piece = got_ref[8 * (4 * part + i) + tile, ENDS : 2 * ENDS, :].astype(F32)
                top = jnp.where(upper == i, piece, top)
                low = jnp.where(lower == i, piece, low)
            top = jnp.where(second, turn(top, 2), top)
            low = jnp.where(second, turn(low, 1), turn(low, 3))
            patches.append(jnp.concatenate([top, low], axis=0).astype(BF16))
    patch = jnp.concatenate(patches, axis=1)
    a = dot(rows_ref[...], jnp.concatenate([patch, patch, patch], axis=0), (1, 0))
    mixed = []
    for k in range(SUBS):
        re = a[:, 2 * k * LANES : (2 * k + 1) * LANES]
        im = a[:, (2 * k + 1) * LANES : (2 * k + 2) * LANES]
        mixed += [re[:SIDE] - im[SIDE:], im[:SIDE] + re[SIDE:]]
    hi, lo = split(jnp.concatenate(mixed, axis=0))
    images = dot(jnp.concatenate([hi, lo, hi], axis=1), cols_ref[...], (1, 0))

    for k in range(SUBS):
        b = images[2 * k * SIDE : 2 * (k + 1) * SIDE]
        i_re = b[:SIDE, :LANES] - b[SIDE:, LANES:]
        i_im = b[:SIDE, LANES:] + b[SIDE:, :LANES]

        sides = []
        for half in range(2):
            g = beam_ref[pl.ds(k + SUBS * half, SIDE, stride=2 * SUBS), :]
            g1, g2 = turn(g, 1), turn(g, 2)
            sides.append((jnp.where(lane == 0, g, jnp.where(lane == 3, g2, g1)), jnp.where(lane < 2, g2, g)))
        (p_re, q_re), (p_im, q_im) = sides

        y_re = i_re * q_re + i_im * q_im
        y_im = i_im * q_re - i_re * q_im
        z_re = (p_re * y_re - p_im * y_im) * taper
        z_im = (p_re * y_im + p_im * y_re) * taper
        for i, part in enumerate((i_re, i_im, p_re, p_im, y_re, y_im)):
            side_ref[k, i] = part * taper if i > 3 else part
        z = jnp.concatenate(
            [jnp.concatenate([z_re, z_im], axis=1), jnp.concatenate([-z_im, z_re], axis=1)], axis=0
        )
        z_hi, z_lo = split(z)
        z_ref[k] = jnp.concatenate([z_hi, z_lo, z_hi], axis=0)

    for copy in copies:
        copy.wait()

    def one(k, carry):
        row_wave = row_wave_ref[k]
        ev_re = column_wave_ref[k, :SIDE, :]
        ev_im = column_wave_ref[k, SIDE:, :]
        w = dot(z_ref[k], jnp.concatenate([row_wave[: 2 * SIDE], row_wave], axis=0), (0, 0))
        reals, imags = [], []
        for pol in range(4):
            w_re = w[pol * SIDE : (pol + 1) * SIDE]
            w_im = w[LANES + pol * SIDE : LANES + (pol + 1) * SIDE]
            reals.append(jnp.sum(w_re * ev_re - w_im * ev_im, axis=0, keepdims=True))
            imags.append(jnp.sum(w_re * ev_im + w_im * ev_re, axis=0, keepdims=True))
        model = jnp.concatenate(reals + imags, axis=0)
        used = flag_ref[pl.ds(k, 1), :].astype(F32)
        res = used * (seen_ref[k] - model)
        res_ref[k] = res
        back = -used * res

        t_re, t_im = [], []
        for pol in range(4):
            d_re = back[pol : pol + 1]
            d_im = back[4 + pol : 5 + pol]
            t_re.append(ev_re * d_re + ev_im * d_im)
            t_im.append(ev_re * d_im - ev_im * d_re)
        t_hi, t_lo = split(jnp.concatenate(t_re + t_im, axis=0))
        held_ref[k, 0] = t_hi
        held_ref[k, 1] = t_lo
        return carry

    def two(k, carry):
        row_wave = row_wave_ref[k]
        t_hi = held_ref[k, 0]
        t_lo = held_ref[k, 1]
        both = dot(row_wave, t_hi, (1, 1))
        dz_ref[k] = both[: 2 * SIDE] + both[2 * SIDE :] + dot(row_wave[: 2 * SIDE], t_lo, (1, 1))
        return carry

    for k in range(SUBS + 1):
        if k < SUBS:
            one(k, 0)
        if k > 0:
            two(k - 1, 0)

    for k in range(SUBS):
        d = dz_ref[k]
        i_re, i_im, p_re, p_im, y_re, y_im = (side_ref[k, i] for i in range(6))
        dz_re = d[:SIDE, :LANES] + d[SIDE:, LANES:]
        dz_im = d[:SIDE, LANES:] - d[SIDE:, :LANES]

        dp_re = dz_re * y_re + dz_im * y_im
        dp_im = dz_im * y_re - dz_re * y_im
        dp_re = dp_re + turn(dp_re, 3)
        dp_im = dp_im + turn(dp_im, 3)
        i_re = i_re * taper
        i_im = i_im * taper
        dy_re = dz_re * p_re + dz_im * p_im
        dy_im = dz_im * p_re - dz_re * p_im
        dq_re = dy_re * i_re + dy_im * i_im
        dq_im = dy_re * i_im - dy_im * i_re
        dq_re = dq_re + turn(dq_re, 2)
        dq_im = dq_im + turn(dq_im, 2)
        for half, (dp, dq) in enumerate(((dp_re, dq_re), (dp_im, dq_im))):
            grad = jnp.where(lane == 0, dp, jnp.where(lane == 1, turn(dp, 3), dq))
            grad_ref[pl.ds(k + SUBS * half, SIDE, stride=2 * SUBS), :] = grad
    out_ref[...] = grad_ref[0:TABLE, :]


SMEM = pl.BlockSpec(memory_space=pltpu.SMEM)
VMEM = pl.BlockSpec(memory_space=pltpu.VMEM)
HBM = pl.BlockSpec(memory_space=pltpu.HBM)
PARAMS = pltpu.CompilerParams(vmem_limit_bytes=40 * 1024 * 1024)


def call(kernel, shapes, specs, out_specs, scratch=(), aliases=None):
    return pl.pallas_call(
        kernel,
        out_shape=shapes,
        in_specs=specs,
        out_specs=out_specs,
        scratch_shapes=list(scratch),
        input_output_aliases=aliases or {},
        compiler_params=PARAMS,
    )


def shape(dims, dtype=F32):
    return jax.ShapeDtypeStruct(dims, dtype)


def cut(place, wanted, grid):
    return pl.pallas_call(
        cut_kernel,
        out_shape=shape((PEERS, 2 * ENDS, LANES), BF16),
        grid_spec=pltpu.PrefetchScalarGridSpec(
            num_scalar_prefetch=2,
            grid=(1,),
            in_specs=[pl.BlockSpec((1, grid.shape[1], LANES), lambda i, place, wanted: (place[1], 0, 0))],
            out_specs=HBM,
            scratch_shapes=[
                pltpu.VMEM((grid.shape[1], LANES), F32),
                pltpu.VMEM((PEERS, ENDS, LANES), BF16),
                pltpu.SemaphoreType.DMA,
            ],
        ),
        compiler_params=PARAMS,
    )(place, wanted, grid)


def in_hbm(x):
    return pltpu.with_memory_space_constraint(x, pltpu.HBM)


def exchange(x, axes):
    return lax.all_to_all(x, axes, split_axis=0, concat_axis=0, tiled=True)


def main(slot, got, row_waves, column_waves, *rest):
    waves = [pltpu.with_memory_space_constraint(x, pltpu.VMEM) for x in (row_waves, column_waves)]
    tables = [jnp.asarray(t) for t in dft_tables()]
    return call(
        main_kernel,
        (shape((SUBS, 8, VIS)), shape((TABLE, LANES))),
        [SMEM] + [VMEM] * 3 + [HBM] * 2 + [VMEM] * 3,
        (VMEM, VMEM),
        [
            pltpu.VMEM((TABLE + 2 * SUBS, LANES), F32),
            pltpu.VMEM((TABLE + 2 * SUBS, LANES), F32),
            pltpu.VMEM((SUBS, 8, VIS), F32),
            pltpu.VMEM((SUBS, VIS), S32),
            pltpu.VMEM((SUBS, 6, SIDE, LANES), F32),
            pltpu.VMEM((SUBS, 6 * SIDE, 2 * LANES), BF16),
            pltpu.VMEM((SUBS, 2 * SIDE, 2 * LANES), F32),
            pltpu.VMEM((SUBS, 2, 2 * LANES, VIS), BF16),
            pltpu.SemaphoreType.DMA((4,)),
        ],
    )(slot, got, *waves, *(in_hbm(x) for x in rest), *tables)


ACROSS = ("z", "tile")
NEAR = ("x", "core")


def body(grid, a_terms, stations, intervals, offsets, uv, observed, flags):
    place = jnp.stack([lax.axis_index(name).astype(S32) for name in ("tile", "z")])
    offsets = offsets.T
    sent = call(
        prep_kernel,
        shape((PEERS, 2, LANES)),
        [HBM] * 4,
        VMEM,
        [
            pltpu.SMEM((2, SUBS), S32),
            pltpu.SMEM((SUBS,), S32),
            pltpu.SMEM((2, SUBS), S32),
            pltpu.VMEM((2, 4, SIDE * SIDE), F32),
            pltpu.SemaphoreType.DMA((4,)),
        ],
    )(*(in_hbm(x) for x in (stations.T, intervals, offsets, a_terms)))
    got_a = exchange(sent, ACROSS)
    spread = call(
        spread_kernel,
        shape((GROUPS, ROWS, LANES)),
        [VMEM],
        HBM,
        [pltpu.VMEM((ROWS, LANES), F32), pltpu.SemaphoreType.DMA((GROUPS,))],
    )(got_a)
    table = exchange(spread, NEAR).reshape(TABLE, LANES)

    wanted = got_a[:, 1, :].astype(S32)
    first = wanted[:, :SUBS].reshape(TABLE)
    second = wanted[:, SUBS:ENDS].reshape(TABLE)
    columns = (first[:, None], second[:, None])
    patches = cut(place, wanted[:, ENDS : ENDS + SLOTS], grid)
    waves = call(
        wave_kernel, (shape((SUBS, 4 * SIDE, VIS), BF16), shape((SUBS, 2 * SIDE, VIS))), [VMEM], (VMEM, VMEM)
    )(uv)

    found = call(
        gather_kernel,
        shape((PEERS, 2 * ENDS, LANES), BF16),
        [VMEM] * 3 + [HBM],
        HBM,
        [pltpu.VMEM((PEERS, ENDS, LANES), BF16), pltpu.SemaphoreType.DMA],
        {3: 0},
    )(table, *columns, patches)
    got_c = exchange(found, ACROSS)

    owner = offsets[0] >> 8
    same = owner[:, None] == owner[None, :]
    earlier = jnp.arange(SUBS)[:, None] > jnp.arange(SUBS)[None, :]
    slot = owner * 2 + jnp.sum((same & earlier).astype(S32), axis=1)
    result, grads = main(slot, got_c, *waves, observed, flags)

    back_c = exchange(grads.reshape(PEERS, SUBS, LANES), ACROSS).reshape(TABLE, LANES)
    dense = call(scatter_kernel, shape((TABLE, LANES)), [VMEM] * 5, VMEM)(
        back_c, *columns, first[None, :], second[None, :]
    )
    back_b = exchange(dense.reshape(GROUPS, ROWS, LANES), NEAR)
    summed = call(add_kernel, shape((PEERS, SUBS, LANES)), [VMEM], VMEM)(back_b)
    back_a = exchange(summed, ACROSS)
    total = call(
        place_kernel,
        shape((SUBS, 2, 4, SIDE * SIDE)),
        [VMEM],
        HBM,
        [pltpu.VMEM((SUBS, 2, 4, SIDE * SIDE), F32), pltpu.SemaphoreType.DMA((8,))],
    )(back_a)
    return (result, total)


def solution(mesh):
    fine = Mesh(mesh.devices.reshape(8, 4, 2, 8), ("z", "x", "core", "tile"))
    st = ("z", "x", "core")
    every = ("z", "x", "core", "tile")
    placed = (
        P(None, "tile", None),
        P(st, None, None, None),
        P(every, None),
        P(every),
        P(every, None),
        P(every, None, None),
        P(every, None, None),
        P(every, None),
    )
    return jax.shard_map(
        body,
        mesh=fine,
        in_specs=placed,
        out_specs=(P(every, None, None), P(st, None, None, None)),
        check_vma=False,
    )
```

```python
import jax
import jax.numpy as jnp
import numpy as np
from jax import lax
from jax.experimental import pallas as pl
from jax.experimental.pallas import tpu as pltpu
from jax.sharding import Mesh
from jax.sharding import PartitionSpec as P

SIDE = 32
SUBS = 8
ENDS = 2 * SUBS
VIS = 512
PEERS = 64
GROUPS = 8
ROWS = 64
TABLE = GROUPS * ROWS
LANES = 128
SLOTS = 16

F32 = jnp.float32
BF16 = jnp.bfloat16
S32 = jnp.int32


def bf16_parts(array, count):
    rest = np.asarray(array, np.float64)
    parts = []
    for _ in range(count):
        part = rest.astype(np.float32).astype(jnp.bfloat16)
        parts.append(part)
        rest = rest - part.astype(np.float64)
    return parts


def dft_tables():
    index = np.arange(SIDE)
    angle = 2.0 * np.pi * (index[:, None] * index[None, :] % SIDE) / SIDE
    f_real = np.cos(angle) / SIDE
    f_imag = np.sin(angle) / SIDE
    rows = np.concatenate([f_real, f_imag], axis=0)
    rows_parts = np.concatenate(bf16_parts(rows, 3), axis=1)
    eye = np.eye(4)
    cols = np.concatenate([np.kron(eye, f_real.T), np.kron(eye, f_imag.T)], axis=1)
    hi, lo = bf16_parts(cols, 2)
    cols_parts = np.concatenate([hi, hi, lo], axis=0)
    edge = np.cos(np.pi * (index - (SIDE - 1) / 2.0) / SIDE)
    taper = np.tile(edge[:, None] * edge[None, :], (1, 4)).astype(np.float32)
    return rows_parts, cols_parts, taper


def turn_polynomials():
    nodes = 0.25 * np.cos(np.pi * (np.arange(400) + 0.5) / 400) ** 2
    r = np.sqrt(nodes)
    scaled = nodes * 4.0
    sine = np.polynomial.polynomial.polyfit(scaled, np.sin(2 * np.pi * r) / r, 7)
    cosine = np.polynomial.polynomial.polyfit(scaled, np.cos(2 * np.pi * r), 8)
    power = 4.0 ** np.arange(9)
    return [float(a) for a in sine * power[:8]], [float(a) for a in cosine * power]


SINE, COSINE = turn_polynomials()


def unit_circle(turns):
    r = turns - jnp.floor(turns + 0.5)
    r2 = r * r
    s = jnp.full_like(r, SINE[-1])
    for a in SINE[-2::-1]:
        s = s * r2 + a
    c = jnp.full_like(r, COSINE[-1])
    for a in COSINE[-2::-1]:
        c = c * r2 + a
    return c, s * r


def split(x):
    hi = x.astype(BF16)
    return hi, (x - hi.astype(F32)).astype(BF16)


def dot(a, b, contract):
    return lax.dot_general(a, b, ((contract[:1], contract[1:]), ((), ())), preferred_element_type=F32)


def slots(offsets_ref):
    tiles = [offsets_ref[0, k] >> 8 for k in range(SUBS)]
    seconds = []
    for k in range(SUBS):
        second = jnp.zeros((), S32)
        for j in range(k):
            second = jnp.where(tiles[j] == tiles[k], 1, second)
        seconds.append(second)
    return tiles, seconds


def prep_kernel(
    stations_in, intervals_in, offsets_in, terms_in, out_ref, stations_ref, intervals_ref, offsets_ref, terms_ref, sems
):
    own = lax.axis_index("tile")
    copies = [
        pltpu.make_async_copy(stations_in, stations_ref, sems.at[0]),
        pltpu.make_async_copy(intervals_in, intervals_ref, sems.at[1]),
        pltpu.make_async_copy(offsets_in, offsets_ref, sems.at[2]),
        pltpu.make_async_copy(terms_in.at[own], terms_ref, sems.at[3]),
    ]
    for copy in copies:
        copy.start()
    for copy in copies:
        copy.wait()
    spot = lax.broadcasted_iota(S32, (1, LANES), 1)
    asked = jnp.zeros((1, LANES), S32)
    tiles, seconds = slots(offsets_ref)
    for k in range(SUBS):
        for end in range(2):
            station = stations_ref[end, k]
            row = ((station >> 3) & 7) * ROWS + (station >> 6) * 8 + (station & 7)
            asked = jnp.where(spot == end * SUBS + k, row + TABLE * intervals_ref[k], asked)
        code = (offsets_ref[0, k] & 255) * LANES + offsets_ref[1, k]
        asked = jnp.where(spot == ENDS + 2 * tiles[k] + seconds[k], code, asked)
    out_ref[:, 1:2, :] = jnp.broadcast_to(asked.astype(F32).reshape(1, 1, LANES), (PEERS, 1, LANES))
    lane = spot // SIDE
    for block in range(8):
        turned = []
        for interval in range(2):
            comps = terms_ref[interval, :, block * LANES : (block + 1) * LANES]
            turned.append([comps if d == 0 else pltpu.roll(comps, d * SIDE, 1) for d in range(4)])
        for i in range(4):
            for half in range(2):
                total = jnp.zeros((1, LANES), F32)
                for place in range(4):
                    comp = 2 * half + (place & 1)
                    piece = turned[place >> 1][(place - i) % 4][comp : comp + 1, :]
                    total = piece if place == 0 else jnp.where(lane == place, piece, total)
                out_ref[(4 * block + i) * 2 + half, 0:1, :] = total


def wave_kernel(uv_ref, row_wave_ref, column_wave_ref):
    centre = (lax.broadcasted_iota(S32, (SIDE, VIS), 0).astype(F32) - SIDE / 2.0) * (1.0 / SIDE)

    def one(k, carry):
        real, imag = unit_circle(uv_ref[k, 0:1, :] * centre)
        hi, lo = split(jnp.concatenate([real, imag], axis=0))
        row_wave_ref[k] = jnp.concatenate([hi, lo], axis=0)
        real, imag = unit_circle(uv_ref[k, 1:2, :] * centre)
        column_wave_ref[k] = jnp.concatenate([real, imag], axis=0)
        return carry

    lax.fori_loop(0, SUBS, one, 0)


def cut_kernel(place_ref, wanted_ref, strip_ref, out_hbm, wide_ref, out_ref, sem):
    wide_ref[...] = strip_ref[0].astype(F32)
    tile = place_ref[0]
    part_of = place_ref[1]
    half = SIDE // 2
    lane = lax.broadcasted_iota(S32, (half, LANES), 1) // SIDE

    def one(i, carry):
        total = jnp.zeros((half, LANES), F32)
        for slot in range(2):
            code = wanted_ref[i, 2 * tile + slot]
            row = code >> 7
            column = code & (LANES - 1)
            for part in range(2):
                spot = (part_of + 2 * slot + part) & 3
                piece = wide_ref[pl.ds(row + half * part, half), :]
                piece = pltpu.roll(piece, (spot * SIDE + LANES - column) & (LANES - 1), 1)
                total = jnp.where(lane == spot, piece, total)
        out_ref[i] = total.astype(BF16)
        return carry

    lax.fori_loop(0, PEERS, one, 0, unroll=8)
    copy = pltpu.make_async_copy(out_ref, out_hbm.at[:, pl.ds(ENDS, ENDS), :], sem)
    copy.start()
    copy.wait()


def spread_kernel(got_ref, out_hbm, part_ref, sems):
    part_ref[...] = got_ref[:, 0:1, :].reshape(ROWS, LANES)
    copies = [pltpu.make_async_copy(part_ref, out_hbm.at[i], sems.at[i]) for i in range(GROUPS)]
    for copy in copies:
        copy.start()
    for copy in copies:
        copy.wait()


def gather_kernel(table_ref, first_ref, second_ref, patched_hbm, out_hbm, out_ref, sem):
    hi, lo = split(table_ref[...])
    table = jnp.concatenate([hi, lo], axis=1)
    ids = lax.broadcasted_iota(S32, (TABLE, TABLE), 1)
    left = lax.broadcasted_iota(S32, (TABLE, LANES), 1) < LANES // 2
    sides = []
    for code_ref in (first_ref, second_ref):
        code = code_ref[...]
        chosen = jnp.where(ids == (code & (TABLE - 1)), 1.0, 0.0).astype(BF16)
        found = dot(chosen, table, (1, 0))
        found = found[:, :LANES] + found[:, LANES:]
        sides.append((found, pltpu.roll(found, LANES // 2, 1), code >= TABLE))
    first = jnp.where(sides[0][2], sides[0][1], sides[0][0])
    second = jnp.where(sides[1][2], sides[1][0], sides[1][1])
    beams = jnp.where(left, first, second)
    hi = beams.astype(BF16).astype(F32)
    both = jnp.concatenate([hi.reshape(PEERS, SUBS, LANES), (beams - hi).reshape(PEERS, SUBS, LANES)], axis=1)
    out_ref[...] = both.astype(BF16)
    copy = pltpu.make_async_copy(out_ref, out_hbm.at[:, pl.ds(0, ENDS), :], sem)
    copy.start()
    copy.wait()


def scatter_kernel(got_ref, first_ref, second_ref, first_row_ref, second_row_ref, out_ref):
    got = got_ref[...]
    turned = pltpu.roll(got, LANES // 2, 1)
    left = lax.broadcasted_iota(S32, (TABLE, LANES), 1) < LANES // 2
    ids = lax.broadcasted_iota(S32, (TABLE, TABLE), 0)
    values, chosen = [], []
    for spread, code_ref, row_ref in (
        (jnp.where(left, got, turned), first_ref, first_row_ref),
        (jnp.where(left, turned, got), second_ref, second_row_ref),
    ):
        late = code_ref[...] >= TABLE
        values.append(jnp.where(late != left, spread, 0.0))
        chosen.append(jnp.where(ids == (row_ref[...] & (TABLE - 1)), 1.0, 0.0).astype(BF16))
    hi, lo = split(jnp.concatenate(values, axis=0))
    total = dot(jnp.concatenate(chosen, axis=1), jnp.concatenate([hi, lo], axis=1), (1, 0))
    out_ref[...] = total[:, :LANES] + total[:, LANES:]


def add_kernel(parts_ref, out_ref):
    total = parts_ref[0]
    for i in range(1, GROUPS):
        total = total + parts_ref[i]
    for i in range(PEERS):
        part = i // 8
        out_ref[i] = total[part * SUBS : (part + 1) * SUBS, :]


def place_kernel(parts_ref, out_hbm, out_ref, sems):
    copies = []
    lane = lax.broadcasted_iota(S32, (SUBS, LANES), 1) // SIDE
    for block in range(8):
        for half in range(2):
            rows = [parts_ref[2 * (4 * block + i) + half] for i in range(4)]
            turned = [[rows[i] if d == 0 else pltpu.roll(rows[i], d * SIDE, 1) for d in range(4)] for i in range(4)]
            for interval in range(2):
                for part in range(2):
                    at = 2 * interval + part
                    total = turned[0][(0 - at) % 4]
                    for i in range(1, 4):
                        total = jnp.where(lane == i, turned[i][(i - at) % 4], total)
                    out_ref[:, interval, 2 * half + part, block * LANES : (block + 1) * LANES] = total
        lanes = pl.ds(block * LANES, LANES)
        copies.append(
            pltpu.make_async_copy(out_ref.at[:, :, :, lanes], out_hbm.at[:, :, :, lanes], sems.at[block])
        )
        copies[-1].start()
    for copy in copies:
        copy.wait()


def main_kernel(
    slot_ref, got_ref, row_wave_ref, column_wave_ref, seen_in, flag_in, rows_ref, cols_ref, taper_ref,
    res_out, out_ref, res_ref, grad_ref, beam_ref, seen_ref, flag_ref, side_ref, z_ref, dz_ref, held_ref, sems,
):
    copies = [
        pltpu.make_async_copy(a, b, sems.at[i])
        for i, (a, b) in enumerate(
            ((seen_in, seen_ref), (flag_in, flag_ref))
        )
    ]
    for copy in copies:
        copy.start()
    got = got_ref[:, 0:ENDS, :].astype(F32)
    beam_ref[0:TABLE, :] = (got[:, :SUBS] + got[:, SUBS:]).reshape(TABLE, LANES)
    narrow = lax.broadcasted_iota(S32, (SIDE // 2, LANES), 1) // SIDE
    lane = lax.broadcasted_iota(S32, (SIDE, LANES), 1) // SIDE
    taper = taper_ref[...]

    def turn(x, blocks):
        return pltpu.roll(x, blocks * SIDE, 1)

    patches = []
    for k in range(SUBS):
        slot = slot_ref[k]
        tile = slot >> 1
        second = (slot & 1) > 0
        shift = 2 * (slot & 1)
        upper = (narrow - shift) & 3
        lower = (narrow - shift - 1) & 3
        for part in range(2):
            top = jnp.zeros((SIDE // 2, LANES), F32)
            low = top
            for i in range(4):
                piece = got_ref[8 * (4 * part + i) + tile, ENDS : 2 * ENDS, :].astype(F32)
                top = jnp.where(upper == i, piece, top)
                low = jnp.where(lower == i, piece, low)
            top = jnp.where(second, turn(top, 2), top)
            low = jnp.where(second, turn(low, 1), turn(low, 3))
            patches.append(jnp.concatenate([top, low], axis=0).astype(BF16))
    patch = jnp.concatenate(patches, axis=1)
    a = dot(rows_ref[...], jnp.concatenate([patch, patch, patch], axis=0), (1, 0))
    mixed = []
    for k in range(SUBS):
        re = a[:, 2 * k * LANES : (2 * k + 1) * LANES]
        im = a[:, (2 * k + 1) * LANES : (2 * k + 2) * LANES]
        mixed += [re[:SIDE] - im[SIDE:], im[:SIDE] + re[SIDE:]]
    hi, lo = split(jnp.concatenate(mixed, axis=0))
    images = dot(jnp.concatenate([hi, lo, hi], axis=1), cols_ref[...], (1, 0))

    for k in range(SUBS):
        b = images[2 * k * SIDE : 2 * (k + 1) * SIDE]
        i_re = b[:SIDE, :LANES] - b[SIDE:, LANES:]
        i_im = b[:SIDE, LANES:] + b[SIDE:, :LANES]

        sides = []
        for half in range(2):
            g = beam_ref[pl.ds(k + SUBS * half, SIDE, stride=2 * SUBS), :]
            g1, g2 = turn(g, 1), turn(g, 2)
            sides.append((jnp.where(lane == 0, g, jnp.where(lane == 3, g2, g1)), jnp.where(lane < 2, g2, g)))
        (p_re, q_re), (p_im, q_im) = sides

        y_re = i_re * q_re + i_im * q_im
        y_im = i_im * q_re - i_re * q_im
        z_re = (p_re * y_re - p_im * y_im) * taper
        z_im = (p_re * y_im + p_im * y_re) * taper
        for i, part in enumerate((i_re, i_im, p_re, p_im, y_re, y_im)):
            side_ref[k, i] = part * taper if i > 3 else part
        z = jnp.concatenate(
            [jnp.concatenate([z_re, z_im], axis=1), jnp.concatenate([-z_im, z_re], axis=1)], axis=0
        )
        z_hi, z_lo = split(z)
        z_ref[k] = jnp.concatenate([z_hi, z_lo, z_hi], axis=0)

    for copy in copies:
        copy.wait()

    def one(k, carry):
        row_wave = row_wave_ref[k]
        ev_re = column_wave_ref[k, :SIDE, :]
        ev_im = column_wave_ref[k, SIDE:, :]
        w = dot(z_ref[k], jnp.concatenate([row_wave[: 2 * SIDE], row_wave], axis=0), (0, 0))
        reals, imags = [], []
        for pol in range(4):
            w_re = w[pol * SIDE : (pol + 1) * SIDE]
            w_im = w[LANES + pol * SIDE : LANES + (pol + 1) * SIDE]
            reals.append(jnp.sum(w_re * ev_re - w_im * ev_im, axis=0, keepdims=True))
            imags.append(jnp.sum(w_re * ev_im + w_im * ev_re, axis=0, keepdims=True))
        model = jnp.concatenate(reals + imags, axis=0)
        used = flag_ref[pl.ds(k, 1), :].astype(F32)
        res = used * (seen_ref[k] - model)
        res_ref[k] = res
        back = -used * res

        t_re, t_im = [], []
        for pol in range(4):
            d_re = back[pol : pol + 1]
            d_im = back[4 + pol : 5 + pol]
            t_re.append(ev_re * d_re + ev_im * d_im)
            t_im.append(ev_re * d_im - ev_im * d_re)
        t_hi, t_lo = split(jnp.concatenate(t_re + t_im, axis=0))
        held_ref[k, 0] = t_hi
        held_ref[k, 1] = t_lo
        return carry

    def two(k, carry):
        row_wave = row_wave_ref[k]
        t_hi = held_ref[k, 0]
        t_lo = held_ref[k, 1]
        both = dot(row_wave, t_hi, (1, 1))
        dz_ref[k] = both[: 2 * SIDE] + both[2 * SIDE :] + dot(row_wave[: 2 * SIDE], t_lo, (1, 1))
        return carry

    for k in range(SUBS + 1):
        if k < SUBS:
            one(k, 0)
        if k > 0:
            two(k - 1, 0)
    sent = pltpu.make_async_copy(res_ref, res_out, sems.at[2])
    sent.start()

    for k in range(SUBS):
        d = dz_ref[k]
        i_re, i_im, p_re, p_im, y_re, y_im = (side_ref[k, i] for i in range(6))
        dz_re = d[:SIDE, :LANES] + d[SIDE:, LANES:]
        dz_im = d[:SIDE, LANES:] - d[SIDE:, :LANES]

        dp_re = dz_re * y_re + dz_im * y_im
        dp_im = dz_im * y_re - dz_re * y_im
        dp_re = dp_re + turn(dp_re, 3)
        dp_im = dp_im + turn(dp_im, 3)
        i_re = i_re * taper
        i_im = i_im * taper
        dy_re = dz_re * p_re + dz_im * p_im
        dy_im = dz_im * p_re - dz_re * p_im
        dq_re = dy_re * i_re + dy_im * i_im
        dq_im = dy_re * i_im - dy_im * i_re
        dq_re = dq_re + turn(dq_re, 2)
        dq_im = dq_im + turn(dq_im, 2)
        for half, (dp, dq) in enumerate(((dp_re, dq_re), (dp_im, dq_im))):
            grad = jnp.where(lane == 0, dp, jnp.where(lane == 1, turn(dp, 3), dq))
            grad_ref[pl.ds(k + SUBS * half, SIDE, stride=2 * SUBS), :] = grad
    out_ref[...] = grad_ref[0:TABLE, :]
    sent.wait()


SMEM = pl.BlockSpec(memory_space=pltpu.SMEM)
VMEM = pl.BlockSpec(memory_space=pltpu.VMEM)
HBM = pl.BlockSpec(memory_space=pltpu.HBM)
PARAMS = pltpu.CompilerParams(vmem_limit_bytes=40 * 1024 * 1024)


def call(kernel, shapes, specs, out_specs, scratch=(), aliases=None):
    return pl.pallas_call(
        kernel,
        out_shape=shapes,
        in_specs=specs,
        out_specs=out_specs,
        scratch_shapes=list(scratch),
        input_output_aliases=aliases or {},
        compiler_params=PARAMS,
    )


def shape(dims, dtype=F32):
    return jax.ShapeDtypeStruct(dims, dtype)


def cut(place, wanted, grid):
    return pl.pallas_call(
        cut_kernel,
        out_shape=shape((PEERS, 2 * ENDS, LANES), BF16),
        grid_spec=pltpu.PrefetchScalarGridSpec(
            num_scalar_prefetch=2,
            grid=(1,),
            in_specs=[pl.BlockSpec((1, grid.shape[1], LANES), lambda i, place, wanted: (place[1], 0, 0))],
            out_specs=HBM,
            scratch_shapes=[
                pltpu.VMEM((grid.shape[1], LANES), F32),
                pltpu.VMEM((PEERS, ENDS, LANES), BF16),
                pltpu.SemaphoreType.DMA,
            ],
        ),
        compiler_params=PARAMS,
    )(place, wanted, grid)


def in_hbm(x):
    return pltpu.with_memory_space_constraint(x, pltpu.HBM)


def exchange(x, axes):
    return lax.all_to_all(x, axes, split_axis=0, concat_axis=0, tiled=True)


def main(slot, got, row_waves, column_waves, *rest):
    waves = [pltpu.with_memory_space_constraint(x, pltpu.VMEM) for x in (row_waves, column_waves)]
    tables = [jnp.asarray(t) for t in dft_tables()]
    return call(
        main_kernel,
        (shape((SUBS, 8, VIS)), shape((TABLE, LANES))),
        [SMEM] + [VMEM] * 3 + [HBM] * 2 + [VMEM] * 3,
        (HBM, VMEM),
        [
            pltpu.VMEM((SUBS, 8, VIS), F32),
            pltpu.VMEM((TABLE + 2 * SUBS, LANES), F32),
            pltpu.VMEM((TABLE + 2 * SUBS, LANES), F32),
            pltpu.VMEM((SUBS, 8, VIS), F32),
            pltpu.VMEM((SUBS, VIS), S32),
            pltpu.VMEM((SUBS, 6, SIDE, LANES), F32),
            pltpu.VMEM((SUBS, 6 * SIDE, 2 * LANES), BF16),
            pltpu.VMEM((SUBS, 2 * SIDE, 2 * LANES), F32),
            pltpu.VMEM((SUBS, 2, 2 * LANES, VIS), BF16),
            pltpu.SemaphoreType.DMA((4,)),
        ],
    )(slot, got, *waves, *(in_hbm(x) for x in rest), *tables)


ACROSS = ("z", "tile")
NEAR = ("x", "core")


def body(grid, a_terms, stations, intervals, offsets, uv, observed, flags):
    place = jnp.stack([lax.axis_index(name).astype(S32) for name in ("tile", "z")])
    offsets = offsets.T
    sent = call(
        prep_kernel,
        shape((PEERS, 2, LANES)),
        [HBM] * 4,
        VMEM,
        [
            pltpu.SMEM((2, SUBS), S32),
            pltpu.SMEM((SUBS,), S32),
            pltpu.SMEM((2, SUBS), S32),
            pltpu.VMEM((2, 4, SIDE * SIDE), F32),
            pltpu.SemaphoreType.DMA((4,)),
        ],
    )(*(in_hbm(x) for x in (stations.T, intervals, offsets, a_terms)))
    got_a = exchange(sent, ACROSS)
    spread = call(
        spread_kernel,
        shape((GROUPS, ROWS, LANES)),
        [VMEM],
        HBM,
        [pltpu.VMEM((ROWS, LANES), F32), pltpu.SemaphoreType.DMA((GROUPS,))],
    )(got_a)
    table = exchange(spread, NEAR).reshape(TABLE, LANES)

    wanted = got_a[:, 1, :].astype(S32)
    first = wanted[:, :SUBS].reshape(TABLE)
    second = wanted[:, SUBS:ENDS].reshape(TABLE)
    columns = (first[:, None], second[:, None])
    patches = cut(place, wanted[:, ENDS : ENDS + SLOTS], grid)
    waves = call(
        wave_kernel, (shape((SUBS, 4 * SIDE, VIS), BF16), shape((SUBS, 2 * SIDE, VIS))), [VMEM], (VMEM, VMEM)
    )(uv)

    found = call(
        gather_kernel,
        shape((PEERS, 2 * ENDS, LANES), BF16),
        [VMEM] * 3 + [HBM],
        HBM,
        [pltpu.VMEM((PEERS, ENDS, LANES), BF16), pltpu.SemaphoreType.DMA],
        {3: 0},
    )(table, *columns, patches)
    got_c = exchange(found, ACROSS)

    owner = offsets[0] >> 8
    same = owner[:, None] == owner[None, :]
    earlier = jnp.arange(SUBS)[:, None] > jnp.arange(SUBS)[None, :]
    slot = owner * 2 + jnp.sum((same & earlier).astype(S32), axis=1)
    result, grads = main(slot, got_c, *waves, observed, flags)

    back_c = exchange(grads.reshape(PEERS, SUBS, LANES), ACROSS).reshape(TABLE, LANES)
    dense = call(scatter_kernel, shape((TABLE, LANES)), [VMEM] * 5, VMEM)(
        back_c, *columns, first[None, :], second[None, :]
    )
    back_b = exchange(dense.reshape(GROUPS, ROWS, LANES), NEAR)
    summed = call(add_kernel, shape((PEERS, SUBS, LANES)), [VMEM], VMEM)(back_b)
    back_a = exchange(summed, ACROSS)
    total = call(
        place_kernel,
        shape((SUBS, 2, 4, SIDE * SIDE)),
        [VMEM],
        HBM,
        [pltpu.VMEM((SUBS, 2, 4, SIDE * SIDE), F32), pltpu.SemaphoreType.DMA((8,))],
    )(back_a)
    return (result, total)


def solution(mesh):
    fine = Mesh(mesh.devices.reshape(8, 4, 2, 8), ("z", "x", "core", "tile"))
    st = ("z", "x", "core")
    every = ("z", "x", "core", "tile")
    placed = (
        P(None, "tile", None),
        P(st, None, None, None),
        P(every, None),
        P(every),
        P(every, None),
        P(every, None, None),
        P(every, None, None),
        P(every, None),
    )
    return jax.shard_map(
        body,
        mesh=fine,
        in_specs=placed,
        out_specs=(P(every, None, None), P(st, None, None, None)),
        check_vma=False,
    )
```

```python
import jax
import jax.numpy as jnp
import numpy as np
from jax import lax
from jax.experimental import pallas as pl
from jax.experimental.pallas import tpu as pltpu
from jax.sharding import Mesh
from jax.sharding import PartitionSpec as P

SIDE = 32
SUBS = 8
ENDS = 2 * SUBS
VIS = 512
PEERS = 64
GROUPS = 8
ROWS = 64
TABLE = GROUPS * ROWS
LANES = 128
SLOTS = 16

F32 = jnp.float32
BF16 = jnp.bfloat16
S32 = jnp.int32


def bf16_parts(array, count):
    rest = np.asarray(array, np.float64)
    parts = []
    for _ in range(count):
        part = rest.astype(np.float32).astype(jnp.bfloat16)
        parts.append(part)
        rest = rest - part.astype(np.float64)
    return parts


def dft_tables():
    index = np.arange(SIDE)
    angle = 2.0 * np.pi * (index[:, None] * index[None, :] % SIDE) / SIDE
    f_real = np.cos(angle) / SIDE
    f_imag = np.sin(angle) / SIDE
    rows = np.concatenate([f_real, f_imag], axis=0)
    rows_parts = np.concatenate(bf16_parts(rows, 3), axis=1)
    eye = np.eye(4)
    cols = np.concatenate([np.kron(eye, f_real.T), np.kron(eye, f_imag.T)], axis=1)
    hi, lo = bf16_parts(cols, 2)
    cols_parts = np.concatenate([hi, hi, lo], axis=0)
    edge = np.cos(np.pi * (index - (SIDE - 1) / 2.0) / SIDE)
    taper = np.tile(edge[:, None] * edge[None, :], (1, 4)).astype(np.float32)
    return rows_parts, cols_parts, taper


def turn_polynomials():
    nodes = 0.25 * np.cos(np.pi * (np.arange(400) + 0.5) / 400) ** 2
    r = np.sqrt(nodes)
    scaled = nodes * 4.0
    sine = np.polynomial.polynomial.polyfit(scaled, np.sin(2 * np.pi * r) / r, 7)
    cosine = np.polynomial.polynomial.polyfit(scaled, np.cos(2 * np.pi * r), 8)
    power = 4.0 ** np.arange(9)
    return [float(a) for a in sine * power[:8]], [float(a) for a in cosine * power]


SINE, COSINE = turn_polynomials()


def unit_circle(turns):
    r = turns - jnp.floor(turns + 0.5)
    r2 = r * r
    s = jnp.full_like(r, SINE[-1])
    for a in SINE[-2::-1]:
        s = s * r2 + a
    c = jnp.full_like(r, COSINE[-1])
    for a in COSINE[-2::-1]:
        c = c * r2 + a
    return c, s * r


def split(x):
    hi = x.astype(BF16)
    return hi, (x - hi.astype(F32)).astype(BF16)


def dot(a, b, contract):
    return lax.dot_general(a, b, ((contract[:1], contract[1:]), ((), ())), preferred_element_type=F32)


def slots(offsets_ref):
    tiles = [offsets_ref[0, k] >> 8 for k in range(SUBS)]
    seconds = []
    for k in range(SUBS):
        second = jnp.zeros((), S32)
        for j in range(k):
            second = jnp.where(tiles[j] == tiles[k], 1, second)
        seconds.append(second)
    return tiles, seconds


def prep_kernel(
    stations_in, intervals_in, offsets_in, terms_in, out_ref, stations_ref, intervals_ref, offsets_ref, terms_ref, sems
):
    own = lax.axis_index("tile")
    copies = [
        pltpu.make_async_copy(stations_in, stations_ref, sems.at[0]),
        pltpu.make_async_copy(intervals_in, intervals_ref, sems.at[1]),
        pltpu.make_async_copy(offsets_in, offsets_ref, sems.at[2]),
        pltpu.make_async_copy(terms_in.at[own], terms_ref, sems.at[3]),
    ]
    for copy in copies:
        copy.start()
    for copy in copies:
        copy.wait()
    spot = lax.broadcasted_iota(S32, (1, LANES), 1)
    asked = jnp.zeros((1, LANES), S32)
    tiles, seconds = slots(offsets_ref)
    for k in range(SUBS):
        for end in range(2):
            station = stations_ref[end, k]
            row = ((station >> 3) & 7) * ROWS + (station >> 6) * 8 + (station & 7)
            asked = jnp.where(spot == end * SUBS + k, row + TABLE * intervals_ref[k], asked)
        code = (offsets_ref[0, k] & 255) * LANES + offsets_ref[1, k]
        asked = jnp.where(spot == ENDS + 2 * tiles[k] + seconds[k], code, asked)
    out_ref[:, 1:2, :] = jnp.broadcast_to(asked.astype(F32).reshape(1, 1, LANES), (PEERS, 1, LANES))
    lane = spot // SIDE
    for block in range(8):
        turned = []
        for interval in range(2):
            comps = terms_ref[interval, :, block * LANES : (block + 1) * LANES]
            turned.append([comps if d == 0 else pltpu.roll(comps, d * SIDE, 1) for d in range(4)])
        for i in range(4):
            for half in range(2):
                total = jnp.zeros((1, LANES), F32)
                for place in range(4):
                    comp = 2 * half + (place & 1)
                    piece = turned[place >> 1][(place - i) % 4][comp : comp + 1, :]
                    total = piece if place == 0 else jnp.where(lane == place, piece, total)
                out_ref[(4 * block + i) * 2 + half, 0:1, :] = total


def wave_kernel(uv_ref, row_wave_ref, column_wave_ref):
    centre = (lax.broadcasted_iota(S32, (SIDE, VIS), 0).astype(F32) - SIDE / 2.0) * (1.0 / SIDE)

    def one(k, carry):
        real, imag = unit_circle(uv_ref[k, 0:1, :] * centre)
        hi, lo = split(jnp.concatenate([real, imag], axis=0))
        row_wave_ref[k] = jnp.concatenate([hi, lo], axis=0)
        real, imag = unit_circle(uv_ref[k, 1:2, :] * centre)
        column_wave_ref[k] = jnp.concatenate([real, imag], axis=0)
        return carry

    lax.fori_loop(0, SUBS, one, 0)


def cut_kernel(place_ref, wanted_ref, strip_ref, out_hbm, wide_ref, out_ref, sem):
    wide_ref[...] = strip_ref[0].astype(F32)
    tile = place_ref[0]
    part_of = place_ref[1]
    half = SIDE // 2
    lane = lax.broadcasted_iota(S32, (half, LANES), 1) // SIDE

    def one(i, carry):
        total = jnp.zeros((half, LANES), F32)
        for slot in range(2):
            code = wanted_ref[i, 2 * tile + slot]
            row = code >> 7
            column = code & (LANES - 1)
            for part in range(2):
                spot = (part_of + 2 * slot + part) & 3
                piece = wide_ref[pl.ds(row + half * part, half), :]
                piece = pltpu.roll(piece, (spot * SIDE + LANES - column) & (LANES - 1), 1)
                total = jnp.where(lane == spot, piece, total)
        out_ref[i] = total.astype(BF16)
        return carry

    lax.fori_loop(0, PEERS, one, 0, unroll=8)
    copy = pltpu.make_async_copy(out_ref, out_hbm.at[:, pl.ds(ENDS, ENDS), :], sem)
    copy.start()
    copy.wait()


def spread_kernel(got_ref, out_hbm, part_ref, sems):
    part_ref[...] = got_ref[:, 0:1, :].reshape(ROWS, LANES)
    copies = [pltpu.make_async_copy(part_ref, out_hbm.at[i], sems.at[i]) for i in range(GROUPS)]
    for copy in copies:
        copy.start()
    for copy in copies:
        copy.wait()


def gather_kernel(table_ref, first_ref, second_ref, patched_hbm, out_hbm, out_ref, sem):
    hi, lo = split(table_ref[...])
    table = jnp.concatenate([hi, lo], axis=1)
    ids = lax.broadcasted_iota(S32, (TABLE, TABLE), 1)
    left = lax.broadcasted_iota(S32, (TABLE, LANES), 1) < LANES // 2
    sides = []
    for code_ref in (first_ref, second_ref):
        code = code_ref[...]
        chosen = jnp.where(ids == (code & (TABLE - 1)), 1.0, 0.0).astype(BF16)
        found = dot(chosen, table, (1, 0))
        found = found[:, :LANES] + found[:, LANES:]
        sides.append((found, pltpu.roll(found, LANES // 2, 1), code >= TABLE))
    first = jnp.where(sides[0][2], sides[0][1], sides[0][0])
    second = jnp.where(sides[1][2], sides[1][0], sides[1][1])
    beams = jnp.where(left, first, second)
    hi = beams.astype(BF16).astype(F32)
    both = jnp.concatenate([hi.reshape(PEERS, SUBS, LANES), (beams - hi).reshape(PEERS, SUBS, LANES)], axis=1)
    out_ref[...] = both.astype(BF16)
    copy = pltpu.make_async_copy(out_ref, out_hbm.at[:, pl.ds(0, ENDS), :], sem)
    copy.start()
    copy.wait()


def scatter_kernel(got_ref, first_ref, second_ref, first_row_ref, second_row_ref, out_ref):
    got = got_ref[...]
    turned = pltpu.roll(got, LANES // 2, 1)
    left = lax.broadcasted_iota(S32, (TABLE, LANES), 1) < LANES // 2
    ids = lax.broadcasted_iota(S32, (TABLE, TABLE), 0)
    values, chosen = [], []
    for spread, code_ref, row_ref in (
        (jnp.where(left, got, turned), first_ref, first_row_ref),
        (jnp.where(left, turned, got), second_ref, second_row_ref),
    ):
        late = code_ref[...] >= TABLE
        values.append(jnp.where(late != left, spread, 0.0))
        chosen.append(jnp.where(ids == (row_ref[...] & (TABLE - 1)), 1.0, 0.0).astype(BF16))
    hi, lo = split(jnp.concatenate(values, axis=0))
    total = dot(jnp.concatenate(chosen, axis=1), jnp.concatenate([hi, lo], axis=1), (1, 0))
    out_ref[...] = total[:, :LANES] + total[:, LANES:]


def add_kernel(parts_ref, out_ref):
    total = parts_ref[0]
    for i in range(1, GROUPS):
        total = total + parts_ref[i]
    for i in range(PEERS):
        part = i // 8
        out_ref[i] = total[part * SUBS : (part + 1) * SUBS, :]


def place_kernel(parts_ref, out_hbm, out_ref, sems):
    copies = []
    lane = lax.broadcasted_iota(S32, (SUBS, LANES), 1) // SIDE
    for block in range(8):
        for half in range(2):
            rows = [parts_ref[2 * (4 * block + i) + half] for i in range(4)]
            turned = [[rows[i] if d == 0 else pltpu.roll(rows[i], d * SIDE, 1) for d in range(4)] for i in range(4)]
            for interval in range(2):
                for part in range(2):
                    at = 2 * interval + part
                    total = turned[0][(0 - at) % 4]
                    for i in range(1, 4):
                        total = jnp.where(lane == i, turned[i][(i - at) % 4], total)
                    out_ref[:, interval, 2 * half + part, block * LANES : (block + 1) * LANES] = total
        if block % 2 == 0:
            continue
        lanes = pl.ds((block - 1) * LANES, 2 * LANES)
        copies.append(
            pltpu.make_async_copy(out_ref.at[:, :, :, lanes], out_hbm.at[:, :, :, lanes], sems.at[block])
        )
        copies[-1].start()
    for copy in copies:
        copy.wait()


def main_kernel(
    slot_ref, got_ref, row_wave_ref, column_wave_ref, seen_in, flag_in, rows_ref, cols_ref, taper_ref,
    res_ref, out_ref, grad_ref, beam_ref, seen_ref, flag_ref, side_ref, z_ref, dz_ref, held_ref, sems,
):
    copies = [
        pltpu.make_async_copy(a, b, sems.at[i])
        for i, (a, b) in enumerate(
            ((seen_in, seen_ref), (flag_in, flag_ref))
        )
    ]
    for copy in copies:
        copy.start()
    got = got_ref[:, 0:ENDS, :].astype(F32)
    beam_ref[0:TABLE, :] = (got[:, :SUBS] + got[:, SUBS:]).reshape(TABLE, LANES)
    narrow = lax.broadcasted_iota(S32, (SIDE // 2, LANES), 1) // SIDE
    lane = lax.broadcasted_iota(S32, (SIDE, LANES), 1) // SIDE
    taper = taper_ref[...]

    def turn(x, blocks):
        return pltpu.roll(x, blocks * SIDE, 1)

    patches = []
    for k in range(SUBS):
        slot = slot_ref[k]
        tile = slot >> 1
        second = (slot & 1) > 0
        shift = 2 * (slot & 1)
        upper = (narrow - shift) & 3
        lower = (narrow - shift - 1) & 3
        for part in range(2):
            top = jnp.zeros((SIDE // 2, LANES), F32)
            low = top
            for i in range(4):
                piece = got_ref[8 * (4 * part + i) + tile, ENDS : 2 * ENDS, :].astype(F32)
                top = jnp.where(upper == i, piece, top)
                low = jnp.where(lower == i, piece, low)
            top = jnp.where(second, turn(top, 2), top)
            low = jnp.where(second, turn(low, 1), turn(low, 3))
            patches.append(jnp.concatenate([top, low], axis=0).astype(BF16))
    patch = jnp.concatenate(patches, axis=1)
    a = dot(rows_ref[...], jnp.concatenate([patch, patch, patch], axis=0), (1, 0))
    mixed = []
    for k in range(SUBS):
        re = a[:, 2 * k * LANES : (2 * k + 1) * LANES]
        im = a[:, (2 * k + 1) * LANES : (2 * k + 2) * LANES]
        mixed += [re[:SIDE] - im[SIDE:], im[:SIDE] + re[SIDE:]]
    hi, lo = split(jnp.concatenate(mixed, axis=0))
    images = dot(jnp.concatenate([hi, lo, hi], axis=1), cols_ref[...], (1, 0))

    for k in range(SUBS):
        b = images[2 * k * SIDE : 2 * (k + 1) * SIDE]
        i_re = b[:SIDE, :LANES] - b[SIDE:, LANES:]
        i_im = b[:SIDE, LANES:] + b[SIDE:, :LANES]

        sides = []
        for half in range(2):
            g = beam_ref[pl.ds(k + SUBS * half, SIDE, stride=2 * SUBS), :]
            g1, g2 = turn(g, 1), turn(g, 2)
            sides.append((jnp.where(lane == 0, g, jnp.where(lane == 3, g2, g1)), jnp.where(lane < 2, g2, g)))
        (p_re, q_re), (p_im, q_im) = sides

        y_re = i_re * q_re + i_im * q_im
        y_im = i_im * q_re - i_re * q_im
        z_re = (p_re * y_re - p_im * y_im) * taper
        z_im = (p_re * y_im + p_im * y_re) * taper
        for i, part in enumerate((i_re, i_im, p_re, p_im, y_re, y_im)):
            side_ref[k, i] = part * taper if i > 3 else part
        z = jnp.concatenate(
            [jnp.concatenate([z_re, z_im], axis=1), jnp.concatenate([-z_im, z_re], axis=1)], axis=0
        )
        z_hi, z_lo = split(z)
        z_ref[k] = jnp.concatenate([z_hi, z_lo, z_hi], axis=0)

    for copy in copies:
        copy.wait()

    def one(k, carry):
        row_wave = row_wave_ref[k]
        ev_re = column_wave_ref[k, :SIDE, :]
        ev_im = column_wave_ref[k, SIDE:, :]
        w = dot(z_ref[k], jnp.concatenate([row_wave[: 2 * SIDE], row_wave], axis=0), (0, 0))
        reals, imags = [], []
        for pol in range(4):
            w_re = w[pol * SIDE : (pol + 1) * SIDE]
            w_im = w[LANES + pol * SIDE : LANES + (pol + 1) * SIDE]
            reals.append(jnp.sum(w_re * ev_re - w_im * ev_im, axis=0, keepdims=True))
            imags.append(jnp.sum(w_re * ev_im + w_im * ev_re, axis=0, keepdims=True))
        model = jnp.concatenate(reals + imags, axis=0)
        used = flag_ref[pl.ds(k, 1), :].astype(F32)
        res = used * (seen_ref[k] - model)
        res_ref[k] = res
        back = -used * res

        t_re, t_im = [], []
        for pol in range(4):
            d_re = back[pol : pol + 1]
            d_im = back[4 + pol : 5 + pol]
            t_re.append(ev_re * d_re + ev_im * d_im)
            t_im.append(ev_re * d_im - ev_im * d_re)
        t_hi, t_lo = split(jnp.concatenate(t_re + t_im, axis=0))
        held_ref[k, 0] = t_hi
        held_ref[k, 1] = t_lo
        return carry

    def two(k, carry):
        row_wave = row_wave_ref[k]
        t_hi = held_ref[k, 0]
        t_lo = held_ref[k, 1]
        both = dot(row_wave, t_hi, (1, 1))
        dz_ref[k] = both[: 2 * SIDE] + both[2 * SIDE :] + dot(row_wave[: 2 * SIDE], t_lo, (1, 1))
        return carry

    for k in range(SUBS + 1):
        if k < SUBS:
            one(k, 0)
        if k > 0:
            two(k - 1, 0)

    for k in range(SUBS):
        d = dz_ref[k]
        i_re, i_im, p_re, p_im, y_re, y_im = (side_ref[k, i] for i in range(6))
        dz_re = d[:SIDE, :LANES] + d[SIDE:, LANES:]
        dz_im = d[:SIDE, LANES:] - d[SIDE:, :LANES]

        dp_re = dz_re * y_re + dz_im * y_im
        dp_im = dz_im * y_re - dz_re * y_im
        dp_re = dp_re + turn(dp_re, 3)
        dp_im = dp_im + turn(dp_im, 3)
        i_re = i_re * taper
        i_im = i_im * taper
        dy_re = dz_re * p_re + dz_im * p_im
        dy_im = dz_im * p_re - dz_re * p_im
        dq_re = dy_re * i_re + dy_im * i_im
        dq_im = dy_re * i_im - dy_im * i_re
        dq_re = dq_re + turn(dq_re, 2)
        dq_im = dq_im + turn(dq_im, 2)
        for half, (dp, dq) in enumerate(((dp_re, dq_re), (dp_im, dq_im))):
            grad = jnp.where(lane == 0, dp, jnp.where(lane == 1, turn(dp, 3), dq))
            grad_ref[pl.ds(k + SUBS * half, SIDE, stride=2 * SUBS), :] = grad
    out_ref[...] = grad_ref[0:TABLE, :]


SMEM = pl.BlockSpec(memory_space=pltpu.SMEM)
VMEM = pl.BlockSpec(memory_space=pltpu.VMEM)
HBM = pl.BlockSpec(memory_space=pltpu.HBM)
PARAMS = pltpu.CompilerParams(vmem_limit_bytes=40 * 1024 * 1024)


def call(kernel, shapes, specs, out_specs, scratch=(), aliases=None):
    return pl.pallas_call(
        kernel,
        out_shape=shapes,
        in_specs=specs,
        out_specs=out_specs,
        scratch_shapes=list(scratch),
        input_output_aliases=aliases or {},
        compiler_params=PARAMS,
    )


def shape(dims, dtype=F32):
    return jax.ShapeDtypeStruct(dims, dtype)


def cut(place, wanted, grid):
    return pl.pallas_call(
        cut_kernel,
        out_shape=shape((PEERS, 2 * ENDS, LANES), BF16),
        grid_spec=pltpu.PrefetchScalarGridSpec(
            num_scalar_prefetch=2,
            grid=(1,),
            in_specs=[pl.BlockSpec((1, grid.shape[1], LANES), lambda i, place, wanted: (place[1], 0, 0))],
            out_specs=HBM,
            scratch_shapes=[
                pltpu.VMEM((grid.shape[1], LANES), F32),
                pltpu.VMEM((PEERS, ENDS, LANES), BF16),
                pltpu.SemaphoreType.DMA,
            ],
        ),
        compiler_params=PARAMS,
    )(place, wanted, grid)


def in_hbm(x):
    return pltpu.with_memory_space_constraint(x, pltpu.HBM)


def exchange(x, axes):
    return lax.all_to_all(x, axes, split_axis=0, concat_axis=0, tiled=True)


def main(slot, got, row_waves, column_waves, *rest):
    waves = [pltpu.with_memory_space_constraint(x, pltpu.VMEM) for x in (row_waves, column_waves)]
    tables = [jnp.asarray(t) for t in dft_tables()]
    return call(
        main_kernel,
        (shape((SUBS, 8, VIS)), shape((TABLE, LANES))),
        [SMEM] + [VMEM] * 3 + [HBM] * 2 + [VMEM] * 3,
        (VMEM, VMEM),
        [
            pltpu.VMEM((TABLE + 2 * SUBS, LANES), F32),
            pltpu.VMEM((TABLE + 2 * SUBS, LANES), F32),
            pltpu.VMEM((SUBS, 8, VIS), F32),
            pltpu.VMEM((SUBS, VIS), S32),
            pltpu.VMEM((SUBS, 6, SIDE, LANES), F32),
            pltpu.VMEM((SUBS, 6 * SIDE, 2 * LANES), BF16),
            pltpu.VMEM((SUBS, 2 * SIDE, 2 * LANES), F32),
            pltpu.VMEM((SUBS, 2, 2 * LANES, VIS), BF16),
            pltpu.SemaphoreType.DMA((4,)),
        ],
    )(slot, got, *waves, *(in_hbm(x) for x in rest), *tables)


ACROSS = ("z", "tile")
NEAR = ("x", "core")


def body(grid, a_terms, stations, intervals, offsets, uv, observed, flags):
    place = jnp.stack([lax.axis_index(name).astype(S32) for name in ("tile", "z")])
    offsets = offsets.T
    sent = call(
        prep_kernel,
        shape((PEERS, 2, LANES)),
        [HBM] * 4,
        VMEM,
        [
            pltpu.SMEM((2, SUBS), S32),
            pltpu.SMEM((SUBS,), S32),
            pltpu.SMEM((2, SUBS), S32),
            pltpu.VMEM((2, 4, SIDE * SIDE), F32),
            pltpu.SemaphoreType.DMA((4,)),
        ],
    )(*(in_hbm(x) for x in (stations.T, intervals, offsets, a_terms)))
    got_a = exchange(sent, ACROSS)
    spread = call(
        spread_kernel,
        shape((GROUPS, ROWS, LANES)),
        [VMEM],
        HBM,
        [pltpu.VMEM((ROWS, LANES), F32), pltpu.SemaphoreType.DMA((GROUPS,))],
    )(got_a)
    table = exchange(spread, NEAR).reshape(TABLE, LANES)

    wanted = got_a[:, 1, :].astype(S32)
    first = wanted[:, :SUBS].reshape(TABLE)
    second = wanted[:, SUBS:ENDS].reshape(TABLE)
    columns = (first[:, None], second[:, None])
    patches = cut(place, wanted[:, ENDS : ENDS + SLOTS], grid)
    waves = call(
        wave_kernel, (shape((SUBS, 4 * SIDE, VIS), BF16), shape((SUBS, 2 * SIDE, VIS))), [VMEM], (VMEM, VMEM)
    )(uv)

    found = call(
        gather_kernel,
        shape((PEERS, 2 * ENDS, LANES), BF16),
        [VMEM] * 3 + [HBM],
        HBM,
        [pltpu.VMEM((PEERS, ENDS, LANES), BF16), pltpu.SemaphoreType.DMA],
        {3: 0},
    )(table, *columns, patches)
    got_c = exchange(found, ACROSS)

    owner = offsets[0] >> 8
    same = owner[:, None] == owner[None, :]
    earlier = jnp.arange(SUBS)[:, None] > jnp.arange(SUBS)[None, :]
    slot = owner * 2 + jnp.sum((same & earlier).astype(S32), axis=1)
    result, grads = main(slot, got_c, *waves, observed, flags)

    back_c = exchange(grads.reshape(PEERS, SUBS, LANES), ACROSS).reshape(TABLE, LANES)
    dense = call(scatter_kernel, shape((TABLE, LANES)), [VMEM] * 5, VMEM)(
        back_c, *columns, first[None, :], second[None, :]
    )
    back_b = exchange(dense.reshape(GROUPS, ROWS, LANES), NEAR)
    summed = call(add_kernel, shape((PEERS, SUBS, LANES)), [VMEM], VMEM)(back_b)
    back_a = exchange(summed, ACROSS)
    total = call(
        place_kernel,
        shape((SUBS, 2, 4, SIDE * SIDE)),
        [VMEM],
        HBM,
        [pltpu.VMEM((SUBS, 2, 4, SIDE * SIDE), F32), pltpu.SemaphoreType.DMA((8,))],
    )(back_a)
    return (result, total)


def solution(mesh):
    fine = Mesh(mesh.devices.reshape(8, 4, 2, 8), ("z", "x", "core", "tile"))
    st = ("z", "x", "core")
    every = ("z", "x", "core", "tile")
    placed = (
        P(None, "tile", None),
        P(st, None, None, None),
        P(every, None),
        P(every),
        P(every, None),
        P(every, None, None),
        P(every, None, None),
        P(every, None),
    )
    return jax.shard_map(
        body,
        mesh=fine,
        in_specs=placed,
        out_specs=(P(every, None, None), P(st, None, None, None)),
        check_vma=False,
    )
```
